256 devices in a mesh: bricks: 256 (over y, x, z, core).
Axes of the slice: x: 4, y: 4, z: 8, core: 2. Of those that a mesh axis runs over, the one named last changes fastest.
Arguments:
- load_field: float32 [3, 4096, 16, 128], P(None, 'bricks'), may hold values from -6 to 6
- material_class: int32 [4096, 16, 128], P('bricks'), may hold values from 0 to 7
- occupancy: int32 [256, 1, 8], P('bricks'), may hold values 0 or 1
- moduli: float32 [8], replicated, may hold values from 0.3 to 3
Outputs:
- correction: float32 [3, 4096, 16, 128], P(None, 'bricks')
The draws below stay inside these ranges and needn't reach their ends.
All inputs are finite; a program needn't handle non-finite values. No bound on the sum of `occupancy` on one device may be relied on, other than what follows from the above.
Results may differ from the reference program's by a relative error of at most 0.0001.
Values sent between devices are 32-bit elements; how exact they have to be, the bound alone decides.
No kernel may reach another device: no remote copies, remote signals or barrier semaphores. Data moves between devices by JAX's collectives and lax.ppermute only.
A program may use at most 128 MiB of HBM per device.

```python
import math
import jax
import jax.numpy as jnp
from jax import lax

BRICK = 16
ROWS = 1
BRICKS_DEV = 8
CLASSES = 8
DEPTH = 4096
WIDE = 16
SPAN = 128
LAYERS = 256


def plant(result, key, low, largest):
    index_at = [jax.random.randint(jax.random.fold_in(key, axis), (), 0, length) for axis, length in enumerate(result.shape)]
    widest = result.shape.index(max(result.shape))
    beside = index_at[:widest] + [(index_at[widest] + 1) % result.shape[widest]] + index_at[widest + 1:]
    return result.at[tuple(index_at)].set(low).at[tuple(beside)].set(largest)


def shard_levels(own_key, extent, shards, least, high):
    factor_of, own = 1.0, jax.random.fold_in(own_key, 6)
    for axis_at, parts in shards:
        draws = jnp.exp(jax.random.uniform(jax.random.fold_in(own, axis_at), (parts,), jnp.float32, least / len(shards), high / len(shards)))
        factor_of = factor_of * jnp.repeat(draws, extent[axis_at] // parts).reshape([-1 if axis == axis_at else 1 for axis in range(len(extent))])
    return factor_of


def gaussian(stream_key, shape, scale, bound, cuts=(), dtype=jnp.bfloat16):
    values = jax.random.normal(stream_key, shape, jnp.float32) * scale
    if len(cuts) > 0:
        values = shard_levels(stream_key, shape, cuts, -0.22, 0.18) * values
    return jnp.clip(values, min=-bound, max=bound).astype(dtype)


def setup_inputs(seed: int = 0) -> dict:
    key_list = jax.random.split(jax.random.key(seed), 5)
    return {
        "load_field": gaussian(key_list[0], (3, DEPTH, WIDE, SPAN), 1.0, 6.0, ((1, 256),), jnp.float32),
        "material_class": plant(jax.random.randint(key_list[1], (DEPTH, WIDE, SPAN), 0, CLASSES), jax.random.fold_in(key_list[1], 1), 0, CLASSES - 1).astype(jnp.int32),
        "occupancy": plant((jax.random.randint(key_list[2], (LAYERS, ROWS, BRICKS_DEV), 0, 4) < 3).astype(jnp.int32), jax.random.fold_in(key_list[2], 1), 0, 1),
        "moduli": jnp.clip(jnp.exp(jax.random.uniform(key_list[3], (CLASSES,), jnp.float32, math.log(0.3), math.log(3.0))), 0.3, 3.0),
    }


diag_shift = 0.5
couple = 0.25
center = (26.0 + diag_shift) / 27.0
lam_top = 3.0
lam_low = 0.3
cheb_mid = (lam_top + lam_low) / 2.0
cheb_half = (lam_top - lam_low) / 2.0
cheb_ratio = cheb_mid / cheb_half
deepest = 5
semi_from = 3

def triple_sum(values, along):
    n = values.shape[along]
    zero = jnp.zeros_like(lax.slice_in_dim(values, 0, 1, axis=along))
    before = jnp.concatenate([zero, lax.slice_in_dim(values, 0, n - 1, axis=along)], axis=along)
    after = jnp.concatenate([lax.slice_in_dim(values, 1, n, axis=along), zero], axis=along)
    return before + values + after

def operate(u, root, solid, factor):
    inner = u * (root * solid)
    boxed = triple_sum(triple_sum(triple_sum(inner, 1), 2), 3)
    w = ((27.0 + diag_shift) * inner - boxed) / 27.0
    mixture = (1.0 - couple) * w + couple * lax.optimization_barrier(jnp.sum(w, axis=0, keepdims=True))
    return factor * root * solid * mixture

def smooth(b, start_x, root, solid, factor, operator_fn):
    inv_diag = solid / (factor * center * root * root)
    if start_x is None:
        residue = b
    else:
        residue = b - operator_fn(start_x)
    update = inv_diag * residue / cheb_mid
    x = update if start_x is None else start_x + update
    rho_old = 1.0 / cheb_ratio
    for k in range(2):
        rho_new = 1.0 / (2.0 * cheb_ratio - rho_old)
        residue = b - operator_fn(x)
        update = rho_new * rho_old * update + 2.0 * rho_new / cheb_half * (inv_diag * residue)
        x = x + update
        rho_old = rho_new
    return x

def coarsen(values, all_dims):
    c, z, h, y = values.shape
    if all_dims:
        return lax.optimization_barrier(jnp.mean(values.reshape(c, z // 2, 2, h // 2, 2, y // 2, 2), axis=(2, 4, 6)))
    return lax.optimization_barrier(jnp.mean(values.reshape(c, z // 2, 2, h, y // 2, 2), axis=(2, 5)))

def refine(values, all_dims):
    finer = jnp.repeat(values, 2, axis=1)
    if all_dims:
        finer = jnp.repeat(finer, 2, axis=2)
    return jnp.repeat(finer, 2, axis=3)

def vcycle(level_no, b, root, solid):
    factor = 0.25 ** level_no

    def operator_fn(u):
        return operate(u, root, solid, factor)
    x = smooth(b, None, root, solid, factor, operator_fn)
    if level_no == deepest:
        return x
    all_dims = level_no < semi_from
    residue = b - operator_fn(x)
    coarse = vcycle(level_no + 1, coarsen(residue, all_dims), coarsen(root, all_dims), coarsen(solid, all_dims))
    return smooth(b, x + refine(coarse, all_dims), root, solid, factor, operator_fn)

def reference(load_field, material_class, occupancy, moduli):
    modulus = jnp.take(moduli, material_class)
    root = jnp.sqrt(modulus)[None]
    bricks_map = occupancy.astype(jnp.float32)
    bricks_map = jnp.repeat(jnp.repeat(jnp.repeat(bricks_map, BRICK, axis=0), BRICK, axis=1), BRICK, axis=2)
    solid = bricks_map[None]
    return vcycle(0, load_field, root, solid)
```

```python
import jax
import jax.numpy as jnp
from jax import lax
from jax.experimental import pallas as pl
from jax.experimental.pallas import tpu as pltpu
from jax.sharding import PartitionSpec as P

F32 = jnp.float32
center = 26.5 / 27.0
cheb_mid = 1.65
cheb_half = 1.35
sigma = cheb_mid / cheb_half
kappa = (0.75, 0.75, 1.5)
HALO = 10
EXT = 16 + 2 * HALO


def cheb_pairs():
    rho, out = 1.0 / sigma, []
    for _ in range(2):
        new = 1.0 / (2.0 * sigma - rho)
        out.append((new * rho, 2.0 * new / cheb_half))
        rho = new
    return out


(A1, C1), (A2, C2) = cheb_pairs()
INV_MID = 1.0 / cheb_mid


def iota(shape, axis):
    return lax.broadcasted_iota(jnp.int32, shape, axis)


def lane_sum(s, step, period):
    axis = s.ndim - 1
    lane = iota(s.shape, axis) & (period - 1)
    before = jnp.where(lane >= step, pltpu.roll(s, step, axis), 0.0)
    after = jnp.where(lane < period - step, pltpu.roll(s, 128 - step, axis), 0.0)
    return s + before + after


def row_sum(s):
    axis = s.ndim - 2
    n = s.shape[axis]
    row = iota(s.shape, axis)
    before = jnp.where(row >= 1, pltpu.roll(s, 1, axis), 0.0)
    after = jnp.where(row < n - 1, pltpu.roll(s, n - 1, axis), 0.0)
    return s + before + after


def lane_pair(s, step):
    axis = s.ndim - 1
    upper = (iota(s.shape, axis) & step) != 0
    return s + jnp.where(upper, pltpu.roll(s, step, axis), pltpu.roll(s, 128 - step, axis))


def safe(root):
    return jnp.where(root > 0.0, root, 1.0)


def solid_lanes(occ_ref, rows):
    lane = iota((rows, 128), 1) >> 4
    out = jnp.zeros((rows, 128), F32)
    for k in range(8):
        out = jnp.where(lane == k, occ_ref[0, 0, k].astype(F32), out)
    return out


def pack_kernel(load_ref, class_ref, occ_ref, moduli_ref, x_ref, o_ref, root_ref):
    odd = lax.axis_index("bricks") & 1

    def fill(z, _):
        cls = class_ref[z]
        modulus = jnp.zeros(cls.shape, F32)
        for k in range(8):
            modulus = jnp.where(cls == k, moduli_ref[k], modulus)
        root_ref[z] = jnp.sqrt(modulus)
        return 0

    lax.fori_loop(0, 16, fill, 0, unroll=4)
    solid = solid_lanes(occ_ref, 16)
    x_ref[37] = solid
    o_ref[37] = solid
    for ref, first in ((x_ref, (1 - odd)), (o_ref, odd)):
        for c in range(3):
            for j in range(9):
                ref[c * 9 + j] = load_ref[c, first * 7 + j]
        for j in range(10):
            ref[27 + j] = root_ref[first * 6 + j]


def down_kernel(
    load_ref, root_own_ref, occ_ref, x_ref, o_ref,
    msg_ref, edge_ref, v0_ref, beta0_ref, root0_ref, v1_ref, beta1_ref, root1_ref, sol_ref,
    b_s, va_s, d_s, sol_s, t_s, tr_s,
):
    odd = lax.axis_index("bricks") & 1
    is_odd = odd == 1

    def left(k):
        return jnp.where(is_odd, x_ref[k], o_ref[k])

    def right(k):
        return jnp.where(is_odd, o_ref[k], x_ref[k])

    own_solid = solid_lanes(occ_ref, 16)
    left_solid, right_solid = left(37), right(37)
    sol_ref[...] = jnp.zeros((8, 128), F32)
    sol_ref[0:1, :] = left_solid[:1]
    sol_ref[1:2, :] = own_solid[:1]
    sol_ref[2:3, :] = right_solid[:1]
    for j in range(HALO):
        sol_s[j] = left_solid
        sol_s[26 + j] = right_solid
        root0_ref[j] = safe(left(27 + j))
        root0_ref[26 + j] = safe(right(27 + j))

    def own(z, _):
        sol_s[z + HALO] = own_solid
        root0_ref[z + HALO] = root_own_ref[z]
        return 0

    lax.fori_loop(0, 16, own, 0, unroll=4)

    def start(e, b0, b1, b2):
        s = b0 + b1 + b2
        third = s * (1.0 / 3.0)
        scale = sol_s[e] / (center * root0_ref[e])
        for c, p in enumerate((b0 - third, b1 - third, s)):
            b_s[c, e] = p
            beta = p * scale
            beta0_ref[c, e] = beta
            va_s[c, e] = beta * INV_MID

    for j in range(9):
        start(1 + j, left(j), left(9 + j), left(18 + j))
        start(26 + j, right(j), right(9 + j), right(18 + j))

    def own_start(z, _):
        start(z + HALO, load_ref[0, z], load_ref[1, z], load_ref[2, z])
        return 0

    lax.fori_loop(0, 16, own_start, 0, unroll=2)

    def stencil(ref, c, e):
        mid = ref[c, e]
        s = ref[c, e - 1] + mid + ref[c, e + 1]
        return mid, 27.5 * mid - lane_sum(row_sum(s), 1, 128)

    def app1(e, _):
        sol = sol_s[e]
        for c in range(3):
            v, t = stencil(va_s, c, e)
            pre = beta0_ref[c, e] - (sol * (kappa[c] / 26.5)) * t
            d = A1 * v + C1 * pre
            d_s[c, e] = d
            v0_ref[c, e] = v + d
        return 0

    lax.fori_loop(2, 34, app1, 0, unroll=2)

    def app2(e, _):
        sol = sol_s[e]
        for c in range(3):
            v, t = stencil(v0_ref, c, e)
            pre = beta0_ref[c, e] - (sol * (kappa[c] / 26.5)) * t
            va_s[c, e] = v + A2 * d_s[c, e] + C2 * pre
        return 0

    lax.fori_loop(3, 33, app2, 0, unroll=2)

    def resid(k, _):
        e = 4 + 2 * k
        for c in range(3):
            total = None
            for j in range(2):
                v, t = stencil(va_s, c, e + j)
                v0_ref[c, e + j] = v
                r = b_s[c, e + j] - (sol_s[e + j] * root0_ref[e + j]) * (kappa[c] / 27.0) * t
                total = r if total is None else total + r
            t_s[c, k] = total
        return 0

    lax.fori_loop(0, 14, resid, 0)

    def root_pair(k, _):
        tr_s[k] = root0_ref[2 * k] + root0_ref[2 * k + 1]
        return 0

    lax.fori_loop(0, 18, root_pair, 0, unroll=2)

    root1 = lane_pair(tr_s[:, pl.ds(0, 8, 2), :] + tr_s[:, pl.ds(1, 8, 2), :], 1) * 0.125
    root1_ref[...] = root1
    rt = root1[2:16]
    sol = jnp.concatenate(
        [
            jnp.broadcast_to(left_solid[None, :8], (3, 8, 128)),
            jnp.broadcast_to(own_solid[None, :8], (8, 8, 128)),
            jnp.broadcast_to(right_solid[None, :8], (3, 8, 128)),
        ],
        axis=0,
    )
    scale1 = sol / (0.25 * center * rt)
    zero = jnp.zeros((1, 8, 128), F32)

    def stencil1(v):
        before = jnp.concatenate([zero, v[:-1]], axis=0)
        after = jnp.concatenate([v[1:], zero], axis=0)
        return 27.5 * v - lane_sum(row_sum(before + v + after), 2, 128)

    gather = 4 * (iota((8, 128), 1) & 31)
    group = (iota((8, 128), 1) >> 5) == (iota((8, 128), 0) >> 1)

    def compact(q):
        q = q + pltpu.roll(q, 126, 1)
        q = jnp.take_along_axis(q, gather, axis=1)
        return jnp.sum(jnp.where(group, q, 0.0), axis=0, keepdims=True) * 0.125

    for c in range(3):
        b1 = lane_pair(t_s[c, :, pl.ds(0, 8, 2), :] + t_s[c, :, pl.ds(1, 8, 2), :], 1) * 0.125
        beta = b1 * scale1
        m = sol * (kappa[c] / 26.5)
        v = beta * INV_MID
        d = A1 * v + C1 * (beta - m * stencil1(v))
        v = v + d
        d = A2 * d + C2 * (beta - m * stencil1(v))
        v = v + d
        v1_ref[c] = v
        beta1_ref[c] = beta
        r = (b1 - (sol * rt) * (0.25 * kappa[c] / 27.0) * stencil1(v))[3:11]
        for z in range(4):
            msg_ref[4 * c + z : 4 * c + z + 1, :] = compact(r[2 * z] + r[2 * z + 1])
        for j in range(4):
            to_after, to_before = v[6 + j], v[4 + j]
            k = 8 * (4 * c + j)
            msg_ref[24 + k : 32 + k, :] = jnp.where(is_odd, to_before, to_after)
            edge_ref[k : k + 8, :] = jnp.where(is_odd, to_after, to_before)
        to_after, to_before = beta[7], beta[6]
        k = 8 * (12 + c)
        msg_ref[24 + k : 32 + k, :] = jnp.where(is_odd, to_before, to_after)
        edge_ref[k : k + 8, :] = jnp.where(is_odd, to_after, to_before)
    for z in range(4):
        msg_ref[12 + z : 13 + z, :] = compact(root1[5 + 2 * z] + root1[6 + 2 * z])
    msg_ref[16:24, :] = jnp.take_along_axis(own_solid[:8], gather, axis=1)


def up_kernel(
    row_ref, far_ref, far2_ref, msg_in_ref, edge_in_ref,
    v0_ref, beta0_ref, root0_ref, v1_ref, beta1_ref, root1_ref, sol_ref,
    out_ref,
    all_s, w_s, f_s, e2_s, pe_s, a_s, bb_s, d_s,
):
    me = lax.axis_index("bricks")
    odd = me & 1
    is_odd = odd == 1

    for t in range(16):
        rows = slice(24 * t, 24 * t + 24)
        far, far2 = far_ref[rows, :], far2_ref[rows, :]
        all_s[t] = jnp.where(is_odd, far2, far)
        all_s[16 + t] = row_ref[rows, :]
        all_s[32 + t] = jnp.where(is_odd, far, far2)
    base = me - odd - 16
    here = me & 15
    other = here ^ 1
    order_left = jnp.where(is_odd, here, other)
    order_right = jnp.where(is_odd, other, here)
    for w in range(34):
        dev = base + w
        rel = (dev >> 4) - (me >> 4)
        order = jnp.where(rel == 0, here, jnp.where(rel < 0, order_left, order_right))
        x = (dev & 15) ^ order
        slot = (rel + 1) * 16 + (x ^ ((x & 8) >> 1))
        for c in range(4):
            w_s[c, 4 * w : 4 * w + 4, :] = all_s[slot, 4 * c : 4 * c + 4, :]
        w_s[4, 4 * w : 4 * w + 4, :] = all_s[slot, 16:20, :]

    def stencil(v, level):
        n = v.shape[0]
        s = v + pltpu.roll(v, 1, 0) + pltpu.roll(v, n - 1, 0)
        if level == 2:
            lane = iota(s.shape, 1)
            s = (
                s
                + jnp.where(lane >= 32, pltpu.roll(s, 32, 1), 0.0)
                + jnp.where(lane < 96, pltpu.roll(s, 96, 1), 0.0)
            )
        else:
            s = s + pltpu.roll(s, 64, 1)
        return 27.5 * v - lane_sum(s, 2 ** (level - 2), 32)

    def first(beta, m, level):
        v = beta * INV_MID
        d = A1 * v + C1 * (beta - m * stencil(v, level))
        v = v + d
        d = A2 * d + C2 * (beta - m * stencil(v, level))
        return v + d

    def again(v, beta, m, level):
        d = INV_MID * (beta - m * stencil(v, level))
        v = v + d
        d = A1 * d + C1 * (beta - m * stencil(v, level))
        v = v + d
        d = A2 * d + C2 * (beta - m * stencil(v, level))
        return v + d

    def coarsen(values, level):
        n = values.shape[0]
        half = (n // 2 + 7) // 8 * 8
        if 2 * half > n:
            f_s[n : 2 * half, :] = jnp.zeros((2 * half - n, 128), F32)
        f_s[0:n, :] = values
        s = f_s[pl.ds(0, half, 2), :] + f_s[pl.ds(1, half, 2), :]
        s = lane_pair(s, 2 ** (level - 2))
        if level == 2:
            return lane_pair(s, 32) * 0.125
        return s * 0.25

    def refine(values, first_row, count):
        n = values.shape[0]
        f_s[pl.ds(0, n, 2), :] = values
        f_s[pl.ds(1, n, 2), :] = values
        return f_s[first_row : first_row + count, :]

    roots = {2: safe(w_s[3])}
    sols = {2: w_s[4]}
    for level in (2, 3, 4):
        roots[level + 1] = safe(coarsen(roots[level], level))
        sols[level + 1] = coarsen(sols[level], level)

    def beta_scale(level):
        sol = sols[level]
        sol = sol * sol if level == 5 else sol
        return sol / (0.25**level * center * roots[level])

    def mask(level):
        sol = sols[level]
        return sol * sol * sol if level == 5 else sol

    scales = {level: beta_scale(level) for level in (2, 3, 4, 5)}
    masks = {level: mask(level) for level in (2, 3, 4, 5)}
    g5 = jnp.where(sols[5] > 0.0, 1.0 / (roots[5] * jnp.where(sols[5] > 0.0, sols[5], 1.0)), 0.0)
    windows = {4: (0, 40), 3: (24, 48), 2: (56, 80)}

    for c in range(3):
        b = w_s[c]
        betas, vs = {}, {}
        for level in (2, 3, 4):
            beta = b * scales[level]
            v = first(beta, masks[level] * (kappa[c] / 26.5), level)
            r = b - (sols[level] * roots[level]) * (0.25**level * kappa[c] / 27.0) * stencil(v, level)
            betas[level], vs[level] = beta, v
            b = coarsen(r, level)
        e = first(b * scales[5], masks[5] * (kappa[c] / 26.5), 5) * g5
        first_row = 0
        for level in (4, 3, 2):
            lo, hi = windows[level]
            e = refine(e, lo - first_row, hi - lo)
            root, sol = roots[level][lo:hi], sols[level][lo:hi]
            v = vs[level][lo:hi] + (root * sol) * e
            v = again(v, betas[level][lo:hi], masks[level][lo:hi] * (kappa[c] / 26.5), level)
            e = jnp.where(sol > 0.0, v / root, e)
            first_row = 2 * lo
        e2_s[c] = e

    rows = {}
    for k, name in enumerate(("left", "own", "right")):
        rows[name] = sol_ref[k : k + 1, :]

    def layers(name, n):
        return jnp.broadcast_to(rows[name][None], (n, 8, 128))

    sol = jnp.concatenate([layers("left", 5), layers("own", 8), layers("right", 5)], axis=0)
    root1 = root1_ref[...]
    spread = (iota((8, 128), 0) >> 1) * 32 + (iota((8, 128), 1) >> 2)
    zero = jnp.zeros((1, 8, 128), F32)

    def stencil1(v):
        before = jnp.concatenate([zero, v[:-1]], axis=0)
        after = jnp.concatenate([v[1:], zero], axis=0)
        return 27.5 * v - lane_sum(row_sum(before + v + after), 2, 128)

    def from_left(k):
        return jnp.where(is_odd, msg_in_ref[24 + 8 * k : 32 + 8 * k, :], edge_in_ref[8 * k : 8 * k + 8, :])[None]

    def from_right(k):
        return jnp.where(is_odd, edge_in_ref[8 * k : 8 * k + 8, :], msg_in_ref[24 + 8 * k : 32 + 8 * k, :])[None]

    for c in range(3):
        v = jnp.concatenate(
            [from_left(4 * c + j) for j in range(4)]
            + [v1_ref[c][2:12]]
            + [from_right(4 * c + j) for j in range(4)],
            axis=0,
        )
        beta = jnp.concatenate([zero, from_left(12 + c), beta1_ref[c], from_right(12 + c), zero], axis=0)
        slabs = []
        for j in range(10):
            row = e2_s[c, pl.ds(5 + 4 * odd + j, 1), :]
            slab = jnp.take_along_axis(jnp.broadcast_to(row, (8, 128)), spread, axis=1)[None]
            slabs += [slab, slab]
        e = jnp.concatenate(slabs[1:19], axis=0)
        m = sol * (kappa[c] / 26.5)
        v = v + (root1 * sol) * e
        d = INV_MID * (beta - m * stencil1(v))
        v = v + d
        d = A1 * d + C1 * (beta - m * stencil1(v))
        v = v + d
        d = A2 * d + C2 * (beta - m * stencil1(v))
        v = v + d
        e = jnp.where(sol > 0.0, v / root1, e)[3:15]
        pe_s[c, :, pl.ds(0, 8, 2), :] = e
        pe_s[c, :, pl.ds(1, 8, 2), :] = e

    shift = HALO - 4

    def sol0(k):
        row = jnp.where(k < 4, rows["left"], jnp.where(k < 20, rows["own"], rows["right"]))
        return jnp.broadcast_to(row, (16, 128))

    def begin(k, _):
        g = root0_ref[k + shift] * sol0(k)
        for c in range(3):
            a_s[c, k] = v0_ref[c, k + shift] + g * pe_s[c, k >> 1]
        return 0

    lax.fori_loop(1, 23, begin, 0, unroll=2)

    def stencil0(ref, c, k):
        mid = ref[c, k]
        s = ref[c, k - 1] + mid + ref[c, k + 1]
        return mid, 27.5 * mid - lane_sum(row_sum(s), 1, 128)

    def app0(k, _):
        sol = sol0(k)
        for c in range(3):
            v, t = stencil0(a_s, c, k)
            d = INV_MID * (beta0_ref[c, k + shift] - (sol * (kappa[c] / 26.5)) * t)
            d_s[c, k] = d
            bb_s[c, k] = v + d
        return 0

    lax.fori_loop(2, 22, app0, 0, unroll=2)

    def app1(k, _):
        sol = sol0(k)
        for c in range(3):
            v, t = stencil0(bb_s, c, k)
            pre = beta0_ref[c, k + shift] - (sol * (kappa[c] / 26.5)) * t
            d = A1 * d_s[c, k] + C1 * pre
            d_s[c, k] = d
            a_s[c, k] = v + d
        return 0

    lax.fori_loop(3, 21, app1, 0, unroll=2)
    own_solid = jnp.broadcast_to(rows["own"], (16, 128))

    def app2(k, _):
        inverse = 1.0 / root0_ref[k + shift]
        x = []
        for c in range(3):
            v, t = stencil0(a_s, c, k)
            pre = beta0_ref[c, k + shift] - (own_solid * (kappa[c] / 26.5)) * t
            v = v + A2 * d_s[c, k] + C2 * pre
            x.append(jnp.where(own_solid > 0.0, v * inverse, pe_s[c, k >> 1]))
        third = x[2] * (1.0 / 3.0)
        out_ref[0, k - 4] = x[0] + third
        out_ref[1, k - 4] = x[1] + third
        out_ref[2, k - 4] = third - x[0] - x[1]
        return 0

    lax.fori_loop(4, 20, app2, 0, unroll=2)


VMEM = pl.BlockSpec(memory_space=pltpu.VMEM)
SMEM = pl.BlockSpec(memory_space=pltpu.SMEM)
PARAMS = pltpu.CompilerParams(vmem_limit_bytes=40 * 2**20)


def shaped(*shape):
    return jax.ShapeDtypeStruct(shape, F32)


def swap_bits(values, bits):
    n = lax.axis_size("bricks")
    return lax.ppermute(values, "bricks", [(i, i ^ bits) for i in range(n)])


def swap_before(values, distance):
    n = lax.axis_size("bricks")
    pairs = []
    for i in range(0, n, 2):
        if i - distance >= 0:
            pairs += [(i, i - distance), (i - distance, i)]
    return lax.ppermute(values, "bricks", sorted(pairs))


def body(load_field, material_class, occupancy, moduli):
    x_msg, o_msg, root = pl.pallas_call(
        pack_kernel,
        out_shape=(shaped(38, 16, 128), shaped(38, 16, 128), shaped(16, 16, 128)),
        in_specs=[VMEM, VMEM, SMEM, SMEM],
        out_specs=(VMEM, VMEM, VMEM),
        compiler_params=PARAMS,
        name="pack",
    )(load_field, material_class, occupancy, moduli)
    x_in = swap_bits(x_msg, 1)
    o_in = swap_before(o_msg, 1)
    msg, edge, *fine = pl.pallas_call(
        down_kernel,
        out_shape=(
            shaped(144, 128), shaped(120, 128),
            shaped(3, EXT, 16, 128), shaped(3, EXT, 16, 128), shaped(EXT, 16, 128),
            shaped(3, 14, 8, 128), shaped(3, 14, 8, 128), shaped(18, 8, 128), shaped(8, 128),
        ),
        in_specs=[VMEM, VMEM, SMEM, VMEM, VMEM],
        out_specs=(VMEM,) * 9,
        scratch_shapes=[
            pltpu.VMEM((3, EXT, 16, 128), F32),
            pltpu.VMEM((3, EXT, 16, 128), F32),
            pltpu.VMEM((3, EXT, 16, 128), F32),
            pltpu.VMEM((EXT, 16, 128), F32),
            pltpu.VMEM((3, 14, 16, 128), F32),
            pltpu.VMEM((18, 16, 128), F32),
        ],
        compiler_params=PARAMS,
        name="down",
    )(load_field, root, occupancy, x_in, o_in)
    msg_in = swap_bits(msg, 1)
    edge_in = swap_before(edge, 1)
    row = jnp.concatenate([msg[:24], msg_in[:24]], axis=0)
    for bits in (2, 4, 12):
        row = jnp.concatenate([row, swap_bits(row, bits)], axis=0)
    far = swap_before(row, 15)
    far2 = swap_bits(far, 1)
    return pl.pallas_call(
        up_kernel,
        out_shape=shaped(3, 16, 16, 128),
        in_specs=[VMEM] * 12,
        out_specs=VMEM,
        scratch_shapes=[
            pltpu.VMEM((48, 24, 128), F32),
            pltpu.VMEM((5, 136, 128), F32),
            pltpu.VMEM((144, 128), F32),
            pltpu.VMEM((3, 24, 128), F32),
            pltpu.VMEM((3, 12, 16, 128), F32),
            pltpu.VMEM((3, 24, 16, 128), F32),
            pltpu.VMEM((3, 24, 16, 128), F32),
            pltpu.VMEM((3, 24, 16, 128), F32),
        ],
        compiler_params=PARAMS,
        name="up",
    )(row, far, far2, msg_in, edge_in, *fine)


def solution(mesh):
    in_specs = (
        P(None, "bricks", None, None),
        P("bricks", None, None),
        P("bricks", None, None),
        P(),
    )
    out_specs = P(None, "bricks", None, None)
    return jax.shard_map(body, mesh=mesh, in_specs=in_specs, out_specs=out_specs, check_vma=False)
```

```python
import jax
import jax.numpy as jnp
from jax import lax
from jax.experimental import pallas as pl
from jax.experimental.pallas import tpu as pltpu
from jax.sharding import PartitionSpec as P

F32 = jnp.float32
center = 26.5 / 27.0
cheb_mid = 1.65
cheb_half = 1.35
sigma = cheb_mid / cheb_half
kappa = (0.75, 0.75, 1.5)
HALO = 10
EXT = 16 + 2 * HALO


def cheb_pairs():
    rho, out = 1.0 / sigma, []
    for _ in range(2):
        new = 1.0 / (2.0 * sigma - rho)
        out.append((new * rho, 2.0 * new / cheb_half))
        rho = new
    return out


(A1, C1), (A2, C2) = cheb_pairs()
INV_MID = 1.0 / cheb_mid


def iota(shape, axis):
    return lax.broadcasted_iota(jnp.int32, shape, axis)


def lane_sum(s, step, period):
    axis = s.ndim - 1
    lane = iota((1,) * axis + (128,), axis) & (period - 1)
    low = jnp.where(lane >= step, 1.0, 0.0).astype(F32)
    high = jnp.where(lane < period - step, 1.0, 0.0).astype(F32)
    return s + low * pltpu.roll(s, step, axis) + high * pltpu.roll(s, 128 - step, axis)


def row_sum(s):
    axis = s.ndim - 2
    n = s.shape[axis]
    row = iota(s.shape, axis)
    before = jnp.where(row >= 1, pltpu.roll(s, 1, axis), 0.0)
    after = jnp.where(row < n - 1, pltpu.roll(s, n - 1, axis), 0.0)
    return s + before + after


def lane_pair(s, step):
    axis = s.ndim - 1
    upper = (iota(s.shape, axis) & step) != 0
    return s + jnp.where(upper, pltpu.roll(s, step, axis), pltpu.roll(s, 128 - step, axis))


def safe(root):
    return jnp.where(root > 0.0, root, 1.0)


def pack_kernel(load_ref, class_ref, occ_ref, moduli_ref, x_ref, o_ref, root_ref, class_s, occ_s, moduli_s, sems):
    odd = lax.axis_index("bricks") & 1
    small = [
        pltpu.make_async_copy(class_ref, class_s, sems.at[0]),
        pltpu.make_async_copy(occ_ref, occ_s, sems.at[1]),
        pltpu.make_async_copy(moduli_ref, moduli_s, sems.at[2]),
    ]
    for copy in small:
        copy.start()
    large = []
    for k, (ref, first) in enumerate(((x_ref, 1 - odd), (o_ref, odd))):
        for c in range(3):
            copy = pltpu.make_async_copy(
                load_ref.at[c, pl.ds(first * 7, 9)], ref.at[pl.ds(9 * c, 9)], sems.at[3 + 3 * k + c]
            )
            copy.start()
            large.append(copy)
    for copy in small:
        copy.wait()

    def fill(z, _):
        cls = class_s[z]
        modulus = jnp.zeros(cls.shape, F32)
        for k in range(8):
            modulus = jnp.where(cls == k, moduli_s[k], modulus)
        root_ref[z] = jnp.sqrt(modulus)
        return 0

    lax.fori_loop(0, 16, fill, 0, unroll=8)
    lane = iota((16, 128), 1) >> 4
    solid = jnp.zeros((16, 128), F32)
    for k in range(8):
        solid = jnp.where(lane == k, occ_s[0, 0, k].astype(F32), solid)
    root_ref[16] = solid
    x_ref[37] = solid
    o_ref[37] = solid
    for ref, first in ((x_ref, 1 - odd), (o_ref, odd)):
        for j in range(10):
            ref[27 + j] = root_ref[first * 6 + j]
    for copy in large:
        copy.wait()


def down_kernel(
    load_ref, root_own_ref, x_ref, o_ref,
    msg_ref, edge_ref, v0_ref, beta0_ref, root0_ref, v1_ref, beta1_ref, root1_ref, sol_ref,
    b_s, va_s, d_s, sol_s, t_s, tr_s,
):
    odd = lax.axis_index("bricks") & 1
    is_odd = odd == 1

    def left(k):
        return jnp.where(is_odd, x_ref[k], o_ref[k])

    def right(k):
        return jnp.where(is_odd, o_ref[k], x_ref[k])

    own_solid = root_own_ref[16]
    left_solid, right_solid = left(37), right(37)
    sol_ref[...] = jnp.zeros((8, 128), F32)
    sol_ref[0:1, :] = left_solid[:1]
    sol_ref[1:2, :] = own_solid[:1]
    sol_ref[2:3, :] = right_solid[:1]
    for j in range(HALO):
        sol_s[j] = left_solid
        sol_s[26 + j] = right_solid
        root0_ref[j] = safe(left(27 + j))
        root0_ref[26 + j] = safe(right(27 + j))

    def own(z, _):
        sol_s[z + HALO] = own_solid
        root0_ref[z + HALO] = root_own_ref[z]
        return 0

    lax.fori_loop(0, 16, own, 0, unroll=16)

    def start(e, b0, b1, b2):
        s = b0 + b1 + b2
        third = s * (1.0 / 3.0)
        scale = sol_s[e] / (center * root0_ref[e])
        for c, p in enumerate((b0 - third, b1 - third, s)):
            b_s[c, e] = p
            beta = p * scale
            beta0_ref[c, e] = beta
            va_s[c, e] = beta * INV_MID

    for j in range(9):
        start(1 + j, left(j), left(9 + j), left(18 + j))
        start(26 + j, right(j), right(9 + j), right(18 + j))

    def own_start(z, _):
        start(z + HALO, load_ref[0, z], load_ref[1, z], load_ref[2, z])
        return 0

    lax.fori_loop(0, 16, own_start, 0, unroll=8)

    def stencil(ref, c, e):
        mid = ref[c, e]
        s = ref[c, e - 1] + mid + ref[c, e + 1]
        return mid, 27.5 * mid - lane_sum(row_sum(s), 1, 128)

    def app1(e, _):
        sol = sol_s[e]
        for c in range(3):
            v, t = stencil(va_s, c, e)
            pre = beta0_ref[c, e] - (sol * (kappa[c] / 26.5)) * t
            d = A1 * v + C1 * pre
            d_s[c, e] = d
            v0_ref[c, e] = v + d
        return 0

    lax.fori_loop(2, 34, app1, 0, unroll=8)

    def app2(e, _):
        sol = sol_s[e]
        for c in range(3):
            v, t = stencil(v0_ref, c, e)
            pre = beta0_ref[c, e] - (sol * (kappa[c] / 26.5)) * t
            va_s[c, e] = v + A2 * d_s[c, e] + C2 * pre
        return 0

    lax.fori_loop(3, 33, app2, 0, unroll=10)

    def resid(k, _):
        e = 4 + 2 * k
        for c in range(3):
            total = None
            for j in range(2):
                v, t = stencil(va_s, c, e + j)
                v0_ref[c, e + j] = v
                r = b_s[c, e + j] - (sol_s[e + j] * root0_ref[e + j]) * (kappa[c] / 27.0) * t
                total = r if total is None else total + r
            t_s[c, k] = total
        return 0

    lax.fori_loop(0, 14, resid, 0, unroll=7)

    def root_pair(k, _):
        tr_s[k] = root0_ref[2 * k] + root0_ref[2 * k + 1]
        return 0

    lax.fori_loop(0, 18, root_pair, 0, unroll=18)

    root1 = lane_pair(tr_s[:, pl.ds(0, 8, 2), :] + tr_s[:, pl.ds(1, 8, 2), :], 1) * 0.125
    root1_ref[...] = root1
    rt = root1[2:16]
    sol = jnp.concatenate(
        [
            jnp.broadcast_to(left_solid[None, :8], (3, 8, 128)),
            jnp.broadcast_to(own_solid[None, :8], (8, 8, 128)),
            jnp.broadcast_to(right_solid[None, :8], (3, 8, 128)),
        ],
        axis=0,
    )
    scale1 = sol / (0.25 * center * rt)
    zero = jnp.zeros((1, 8, 128), F32)

    def stencil1(v):
        before = jnp.concatenate([zero, v[:-1]], axis=0)
        after = jnp.concatenate([v[1:], zero], axis=0)
        return 27.5 * v - lane_sum(row_sum(before + v + after), 2, 128)

    gather = 4 * (iota((8, 128), 1) & 31)
    group = (iota((8, 128), 1) >> 5) == (iota((8, 128), 0) >> 1)

    def compact(q):
        q = q + pltpu.roll(q, 126, 1)
        q = jnp.take_along_axis(q, gather, axis=1)
        return jnp.sum(jnp.where(group, q, 0.0), axis=0, keepdims=True) * 0.125

    for c in range(3):
        b1 = lane_pair(t_s[c, :, pl.ds(0, 8, 2), :] + t_s[c, :, pl.ds(1, 8, 2), :], 1) * 0.125
        beta = b1 * scale1
        m = sol * (kappa[c] / 26.5)
        v = beta * INV_MID
        d = A1 * v + C1 * (beta - m * stencil1(v))
        v = v + d
        d = A2 * d + C2 * (beta - m * stencil1(v))
        v = v + d
        v1_ref[c] = v
        beta1_ref[c] = beta
        r = (b1 - (sol * rt) * (0.25 * kappa[c] / 27.0) * stencil1(v))[3:11]
        for z in range(4):
            msg_ref[4 * c + z : 4 * c + z + 1, :] = compact(r[2 * z] + r[2 * z + 1])
        for j in range(4):
            to_after, to_before = v[6 + j], v[4 + j]
            k = 8 * (4 * c + j)
            msg_ref[24 + k : 32 + k, :] = jnp.where(is_odd, to_before, to_after)
            edge_ref[k : k + 8, :] = jnp.where(is_odd, to_after, to_before)
        to_after, to_before = beta[7], beta[6]
        k = 8 * (12 + c)
        msg_ref[24 + k : 32 + k, :] = jnp.where(is_odd, to_before, to_after)
        edge_ref[k : k + 8, :] = jnp.where(is_odd, to_after, to_before)
    for z in range(4):
        msg_ref[12 + z : 13 + z, :] = compact(root1[5 + 2 * z] + root1[6 + 2 * z])
    msg_ref[16:24, :] = jnp.take_along_axis(own_solid[:8], gather, axis=1)


def up_kernel(
    row_ref, far_ref, far2_ref, msg_in_ref, edge_in_ref,
    v0_ref, beta0_ref, root0_ref, v1_ref, beta1_ref, root1_ref, sol_ref,
    out_ref,
    all_s, w_s, f_s, e2_s, pe_s, a_s, bb_s, d_s,
):
    me = lax.axis_index("bricks")
    odd = me & 1
    is_odd = odd == 1

    for t in range(16):
        rows = slice(24 * t, 24 * t + 24)
        far, far2 = far_ref[rows, :], far2_ref[rows, :]
        all_s[t] = jnp.where(is_odd, far2, far)
        all_s[16 + t] = row_ref[rows, :]
        all_s[32 + t] = jnp.where(is_odd, far, far2)
    base = me - odd - 16
    here = me & 15
    other = here ^ 1
    order_left = jnp.where(is_odd, here, other)
    order_right = jnp.where(is_odd, other, here)
    for w in range(34):
        dev = base + w
        rel = (dev >> 4) - (me >> 4)
        order = jnp.where(rel == 0, here, jnp.where(rel < 0, order_left, order_right))
        x = (dev & 15) ^ order
        slot = (rel + 1) * 16 + (x ^ ((x & 8) >> 1))
        for c in range(4):
            w_s[c, 4 * w : 4 * w + 4, :] = all_s[slot, 4 * c : 4 * c + 4, :]
        w_s[4, 4 * w : 4 * w + 4, :] = all_s[slot, 16:20, :]

    lane = iota((1, 1, 128), 2)

    def lane_mask(cond):
        return jnp.where(cond, 1.0, 0.0).astype(F32)

    masks_x = (lane_mask(lane >= 32), lane_mask(lane < 96))
    masks_y = {
        level: (lane_mask((lane & 31) >= step), lane_mask((lane & 31) < 32 - step))
        for level, step in ((2, 1), (3, 2), (4, 4), (5, 8))
    }
    scale27 = jnp.concatenate([jnp.full((1, 1, 128), k, F32) for k in kappa], axis=0)
    by26 = scale27 * (1.0 / 26.5)

    def stencil(v, level):
        n = v.shape[1]
        s = v + pltpu.roll(v, 1, 1) + pltpu.roll(v, n - 1, 1)
        if level == 2:
            s = s + masks_x[0] * pltpu.roll(s, 32, 2) + masks_x[1] * pltpu.roll(s, 96, 2)
        else:
            s = s + pltpu.roll(s, 64, 2)
        step = 2 ** (level - 2)
        low, high = masks_y[level]
        s = s + low * pltpu.roll(s, step, 2) + high * pltpu.roll(s, 128 - step, 2)
        return 27.5 * v - s

    def first(beta, m, level):
        v = beta * INV_MID
        d = A1 * v + C1 * (beta - m * stencil(v, level))
        v = v + d
        d = A2 * d + C2 * (beta - m * stencil(v, level))
        return v + d

    def again(v, beta, m, level):
        d = INV_MID * (beta - m * stencil(v, level))
        v = v + d
        d = A1 * d + C1 * (beta - m * stencil(v, level))
        v = v + d
        d = A2 * d + C2 * (beta - m * stencil(v, level))
        return v + d

    def coarsen(values, level):
        k, n = values.shape[:2]
        half = (n // 2 + 7) // 8 * 8
        if 2 * half > n:
            f_s[0:k, n : 2 * half, :] = jnp.zeros((k, 2 * half - n, 128), F32)
        f_s[0:k, 0:n, :] = values
        s = f_s[0:k, pl.ds(0, half, 2), :] + f_s[0:k, pl.ds(1, half, 2), :]
        s = lane_pair(s, 2 ** (level - 2))
        if level == 2:
            return lane_pair(s, 32) * 0.125
        return s * 0.25

    def refine(values, first_row, count):
        n = values.shape[1]
        f_s[0:3, pl.ds(0, n, 2), :] = values
        f_s[0:3, pl.ds(1, n, 2), :] = values
        return f_s[0:3, first_row : first_row + count, :]

    both = w_s[3:5]
    roots, sols = {2: safe(both[0:1])}, {2: both[1:2]}
    for level in (2, 3, 4):
        both = coarsen(jnp.concatenate([roots[level], sols[level]], axis=0), level)
        roots[level + 1], sols[level + 1] = safe(both[0:1]), both[1:2]
    sol5 = sols[5]
    sol5_safe = jnp.where(sol5 > 0.0, sol5, 1.0)
    inverse = {level: 1.0 / roots[level] for level in (2, 3, 4, 5)}
    powers = {level: (sols[level], sols[level]) for level in (2, 3, 4)}
    powers[5] = (sol5 * sol5, sol5 * sol5 * sol5)
    g5 = jnp.where(sol5 > 0.0, inverse[5] / sol5_safe, 0.0)
    scales = {level: powers[level][0] * inverse[level] * (1.0 / (0.25**level * center)) for level in (2, 3, 4, 5)}
    masks = {level: powers[level][1] * by26 for level in (2, 3, 4, 5)}
    windows = {4: (0, 40), 3: (24, 48), 2: (56, 80)}

    b = w_s[0:3]
    betas, vs = {}, {}
    for level in (2, 3, 4):
        beta = b * scales[level]
        v = first(beta, masks[level], level)
        r = b - (sols[level] * roots[level]) * (scale27 * (0.25**level / 27.0)) * stencil(v, level)
        betas[level], vs[level] = beta, v
        b = coarsen(r, level)
    e = first(b * scales[5], masks[5], 5) * g5
    first_row = 0
    for level in (4, 3, 2):
        lo, hi = windows[level]
        e = refine(e, lo - first_row, hi - lo)
        root, sol = roots[level][:, lo:hi], sols[level][:, lo:hi]
        v = vs[level][:, lo:hi] + (root * sol) * e
        v = again(v, betas[level][:, lo:hi], masks[level][:, lo:hi], level)
        e = jnp.where(sol > 0.0, v * inverse[level][:, lo:hi], e)
        first_row = 2 * lo
    e2_s[...] = e

    rows = {}
    for k, name in enumerate(("left", "own", "right")):
        rows[name] = sol_ref[k : k + 1, :]

    def layers(name, n):
        return jnp.broadcast_to(rows[name][None], (n, 8, 128))

    sol = jnp.concatenate([layers("left", 5), layers("own", 8), layers("right", 5)], axis=0)
    root1 = root1_ref[...]
    spread = (iota((8, 128), 0) >> 1) * 32 + (iota((8, 128), 1) >> 2)
    zero = jnp.zeros((1, 8, 128), F32)

    def stencil1(v):
        before = jnp.concatenate([zero, v[:-1]], axis=0)
        after = jnp.concatenate([v[1:], zero], axis=0)
        return 27.5 * v - lane_sum(row_sum(before + v + after), 2, 128)

    def from_left(k):
        return jnp.where(is_odd, msg_in_ref[24 + 8 * k : 32 + 8 * k, :], edge_in_ref[8 * k : 8 * k + 8, :])[None]

    def from_right(k):
        return jnp.where(is_odd, edge_in_ref[8 * k : 8 * k + 8, :], msg_in_ref[24 + 8 * k : 32 + 8 * k, :])[None]

    for c in range(3):
        v = jnp.concatenate(
            [from_left(4 * c + j) for j in range(4)]
            + [v1_ref[c][2:12]]
            + [from_right(4 * c + j) for j in range(4)],
            axis=0,
        )
        beta = jnp.concatenate([zero, from_left(12 + c), beta1_ref[c], from_right(12 + c), zero], axis=0)
        slabs = []
        for j in range(10):
            row = e2_s[c, pl.ds(5 + 4 * odd + j, 1), :]
            slab = jnp.take_along_axis(jnp.broadcast_to(row, (8, 128)), spread, axis=1)[None]
            slabs += [slab, slab]
        e = jnp.concatenate(slabs[1:19], axis=0)
        m = sol * (kappa[c] / 26.5)
        v = v + (root1 * sol) * e
        d = INV_MID * (beta - m * stencil1(v))
        v = v + d
        d = A1 * d + C1 * (beta - m * stencil1(v))
        v = v + d
        d = A2 * d + C2 * (beta - m * stencil1(v))
        v = v + d
        e = jnp.where(sol > 0.0, v / root1, e)[3:15]
        pe_s[c, :, pl.ds(0, 8, 2), :] = e
        pe_s[c, :, pl.ds(1, 8, 2), :] = e

    shift = HALO - 4

    def sol0(k):
        row = jnp.where(k < 4, rows["left"], jnp.where(k < 20, rows["own"], rows["right"]))
        return jnp.broadcast_to(row, (16, 128))

    def begin(k, _):
        g = root0_ref[k + shift] * sol0(k)
        for c in range(3):
            a_s[c, k] = v0_ref[c, k + shift] + g * pe_s[c, k >> 1]
        return 0

    lax.fori_loop(1, 23, begin, 0, unroll=11)

    def stencil0(ref, c, k):
        mid = ref[c, k]
        s = ref[c, k - 1] + mid + ref[c, k + 1]
        return mid, 27.5 * mid - lane_sum(row_sum(s), 1, 128)

    def app0(k, _):
        sol = sol0(k)
        for c in range(3):
            v, t = stencil0(a_s, c, k)
            d = INV_MID * (beta0_ref[c, k + shift] - (sol * (kappa[c] / 26.5)) * t)
            d_s[c, k] = d
            bb_s[c, k] = v + d
        return 0

    lax.fori_loop(2, 22, app0, 0, unroll=10)

    def app1(k, _):
        sol = sol0(k)
        for c in range(3):
            v, t = stencil0(bb_s, c, k)
            pre = beta0_ref[c, k + shift] - (sol * (kappa[c] / 26.5)) * t
            d = A1 * d_s[c, k] + C1 * pre
            d_s[c, k] = d
            a_s[c, k] = v + d
        return 0

    lax.fori_loop(3, 21, app1, 0, unroll=9)
    own_solid = jnp.broadcast_to(rows["own"], (16, 128))

    def app2(k, _):
        inverse = 1.0 / root0_ref[k + shift]
        x = []
        for c in range(3):
            v, t = stencil0(a_s, c, k)
            pre = beta0_ref[c, k + shift] - (own_solid * (kappa[c] / 26.5)) * t
            v = v + A2 * d_s[c, k] + C2 * pre
            x.append(jnp.where(own_solid > 0.0, v * inverse, pe_s[c, k >> 1]))
        third = x[2] * (1.0 / 3.0)
        out_ref[0, k - 4] = x[0] + third
        out_ref[1, k - 4] = x[1] + third
        out_ref[2, k - 4] = third - x[0] - x[1]
        return 0

    lax.fori_loop(4, 20, app2, 0, unroll=8)


VMEM = pl.BlockSpec(memory_space=pltpu.VMEM)
HBM = pl.BlockSpec(memory_space=pltpu.HBM)
PARAMS = pltpu.CompilerParams(vmem_limit_bytes=40 * 2**20)


def shaped(*shape):
    return jax.ShapeDtypeStruct(shape, F32)


def swap_bits(values, bits):
    n = lax.axis_size("bricks")
    return lax.ppermute(values, "bricks", [(i, i ^ bits) for i in range(n)])


def swap_before(values, distance):
    n = lax.axis_size("bricks")
    pairs = []
    for i in range(0, n, 2):
        if i - distance >= 0:
            pairs += [(i, i - distance), (i - distance, i)]
    return lax.ppermute(values, "bricks", sorted(pairs))


def body(load_field, material_class, occupancy, moduli):
    x_msg, o_msg, root = pl.pallas_call(
        pack_kernel,
        out_shape=(shaped(38, 16, 128), shaped(38, 16, 128), shaped(17, 16, 128)),
        in_specs=[HBM, HBM, HBM, HBM],
        out_specs=(VMEM, VMEM, VMEM),
        scratch_shapes=[
            pltpu.VMEM((16, 16, 128), jnp.int32),
            pltpu.SMEM((1, 1, 8), jnp.int32),
            pltpu.SMEM((8,), F32),
            pltpu.SemaphoreType.DMA((9,)),
        ],
        compiler_params=pltpu.CompilerParams(vmem_limit_bytes=56 * 2**20),
        name="pack",
    )(load_field, material_class, occupancy, moduli)
    x_in = swap_bits(x_msg, 1)
    o_in = swap_before(o_msg, 1)
    msg, edge, *fine = pl.pallas_call(
        down_kernel,
        out_shape=(
            shaped(144, 128), shaped(120, 128),
            shaped(3, EXT, 16, 128), shaped(3, EXT, 16, 128), shaped(EXT, 16, 128),
            shaped(3, 14, 8, 128), shaped(3, 14, 8, 128), shaped(18, 8, 128), shaped(8, 128),
        ),
        in_specs=[VMEM] * 4,
        out_specs=(VMEM,) * 9,
        scratch_shapes=[
            pltpu.VMEM((3, EXT, 16, 128), F32),
            pltpu.VMEM((3, EXT, 16, 128), F32),
            pltpu.VMEM((3, EXT, 16, 128), F32),
            pltpu.VMEM((EXT, 16, 128), F32),
            pltpu.VMEM((3, 14, 16, 128), F32),
            pltpu.VMEM((18, 16, 128), F32),
        ],
        compiler_params=PARAMS,
        name="down",
    )(load_field, root, x_in, o_in)
    msg_in = swap_bits(msg, 1)
    edge_in = swap_before(edge, 1)
    row = jnp.concatenate([msg[:24], msg_in[:24]], axis=0)
    for bits in (2, 4, 12):
        row = jnp.concatenate([row, swap_bits(row, bits)], axis=0)
        if bits == 4:
            row, edge_in = lax.optimization_barrier((row, edge_in))
    far = swap_before(row, 15)
    far2 = swap_bits(far, 1)
    return pl.pallas_call(
        up_kernel,
        out_shape=shaped(3, 16, 16, 128),
        in_specs=[VMEM] * 12,
        out_specs=VMEM,
        scratch_shapes=[
            pltpu.VMEM((48, 24, 128), F32),
            pltpu.VMEM((5, 136, 128), F32),
            pltpu.VMEM((3, 144, 128), F32),
            pltpu.VMEM((3, 24, 128), F32),
            pltpu.VMEM((3, 12, 16, 128), F32),
            pltpu.VMEM((3, 24, 16, 128), F32),
            pltpu.VMEM((3, 24, 16, 128), F32),
            pltpu.VMEM((3, 24, 16, 128), F32),
        ],
        compiler_params=PARAMS,
        name="up",
    )(row, far, far2, msg_in, edge_in, *fine)


def solution(mesh):
    in_specs = (
        P(None, "bricks", None, None),
        P("bricks", None, None),
        P("bricks", None, None),
        P(),
    )
    out_specs = P(None, "bricks", None, None)
    return jax.shard_map(body, mesh=mesh, in_specs=in_specs, out_specs=out_specs, check_vma=False)
```

```python
import jax
import jax.numpy as jnp
from jax import lax
from jax.experimental import pallas as pl
from jax.experimental.pallas import tpu as pltpu
from jax.sharding import PartitionSpec as P

F32 = jnp.float32
center = 26.5 / 27.0
cheb_mid = 1.65
cheb_half = 1.35
sigma = cheb_mid / cheb_half
kappa = (0.75, 0.75, 1.5)
HALO = 10
EXT = 16 + 2 * HALO


def cheb_pairs():
    rho, out = 1.0 / sigma, []
    for _ in range(2):
        new = 1.0 / (2.0 * sigma - rho)
        out.append((new * rho, 2.0 * new / cheb_half))
        rho = new
    return out


(A1, C1), (A2, C2) = cheb_pairs()
INV_MID = 1.0 / cheb_mid


def iota(shape, axis):
    return lax.broadcasted_iota(jnp.int32, shape, axis)


def lane_sum(s, step, period):
    axis = s.ndim - 1
    lane = iota((1,) * axis + (128,), axis) & (period - 1)
    low = jnp.where(lane >= step, 1.0, 0.0).astype(F32)
    high = jnp.where(lane < period - step, 1.0, 0.0).astype(F32)
    return s + low * pltpu.roll(s, step, axis) + high * pltpu.roll(s, 128 - step, axis)


def row_sum(s):
    axis = s.ndim - 2
    n = s.shape[axis]
    row = iota(s.shape, axis)
    before = jnp.where(row >= 1, pltpu.roll(s, 1, axis), 0.0)
    after = jnp.where(row < n - 1, pltpu.roll(s, n - 1, axis), 0.0)
    return s + before + after


def lane_pair(s, step):
    axis = s.ndim - 1
    upper = (iota(s.shape, axis) & step) != 0
    return s + jnp.where(upper, pltpu.roll(s, step, axis), pltpu.roll(s, 128 - step, axis))


def safe(root):
    return jnp.where(root > 0.0, root, 1.0)


def pack_kernel(load_ref, class_ref, occ_ref, moduli_ref, x_ref, o_ref, root_ref, class_s, occ_s, moduli_s, sems):
    odd = lax.axis_index("bricks") & 1
    small = [
        pltpu.make_async_copy(class_ref, class_s, sems.at[0]),
        pltpu.make_async_copy(occ_ref, occ_s, sems.at[1]),
        pltpu.make_async_copy(moduli_ref, moduli_s, sems.at[2]),
    ]
    for copy in small:
        copy.start()
    large = []
    for k, (ref, first) in enumerate(((x_ref, 1 - odd), (o_ref, odd))):
        for c in range(3):
            copy = pltpu.make_async_copy(
                load_ref.at[c, pl.ds(first * 7, 9)], ref.at[pl.ds(9 * c, 9)], sems.at[3 + 3 * k + c]
            )
            copy.start()
            large.append(copy)
    for copy in small:
        copy.wait()

    def fill(z, _):
        cls = class_s[z]
        modulus = jnp.zeros(cls.shape, F32)
        for k in range(8):
            modulus = jnp.where(cls == k, moduli_s[k], modulus)
        root_ref[z] = jnp.sqrt(modulus)
        return 0

    lax.fori_loop(0, 16, fill, 0, unroll=8)
    lane = iota((16, 128), 1) >> 4
    solid = jnp.zeros((16, 128), F32)
    for k in range(8):
        solid = jnp.where(lane == k, occ_s[0, 0, k].astype(F32), solid)
    root_ref[16] = solid
    x_ref[37] = solid
    o_ref[37] = solid
    for ref, first in ((x_ref, 1 - odd), (o_ref, odd)):
        for j in range(10):
            ref[27 + j] = root_ref[first * 6 + j]
    for copy in large:
        copy.wait()


def start0(e, loads, scale, b_ref, beta_ref, va_ref):
    total = loads[0] + loads[1] + loads[2]
    third = total * (1.0 / 3.0)
    for c, p in enumerate((loads[0] - third, loads[1] - third, total)):
        b_ref[c, e] = p
        beta = p * scale
        beta_ref[c, e] = beta
        va_ref[c, e] = beta * INV_MID


def stencil0(ref, c, e):
    mid = ref[c, e]
    s = ref[c, e - 1] + mid + ref[c, e + 1]
    return mid, 27.5 * mid - lane_sum(row_sum(s), 1, 128)


def first0(e, sol, beta_ref, va_ref, d_ref, vb_ref):
    for c in range(3):
        v, t = stencil0(va_ref, c, e)
        d = A1 * v + C1 * (beta_ref[c, e] - (sol * (kappa[c] / 26.5)) * t)
        d_ref[c, e] = d
        vb_ref[c, e] = v + d


def second0(e, sol, beta_ref, vb_ref, d_ref, v0_ref):
    for c in range(3):
        v, t = stencil0(vb_ref, c, e)
        pre = beta_ref[c, e] - (sol * (kappa[c] / 26.5)) * t
        v0_ref[c, e] = v + A2 * d_ref[c, e] + C2 * pre


def residual0(k, sols, root_ref, b_ref, v0_ref, t_ref):
    for c in range(3):
        total = None
        for j in range(2):
            e = 4 + 2 * k + j
            _, t = stencil0(v0_ref, c, e)
            r = b_ref[c, e] - (sols[j] * root_ref[e]) * (kappa[c] / 27.0) * t
            total = r if total is None else total + r
        t_ref[c, k] = total


def inner_kernel(load_ref, own_ref, b_ref, beta_ref, root0_ref, va_ref, d_ref, vb_ref, v0_ref, t_ref):
    solid = own_ref[16]

    def start(z, _):
        root = own_ref[z]
        root0_ref[z + HALO] = root
        scale = solid / (center * root)
        start0(z + HALO, [load_ref[c, z] for c in range(3)], scale, b_ref, beta_ref, va_ref)
        return 0

    lax.fori_loop(0, 16, start, 0, unroll=8)

    def app1(e, _):
        first0(e, solid, beta_ref, va_ref, d_ref, vb_ref)
        return 0

    lax.fori_loop(HALO + 1, HALO + 15, app1, 0, unroll=7)

    def app2(e, _):
        second0(e, solid, beta_ref, vb_ref, d_ref, v0_ref)
        return 0

    lax.fori_loop(HALO + 2, HALO + 14, app2, 0, unroll=6)

    def resid(k, _):
        residual0(k, (solid, solid), root0_ref, b_ref, v0_ref, t_ref)
        return 0

    lax.fori_loop(5, 9, resid, 0, unroll=4)


def down_kernel(
    own_ref, x_ref, o_ref, b_in, beta_in, root_in, va_in, d_in, vb_in, v0_in, t_in,
    b_ref, beta0_ref, root0_ref, va_ref, d_ref, vb_ref, v0_ref, t_s,
    msg_ref, edge_ref, v1_ref, beta1_ref, root1_ref, sol_ref,
    sol_s, tr_s,
):
    odd = lax.axis_index("bricks") & 1
    is_odd = odd == 1

    def left(k):
        return jnp.where(is_odd, x_ref[k], o_ref[k])

    def right(k):
        return jnp.where(is_odd, o_ref[k], x_ref[k])

    own_solid = own_ref[16]
    left_solid, right_solid = left(37), right(37)
    sol_ref[...] = jnp.zeros((8, 128), F32)
    sol_ref[0:1, :] = left_solid[:1]
    sol_ref[1:2, :] = own_solid[:1]
    sol_ref[2:3, :] = right_solid[:1]
    for j in range(HALO):
        sol_s[j] = left_solid
        sol_s[26 + j] = right_solid
        sol_s[HALO + j if j < 5 else 16 + j] = own_solid
        root0_ref[j] = safe(left(27 + j))
        root0_ref[26 + j] = safe(right(27 + j))
    for j in range(9):
        for e, side, solid in ((1 + j, left, left_solid), (26 + j, right, right_solid)):
            scale = solid / (center * root0_ref[e])
            start0(e, [side(9 * c + j) for c in range(3)], scale, b_ref, beta0_ref, va_ref)

    def app1(j, _):
        for e in (2 + j, 25 + j):
            first0(e, sol_s[e], beta0_ref, va_ref, d_ref, vb_ref)
        return 0

    lax.fori_loop(0, 9, app1, 0, unroll=9)

    def app2(j, _):
        for e in (3 + j, 24 + j):
            second0(e, sol_s[e], beta0_ref, vb_ref, d_ref, v0_ref)
        return 0

    lax.fori_loop(0, 9, app2, 0, unroll=9)

    def resid(j, _):
        for k in (j, 9 + j):
            e = 4 + 2 * k
            residual0(k, (sol_s[e], sol_s[e + 1]), root0_ref, b_ref, v0_ref, t_s)
        return 0

    lax.fori_loop(0, 5, resid, 0, unroll=5)

    def root_pair(k, _):
        tr_s[k] = root0_ref[2 * k] + root0_ref[2 * k + 1]
        return 0

    lax.fori_loop(0, 18, root_pair, 0, unroll=18)

    root1 = lane_pair(tr_s[:, pl.ds(0, 8, 2), :] + tr_s[:, pl.ds(1, 8, 2), :], 1) * 0.125
    root1_ref[...] = root1
    rt = root1[2:16]
    sol = jnp.concatenate(
        [
            jnp.broadcast_to(left_solid[None, :8], (3, 8, 128)),
            jnp.broadcast_to(own_solid[None, :8], (8, 8, 128)),
            jnp.broadcast_to(right_solid[None, :8], (3, 8, 128)),
        ],
        axis=0,
    )
    scale1 = sol / (0.25 * center * rt)
    zero = jnp.zeros((1, 8, 128), F32)

    def stencil1(v):
        before = jnp.concatenate([zero, v[:-1]], axis=0)
        after = jnp.concatenate([v[1:], zero], axis=0)
        return 27.5 * v - lane_sum(row_sum(before + v + after), 2, 128)

    gather = 4 * (iota((8, 128), 1) & 31)
    group = (iota((8, 128), 1) >> 5) == (iota((8, 128), 0) >> 1)

    def compact(q):
        q = q + pltpu.roll(q, 126, 1)
        q = jnp.take_along_axis(q, gather, axis=1)
        return jnp.sum(jnp.where(group, q, 0.0), axis=0, keepdims=True) * 0.125

    odd_lane = (iota((8, 128), 1) & 1) == 1
    to_after, to_before = [], []

    def pair(a, b):
        return jnp.where(odd_lane, b, a)

    def send_edge(k, after, before):
        msg_ref[24 + 8 * k : 32 + 8 * k, :] = jnp.where(is_odd, before, after)
        edge_ref[8 * k : 8 * k + 8, :] = jnp.where(is_odd, after, before)

    for c in range(3):
        b1 = lane_pair(t_s[c, :, pl.ds(0, 8, 2), :] + t_s[c, :, pl.ds(1, 8, 2), :], 1) * 0.125
        beta = b1 * scale1
        m = sol * (kappa[c] / 26.5)
        v = beta * INV_MID
        d = A1 * v + C1 * (beta - m * stencil1(v))
        v = v + d
        d = A2 * d + C2 * (beta - m * stencil1(v))
        v = v + d
        v1_ref[c] = v
        beta1_ref[c] = beta
        r = (b1 - (sol * rt) * (0.25 * kappa[c] / 27.0) * stencil1(v))[3:11]
        for z in range(4):
            msg_ref[4 * c + z : 4 * c + z + 1, :] = compact(r[2 * z] + r[2 * z + 1])
        for j in range(2):
            send_edge(2 * c + j, pair(v[6 + 2 * j], v[7 + 2 * j]), pair(v[4 + 2 * j], v[5 + 2 * j]))
        to_after.append(beta[7])
        to_before.append(beta[6])
    send_edge(6, pair(*to_after[:2]), pair(*to_before[:2]))
    send_edge(7, to_after[2], to_before[2])
    for z in range(4):
        msg_ref[12 + z : 13 + z, :] = compact(root1[5 + 2 * z] + root1[6 + 2 * z])
    msg_ref[16:24, :] = jnp.take_along_axis(own_solid[:8], gather, axis=1)


def up_kernel(
    row_ref, far_ref, far2_ref, msg_in_ref,
    v0_ref, beta0_ref, root0_ref, v1_ref, beta1_ref, root1_ref, sol_ref,
    out_ref,
    all_s, solid_s, w_s, f_s, e2_s, pe_s, a_s, bb_s, d_s,
):
    me = lax.axis_index("bricks")
    odd = me & 1
    is_odd = odd == 1

    for t in range(16):
        rows = slice(16 * t, 16 * t + 16)
        far, far2 = far_ref[rows, :], far2_ref[rows, :]
        all_s[t] = jnp.where(is_odd, far2, far)
        all_s[16 + t] = row_ref[rows, :]
        all_s[32 + t] = jnp.where(is_odd, far, far2)
    far, far2 = far_ref[256:272, :], far2_ref[256:272, :]
    solid_s[0:16, :] = jnp.where(is_odd, far2, far)
    solid_s[16:32, :] = row_ref[256:272, :]
    solid_s[32:48, :] = jnp.where(is_odd, far, far2)
    base = me - odd - 16
    here = (me >> 1) & 7
    for w in range(34):
        dev = base + w
        rel = (dev >> 4) - (me >> 4)
        chip = (dev >> 1) & 7
        holder = jnp.where(rel == 0, odd, jnp.where(rel < 0, 0, 1))
        beside = (chip ^ here) & 1
        via = (chip + beside * (1 - 2 * holder)) & 7
        x = via ^ here
        block = ((w & 1) ^ holder ^ beside) + 2 * beside + 4 * (((x >> 1) ^ (x >> 2)) & 1) + 8 * (x >> 2)
        slot = (rel + 1) * 16 + block
        for c in range(4):
            w_s[c, 4 * w : 4 * w + 4, :] = all_s[slot, 4 * c : 4 * c + 4, :]
        w_s[4, 4 * w : 4 * w + 4, :] = jnp.broadcast_to(solid_s[pl.ds(slot, 1), :], (4, 128))

    lane = iota((1, 1, 128), 2)

    def lane_mask(cond):
        return jnp.where(cond, 1.0, 0.0).astype(F32)

    masks_x = (lane_mask(lane >= 32), lane_mask(lane < 96))
    masks_y = {
        level: (lane_mask((lane & 31) >= step), lane_mask((lane & 31) < 32 - step))
        for level, step in ((2, 1), (3, 2), (4, 4), (5, 8))
    }
    scale27 = jnp.concatenate([jnp.full((1, 1, 128), k, F32) for k in kappa], axis=0)
    by26 = scale27 * (1.0 / 26.5)

    def stencil(v, level):
        n = v.shape[1]
        s = v + pltpu.roll(v, 1, 1) + pltpu.roll(v, n - 1, 1)
        if level == 2:
            s = s + masks_x[0] * pltpu.roll(s, 32, 2) + masks_x[1] * pltpu.roll(s, 96, 2)
        else:
            s = s + pltpu.roll(s, 64, 2)
        step = 2 ** (level - 2)
        low, high = masks_y[level]
        s = s + low * pltpu.roll(s, step, 2) + high * pltpu.roll(s, 128 - step, 2)
        return 27.5 * v - s

    def first(beta, m, level):
        v = beta * INV_MID
        d = A1 * v + C1 * (beta - m * stencil(v, level))
        v = v + d
        d = A2 * d + C2 * (beta - m * stencil(v, level))
        return v + d

    def again(v, beta, m, level):
        d = INV_MID * (beta - m * stencil(v, level))
        v = v + d
        d = A1 * d + C1 * (beta - m * stencil(v, level))
        v = v + d
        d = A2 * d + C2 * (beta - m * stencil(v, level))
        return v + d

    def coarsen(values, level):
        k, n = values.shape[:2]
        half = (n // 2 + 7) // 8 * 8
        if 2 * half > n:
            f_s[0:k, n : 2 * half, :] = jnp.zeros((k, 2 * half - n, 128), F32)
        f_s[0:k, 0:n, :] = values
        s = f_s[0:k, pl.ds(0, half, 2), :] + f_s[0:k, pl.ds(1, half, 2), :]
        s = lane_pair(s, 2 ** (level - 2))
        if level == 2:
            return lane_pair(s, 32) * 0.125
        return s * 0.25

    def refine(values, first_row, count):
        n = values.shape[1]
        f_s[0:3, pl.ds(0, n, 2), :] = values
        f_s[0:3, pl.ds(1, n, 2), :] = values
        return f_s[0:3, first_row : first_row + count, :]

    both = w_s[3:5]
    roots, sols = {2: safe(both[0:1])}, {2: both[1:2]}
    for level in (2, 3, 4):
        both = coarsen(jnp.concatenate([roots[level], sols[level]], axis=0), level)
        roots[level + 1], sols[level + 1] = safe(both[0:1]), both[1:2]
    sol5 = sols[5]
    sol5_safe = jnp.where(sol5 > 0.0, sol5, 1.0)
    inverse = {level: 1.0 / roots[level] for level in (2, 3, 4, 5)}
    powers = {level: (sols[level], sols[level]) for level in (2, 3, 4)}
    powers[5] = (sol5 * sol5, sol5 * sol5 * sol5)
    g5 = jnp.where(sol5 > 0.0, inverse[5] / sol5_safe, 0.0)
    scales = {level: powers[level][0] * inverse[level] * (1.0 / (0.25**level * center)) for level in (2, 3, 4, 5)}
    masks = {level: powers[level][1] * by26 for level in (2, 3, 4, 5)}
    windows = {4: (0, 40), 3: (24, 48), 2: (56, 80)}

    b = w_s[0:3]
    betas, vs = {}, {}
    for level in (2, 3, 4):
        beta = b * scales[level]
        v = first(beta, masks[level], level)
        r = b - (sols[level] * roots[level]) * (scale27 * (0.25**level / 27.0)) * stencil(v, level)
        betas[level], vs[level] = beta, v
        b = coarsen(r, level)
    e = first(b * scales[5], masks[5], 5) * g5
    first_row = 0
    for level in (4, 3, 2):
        lo, hi = windows[level]
        e = refine(e, lo - first_row, hi - lo)
        root, sol = roots[level][:, lo:hi], sols[level][:, lo:hi]
        v = vs[level][:, lo:hi] + (root * sol) * e
        v = again(v, betas[level][:, lo:hi], masks[level][:, lo:hi], level)
        e = jnp.where(sol > 0.0, v * inverse[level][:, lo:hi], e)
        first_row = 2 * lo
    e2_s[...] = e

    rows = {}
    for k, name in enumerate(("left", "own", "right")):
        rows[name] = sol_ref[k : k + 1, :]

    def layers(name, n):
        return jnp.broadcast_to(rows[name][None], (n, 8, 128))

    sol = jnp.concatenate([layers("left", 5), layers("own", 8), layers("right", 5)], axis=0)
    root1 = root1_ref[...]
    spread = (iota((8, 128), 0) >> 1) * 32 + (iota((8, 128), 1) >> 2)
    zero = jnp.zeros((1, 8, 128), F32)

    def stencil1(v):
        before = jnp.concatenate([zero, v[:-1]], axis=0)
        after = jnp.concatenate([v[1:], zero], axis=0)
        return 27.5 * v - lane_sum(row_sum(before + v + after), 2, 128)

    odd_lane = (iota((8, 128), 1) & 1) == 1
    across = jnp.where(is_odd, here == 7, here == 0)

    def edge_slabs(k, left):
        mine = msg_in_ref[24 + 8 * k : 32 + 8 * k, :]
        other = jnp.where(across, far_ref[272 + 8 * k : 280 + 8 * k, :], row_ref[272 + 8 * k : 280 + 8 * k, :])
        p = jnp.where(is_odd == left, mine, other)
        first = jnp.where(odd_lane, pltpu.roll(p, 1, 1), p)
        second = jnp.where(odd_lane, p, pltpu.roll(p, 127, 1))
        return [first[None], second[None]]

    edges = {}
    for left in (True, False):
        slabs = [edge_slabs(k, left) for k in range(8)]
        edges[left] = [slabs[2 * c] + slabs[2 * c + 1] for c in range(3)], [slabs[6][0], slabs[6][1], slabs[7][0]]

    for c in range(3):
        v = jnp.concatenate(
            edges[True][0][c] + [v1_ref[c][2:12]] + edges[False][0][c],
            axis=0,
        )
        beta = jnp.concatenate([zero, edges[True][1][c], beta1_ref[c], edges[False][1][c], zero], axis=0)
        slabs = []
        for j in range(10):
            row = e2_s[c, pl.ds(5 + 4 * odd + j, 1), :]
            slab = jnp.take_along_axis(jnp.broadcast_to(row, (8, 128)), spread, axis=1)[None]
            slabs += [slab, slab]
        e = jnp.concatenate(slabs[1:19], axis=0)
        m = sol * (kappa[c] / 26.5)
        v = v + (root1 * sol) * e
        d = INV_MID * (beta - m * stencil1(v))
        v = v + d
        d = A1 * d + C1 * (beta - m * stencil1(v))
        v = v + d
        d = A2 * d + C2 * (beta - m * stencil1(v))
        v = v + d
        e = jnp.where(sol > 0.0, v / root1, e)[3:15]
        pe_s[c, :, pl.ds(0, 8, 2), :] = e
        pe_s[c, :, pl.ds(1, 8, 2), :] = e

    shift = HALO - 4

    def sol0(k):
        row = jnp.where(k < 4, rows["left"], jnp.where(k < 20, rows["own"], rows["right"]))
        return jnp.broadcast_to(row, (16, 128))

    def begin(k, _):
        g = root0_ref[k + shift] * sol0(k)
        for c in range(3):
            a_s[c, k] = v0_ref[c, k + shift] + g * pe_s[c, k >> 1]
        return 0

    lax.fori_loop(1, 23, begin, 0, unroll=11)

    def app0(k, _):
        sol = sol0(k)
        for c in range(3):
            v, t = stencil0(a_s, c, k)
            d = INV_MID * (beta0_ref[c, k + shift] - (sol * (kappa[c] / 26.5)) * t)
            d_s[c, k] = d
            bb_s[c, k] = v + d
        return 0

    lax.fori_loop(2, 22, app0, 0, unroll=10)

    def app1(k, _):
        sol = sol0(k)
        for c in range(3):
            v, t = stencil0(bb_s, c, k)
            pre = beta0_ref[c, k + shift] - (sol * (kappa[c] / 26.5)) * t
            d = A1 * d_s[c, k] + C1 * pre
            d_s[c, k] = d
            a_s[c, k] = v + d
        return 0

    lax.fori_loop(3, 21, app1, 0, unroll=9)
    own_solid = jnp.broadcast_to(rows["own"], (16, 128))

    def app2(k, _):
        inverse = 1.0 / root0_ref[k + shift]
        x = []
        for c in range(3):
            v, t = stencil0(a_s, c, k)
            pre = beta0_ref[c, k + shift] - (own_solid * (kappa[c] / 26.5)) * t
            v = v + A2 * d_s[c, k] + C2 * pre
            x.append(jnp.where(own_solid > 0.0, v * inverse, pe_s[c, k >> 1]))
        third = x[2] * (1.0 / 3.0)
        out_ref[0, k - 4] = x[0] + third
        out_ref[1, k - 4] = x[1] + third
        out_ref[2, k - 4] = third - x[0] - x[1]
        return 0

    lax.fori_loop(4, 20, app2, 0, unroll=8)


VMEM = pl.BlockSpec(memory_space=pltpu.VMEM)
HBM = pl.BlockSpec(memory_space=pltpu.HBM)
PARAMS = pltpu.CompilerParams(vmem_limit_bytes=40 * 2**20)


def shaped(*shape):
    return jax.ShapeDtypeStruct(shape, F32)


def swap_bits(values, bits):
    n = lax.axis_size("bricks")
    return lax.ppermute(values, "bricks", [(i, i ^ bits) for i in range(n)])


def swap_before(values):
    n = lax.axis_size("bricks")
    return lax.ppermute(values, "bricks", [(i, i + 1 if i % 2 else i - 1) for i in range(1, n - 1)])


def swap_ring(values):
    n = lax.axis_size("bricks")
    pairs = []
    for i in range(0, n, 2):
        j = i // 16 * 16 + (i - 1) % 16
        pairs += [(i, j), (j, i)]
    return lax.ppermute(values, "bricks", sorted(pairs))


def next_rows(values):
    n = lax.axis_size("bricks")
    pairs = [(i, i + 16 if i % 2 == 0 else i - 16) for i in range(n)]
    return lax.ppermute(values, "bricks", [(i, j) for i, j in pairs if 0 <= j < n])


def body(load_field, material_class, occupancy, moduli):
    x_msg, o_msg, root = pl.pallas_call(
        pack_kernel,
        out_shape=(shaped(38, 16, 128), shaped(38, 16, 128), shaped(17, 16, 128)),
        in_specs=[HBM, HBM, HBM, HBM],
        out_specs=(VMEM,) * 3,
        scratch_shapes=[
            pltpu.VMEM((16, 16, 128), jnp.int32),
            pltpu.SMEM((1, 1, 8), jnp.int32),
            pltpu.SMEM((8,), F32),
            pltpu.SemaphoreType.DMA((9,)),
        ],
        compiler_params=pltpu.CompilerParams(vmem_limit_bytes=56 * 2**20),
        name="pack",
    )(load_field, material_class, occupancy, moduli)
    x_in = swap_bits(x_msg, 1)
    o_in = swap_before(o_msg)
    ext = shaped(3, EXT, 16, 128)
    fine = (ext, ext, shaped(EXT, 16, 128), ext, ext, ext, ext, shaped(3, 14, 16, 128))
    inner = pl.pallas_call(
        inner_kernel,
        out_shape=fine,
        in_specs=[VMEM] * 2,
        out_specs=(VMEM,) * 8,
        compiler_params=PARAMS,
        cost_estimate=pl.CostEstimate(flops=10_000_000, bytes_accessed=4_000_000, transcendentals=0),
        name="inner",
    )(load_field, root)
    _, beta0, root0, _, _, _, v0, _, msg, edge, v1, beta1, root1, solid_rows = pl.pallas_call(
        down_kernel,
        out_shape=fine
        + (
            shaped(88, 128), shaped(64, 128),
            shaped(3, 14, 8, 128), shaped(3, 14, 8, 128), shaped(18, 8, 128), shaped(8, 128),
        ),
        in_specs=[VMEM] * 11,
        out_specs=(VMEM,) * 14,
        input_output_aliases={3 + k: k for k in range(8)},
        scratch_shapes=[
            pltpu.VMEM((EXT, 16, 128), F32),
            pltpu.VMEM((18, 16, 128), F32),
        ],
        compiler_params=PARAMS,
        name="down",
    )(root, x_in, o_in, *inner)
    row_of = iota((8, 128), 0)

    def joined(a, b, bit):
        return jnp.where((row_of & bit) == 0, a, b)

    msg_in = swap_bits(msg, 1)
    blocks = jnp.concatenate([msg[:16], msg_in[:16]], axis=0)
    solids = joined(msg[16:24], msg_in[16:24], 1)
    got = swap_ring(jnp.concatenate([blocks, solids, edge], axis=0))
    blocks = jnp.concatenate([blocks, got[:32]], axis=0)
    solids = joined(solids, got[32:40], 2)
    edge_in = got[40:]
    got = swap_bits(jnp.concatenate([blocks, solids], axis=0), 4)
    blocks = jnp.concatenate([blocks, got[:64]], axis=0)
    solids = joined(solids, got[64:], 4)
    got = swap_bits(jnp.concatenate([blocks, solids], axis=0), 12)
    row = jnp.concatenate([blocks, got[:128], solids, got[128:], edge_in], axis=0)
    far = next_rows(row)
    far2 = swap_bits(far, 1)
    return pl.pallas_call(
        up_kernel,
        out_shape=shaped(3, 16, 16, 128),
        in_specs=[VMEM] * 11,
        out_specs=VMEM,
        scratch_shapes=[
            pltpu.VMEM((48, 16, 128), F32),
            pltpu.VMEM((48, 128), F32),
            pltpu.VMEM((5, 136, 128), F32),
            pltpu.VMEM((3, 144, 128), F32),
            pltpu.VMEM((3, 24, 128), F32),
            pltpu.VMEM((3, 12, 16, 128), F32),
            pltpu.VMEM((3, 24, 16, 128), F32),
            pltpu.VMEM((3, 24, 16, 128), F32),
            pltpu.VMEM((3, 24, 16, 128), F32),
        ],
        compiler_params=PARAMS,
        name="up",
    )(row, far, far2, msg_in, v0, beta0, root0, v1, beta1, root1, solid_rows)


def solution(mesh):
    in_specs = (
        P(None, "bricks", None, None),
        P("bricks", None, None),
        P("bricks", None, None),
        P(),
    )
    out_specs = P(None, "bricks", None, None)
    return jax.shard_map(body, mesh=mesh, in_specs=in_specs, out_specs=out_specs, check_vma=False)
```

```python
import jax
import jax.numpy as jnp
from jax import lax
from jax.experimental import pallas as pl
from jax.experimental.pallas import tpu as pltpu
from jax.sharding import PartitionSpec as P

F32 = jnp.float32
center = 26.5 / 27.0
cheb_mid = 1.65
cheb_half = 1.35
sigma = cheb_mid / cheb_half
kappa = (0.75, 0.75, 1.5)
HALO = 10
EXT = 16 + 2 * HALO


def cheb_pairs():
    rho, out = 1.0 / sigma, []
    for _ in range(2):
        new = 1.0 / (2.0 * sigma - rho)
        out.append((new * rho, 2.0 * new / cheb_half))
        rho = new
    return out


(A1, C1), (A2, C2) = cheb_pairs()
INV_MID = 1.0 / cheb_mid


def iota(shape, axis):
    return lax.broadcasted_iota(jnp.int32, shape, axis)


def lane_sum(s, step, period):
    axis = s.ndim - 1
    lane = iota((1,) * axis + (128,), axis) & (period - 1)
    low = jnp.where(lane >= step, 1.0, 0.0).astype(F32)
    high = jnp.where(lane < period - step, 1.0, 0.0).astype(F32)
    return s + low * pltpu.roll(s, step, axis) + high * pltpu.roll(s, 128 - step, axis)


def row_sum(s):
    axis = s.ndim - 2
    n = s.shape[axis]
    row = iota(s.shape, axis)
    before = jnp.where(row >= 1, pltpu.roll(s, 1, axis), 0.0)
    after = jnp.where(row < n - 1, pltpu.roll(s, n - 1, axis), 0.0)
    return s + before + after


def lane_pair(s, step):
    axis = s.ndim - 1
    upper = (iota(s.shape, axis) & step) != 0
    return s + jnp.where(upper, pltpu.roll(s, step, axis), pltpu.roll(s, 128 - step, axis))


def safe(root):
    return jnp.where(root > 0.0, root, 1.0)


def pack_kernel(load_ref, class_ref, occ_ref, moduli_ref, x_ref, o_ref, root_ref, class_s, occ_s, moduli_s, sems):
    odd = lax.axis_index("bricks") & 1
    small = [
        pltpu.make_async_copy(class_ref, class_s, sems.at[0]),
        pltpu.make_async_copy(occ_ref, occ_s, sems.at[1]),
        pltpu.make_async_copy(moduli_ref, moduli_s, sems.at[2]),
    ]
    for copy in small:
        copy.start()
    large = []
    for k, (ref, first) in enumerate(((x_ref, 1 - odd), (o_ref, odd))):
        for c in range(3):
            copy = pltpu.make_async_copy(
                load_ref.at[c, pl.ds(first * 7, 9)], ref.at[pl.ds(9 * c, 9)], sems.at[3 + 3 * k + c]
            )
            copy.start()
            large.append(copy)
    for copy in small:
        copy.wait()

    def fill(z, _):
        cls = class_s[z]
        modulus = jnp.zeros(cls.shape, F32)
        for k in range(8):
            modulus = jnp.where(cls == k, moduli_s[k], modulus)
        root_ref[z] = jnp.sqrt(modulus)
        return 0

    lax.fori_loop(0, 16, fill, 0, unroll=8)
    lane = iota((16, 128), 1) >> 4
    solid = jnp.zeros((16, 128), F32)
    for k in range(8):
        solid = jnp.where(lane == k, occ_s[0, 0, k].astype(F32), solid)
    root_ref[16] = solid
    x_ref[37] = solid
    o_ref[37] = solid
    for ref, first in ((x_ref, 1 - odd), (o_ref, odd)):
        for j in range(10):
            ref[27 + j] = root_ref[first * 6 + j]
    for copy in large:
        copy.wait()


def start0(e, loads, scale, b_ref, beta_ref, va_ref):
    total = loads[0] + loads[1] + loads[2]
    third = total * (1.0 / 3.0)
    for c, p in enumerate((loads[0] - third, loads[1] - third, total)):
        b_ref[c, e] = p
        beta = p * scale
        beta_ref[c, e] = beta
        va_ref[c, e] = beta * INV_MID


def stencil0(ref, c, e):
    mid = ref[c, e]
    s = ref[c, e - 1] + mid + ref[c, e + 1]
    return mid, 27.5 * mid - lane_sum(row_sum(s), 1, 128)


def first0(e, sol, beta_ref, va_ref, d_ref, vb_ref):
    for c in range(3):
        v, t = stencil0(va_ref, c, e)
        d = A1 * v + C1 * (beta_ref[c, e] - (sol * (kappa[c] / 26.5)) * t)
        d_ref[c, e] = d
        vb_ref[c, e] = v + d


def second0(e, sol, beta_ref, vb_ref, d_ref, v0_ref):
    for c in range(3):
        v, t = stencil0(vb_ref, c, e)
        pre = beta_ref[c, e] - (sol * (kappa[c] / 26.5)) * t
        v0_ref[c, e] = v + A2 * d_ref[c, e] + C2 * pre


def residual0(k, sols, root_ref, b_ref, v0_ref, t_ref):
    for c in range(3):
        total = None
        for j in range(2):
            e = 4 + 2 * k + j
            _, t = stencil0(v0_ref, c, e)
            r = b_ref[c, e] - (sols[j] * root_ref[e]) * (kappa[c] / 27.0) * t
            total = r if total is None else total + r
        t_ref[c, k] = total


def side0(before, message, own_solid, b_ref, beta_ref, root0_ref, va_ref, d_ref, vb_ref, v0_ref, t_ref):
    side_solid = message[37]

    def at(after_e, before_e):
        return after_e + before * (before_e - after_e)

    first = at(26, 0)
    for j in range(HALO):
        root0_ref[first + j] = safe(message[27 + j])
    first = at(26, 1)
    for j in range(9):
        scale = side_solid / (center * root0_ref[first + j])
        start0(first + j, [message[9 * c + j] for c in range(3)], scale, b_ref, beta_ref, va_ref)
    sign = at(1, -1)
    for j in range(9):
        first0(at(25, 10) + sign * j, own_solid if j < 1 else side_solid, beta_ref, va_ref, d_ref, vb_ref)
    for j in range(9):
        second0(at(24, 11) + sign * j, own_solid if j < 2 else side_solid, beta_ref, vb_ref, d_ref, v0_ref)
    for j in range(5):
        sol = own_solid if j < 2 else side_solid
        residual0(at(9, 4) + sign * j, (sol, sol), root0_ref, b_ref, v0_ref, t_ref)


def inner_kernel(load_ref, own_ref, x_ref, b_ref, beta_ref, root0_ref, va_ref, d_ref, vb_ref, v0_ref, t_ref):
    odd = lax.axis_index("bricks") & 1
    solid = own_ref[16]

    def start(z, _):
        root = own_ref[z]
        root0_ref[z + HALO] = root
        scale = solid / (center * root)
        start0(z + HALO, [load_ref[c, z] for c in range(3)], scale, b_ref, beta_ref, va_ref)
        return 0

    lax.fori_loop(0, 16, start, 0, unroll=8)

    def app1(e, _):
        first0(e, solid, beta_ref, va_ref, d_ref, vb_ref)
        return 0

    lax.fori_loop(HALO + 1, HALO + 15, app1, 0, unroll=7)

    def app2(e, _):
        second0(e, solid, beta_ref, vb_ref, d_ref, v0_ref)
        return 0

    lax.fori_loop(HALO + 2, HALO + 14, app2, 0, unroll=6)

    def resid(k, _):
        residual0(k, (solid, solid), root0_ref, b_ref, v0_ref, t_ref)
        return 0

    lax.fori_loop(5, 9, resid, 0, unroll=4)
    side0(odd, x_ref, solid, b_ref, beta_ref, root0_ref, va_ref, d_ref, vb_ref, v0_ref, t_ref)


def down_kernel(
    own_ref, x_solid_ref, o_ref, b_in, beta_in, root_in, va_in, d_in, vb_in, v0_in, t_in,
    b_ref, beta0_ref, root0_ref, va_ref, d_ref, vb_ref, v0_ref, t_s,
    msg_ref, edge_ref, v1_ref, beta1_ref, root1_ref, sol_ref,
    tr_s,
):
    odd = lax.axis_index("bricks") & 1
    is_odd = odd == 1
    own_solid = own_ref[16]
    x_solid, o_solid = x_solid_ref[37], o_ref[37]
    left_solid = jnp.where(is_odd, x_solid, o_solid)
    right_solid = jnp.where(is_odd, o_solid, x_solid)
    sol_ref[...] = jnp.zeros((8, 128), F32)
    sol_ref[0:1, :] = left_solid[:1]
    sol_ref[1:2, :] = own_solid[:1]
    sol_ref[2:3, :] = right_solid[:1]
    side0(1 - odd, o_ref, own_solid, b_ref, beta0_ref, root0_ref, va_ref, d_ref, vb_ref, v0_ref, t_s)

    def root_pair(k, _):
        tr_s[k] = root0_ref[2 * k] + root0_ref[2 * k + 1]
        return 0

    lax.fori_loop(0, 18, root_pair, 0, unroll=18)

    root1 = lane_pair(tr_s[:, pl.ds(0, 8, 2), :] + tr_s[:, pl.ds(1, 8, 2), :], 1) * 0.125
    root1_ref[...] = root1
    rt = root1[2:16]
    sol = jnp.concatenate(
        [
            jnp.broadcast_to(left_solid[None, :8], (3, 8, 128)),
            jnp.broadcast_to(own_solid[None, :8], (8, 8, 128)),
            jnp.broadcast_to(right_solid[None, :8], (3, 8, 128)),
        ],
        axis=0,
    )
    scale1 = sol / (0.25 * center * rt)
    zero = jnp.zeros((1, 8, 128), F32)

    def stencil1(v):
        before = jnp.concatenate([zero, v[:-1]], axis=0)
        after = jnp.concatenate([v[1:], zero], axis=0)
        return 27.5 * v - lane_sum(row_sum(before + v + after), 2, 128)

    gather = 4 * (iota((8, 128), 1) & 31)
    group = (iota((8, 128), 1) >> 5) == (iota((8, 128), 0) >> 1)

    def compact(q):
        q = q + pltpu.roll(q, 126, 1)
        q = jnp.take_along_axis(q, gather, axis=1)
        return jnp.sum(jnp.where(group, q, 0.0), axis=0, keepdims=True) * 0.125

    odd_lane = (iota((8, 128), 1) & 1) == 1
    to_after, to_before = [], []

    def pair(a, b):
        return jnp.where(odd_lane, b, a)

    def send_edge(k, after, before):
        msg_ref[24 + 8 * k : 32 + 8 * k, :] = jnp.where(is_odd, before, after)
        edge_ref[8 * k : 8 * k + 8, :] = jnp.where(is_odd, after, before)

    for c in range(3):
        b1 = lane_pair(t_s[c, :, pl.ds(0, 8, 2), :] + t_s[c, :, pl.ds(1, 8, 2), :], 1) * 0.125
        beta = b1 * scale1
        m = sol * (kappa[c] / 26.5)
        v = beta * INV_MID
        d = A1 * v + C1 * (beta - m * stencil1(v))
        v = v + d
        d = A2 * d + C2 * (beta - m * stencil1(v))
        v = v + d
        v1_ref[c] = v
        beta1_ref[c] = beta
        r = (b1 - (sol * rt) * (0.25 * kappa[c] / 27.0) * stencil1(v))[3:11]
        for z in range(4):
            msg_ref[4 * c + z : 4 * c + z + 1, :] = compact(r[2 * z] + r[2 * z + 1])
        for j in range(2):
            send_edge(2 * c + j, pair(v[6 + 2 * j], v[7 + 2 * j]), pair(v[4 + 2 * j], v[5 + 2 * j]))
        to_after.append(beta[7])
        to_before.append(beta[6])
    send_edge(6, pair(*to_after[:2]), pair(*to_before[:2]))
    send_edge(7, to_after[2], to_before[2])
    for z in range(4):
        msg_ref[12 + z : 13 + z, :] = compact(root1[5 + 2 * z] + root1[6 + 2 * z])
    msg_ref[16:24, :] = jnp.take_along_axis(own_solid[:8], gather, axis=1)


def up_kernel(
    row_ref, far_ref, far2_ref, msg_in_ref,
    v0_ref, beta0_ref, root0_ref, v1_ref, beta1_ref, root1_ref, sol_ref,
    out_hbm,
    all_s, solid_s, w_s, coef_s, f_s, e2_s, pe_s, a_s, bb_s, d_s, out_ref, sems,
):
    me = lax.axis_index("bricks")
    odd = me & 1
    is_odd = odd == 1

    for t in range(16):
        rows = slice(16 * t, 16 * t + 16)
        far, far2 = far_ref[rows, :], far2_ref[rows, :]
        all_s[t] = jnp.where(is_odd, far2, far)
        all_s[16 + t] = row_ref[rows, :]
        all_s[32 + t] = jnp.where(is_odd, far, far2)
    far, far2 = far_ref[256:272, :], far2_ref[256:272, :]
    solid_s[0:16, :] = jnp.where(is_odd, far2, far)
    solid_s[16:32, :] = row_ref[256:272, :]
    solid_s[32:48, :] = jnp.where(is_odd, far, far2)
    chip0 = (me >> 1) - 8
    here = (me >> 1) & 7
    low_rows = iota((8, 128), 0) < 4
    for w in range(17):
        chip = chip0 + w
        rel = (chip >> 3) - (me >> 4)
        holder = jnp.where(rel == 0, odd, jnp.where(rel < 0, 0, 1))
        beside = (chip ^ here) & 1
        x = ((chip + beside * (1 - 2 * holder)) ^ here) & 7
        slot = (rel + 1) * 16 + 2 * beside + 4 * (((x >> 1) ^ (x >> 2)) & 1) + 8 * (x >> 2)
        flip = holder ^ beside
        blocks = (slot + flip, slot + 1 - flip)
        for half in range(2):
            first, second = (all_s[block, 8 * half : 8 * half + 8, :] for block in blocks)
            w_s[2 * half, 8 * w : 8 * w + 8, :] = jnp.where(low_rows, first, pltpu.roll(second, 4, 0))
            w_s[2 * half + 1, 8 * w : 8 * w + 8, :] = jnp.where(low_rows, pltpu.roll(first, 4, 0), second)
        solid = (jnp.broadcast_to(solid_s[pl.ds(block, 1), :], (8, 128)) for block in blocks)
        w_s[4, 8 * w : 8 * w + 8, :] = jnp.where(low_rows, *solid)

    lane = iota((1, 1, 128), 2)

    def lane_mask(cond):
        return jnp.where(cond, 1.0, 0.0).astype(F32)

    masks_x = (lane_mask(lane >= 32), lane_mask(lane < 96))
    masks_y = {
        level: (lane_mask((lane & 31) >= step), lane_mask((lane & 31) < 32 - step))
        for level, step in ((2, 1), (3, 2), (4, 4), (5, 8))
    }
    scale27 = jnp.concatenate([jnp.full((1, 1, 128), k, F32) for k in kappa], axis=0)
    by26 = scale27 * (1.0 / 26.5)

    def stencil(v, level):
        n = v.shape[1]
        s = v + pltpu.roll(v, 1, 1) + pltpu.roll(v, n - 1, 1)
        step = 2 ** (level - 2)
        low, high = masks_y[level]
        if level > 2:
            beside = low * (pltpu.roll(s, step, 2) + pltpu.roll(s, 64 + step, 2))
            beside = beside + high * (pltpu.roll(s, 128 - step, 2) + pltpu.roll(s, 64 - step, 2))
            return (27.5 * v - (s + pltpu.roll(s, 64, 2))) - beside
        lower, upper = masks_x
        s = s + lower * pltpu.roll(s, 32, 2) + upper * pltpu.roll(s, 96, 2)
        return 27.5 * v - (s + low * pltpu.roll(s, 1, 2) + high * pltpu.roll(s, 127, 2))

    def first(beta, m, level):
        v = beta * INV_MID
        d = A1 * v + C1 * (beta - m * stencil(v, level))
        v = v + d
        d = A2 * d + C2 * (beta - m * stencil(v, level))
        return v + d

    def again(v, beta, m, level):
        d = INV_MID * (beta - m * stencil(v, level))
        v = v + d
        d = A1 * d + C1 * (beta - m * stencil(v, level))
        v = v + d
        d = A2 * d + C2 * (beta - m * stencil(v, level))
        return v + d

    def coarsen(values, level, room):
        k, n = values.shape[:2]
        half = (n // 2 + 7) // 8 * 8
        if 2 * half > n:
            room[0:k, n : 2 * half, :] = jnp.zeros((k, 2 * half - n, 128), F32)
        room[0:k, 0:n, :] = values
        s = room[0:k, pl.ds(0, half, 2), :] + room[0:k, pl.ds(1, half, 2), :]
        s = lane_pair(s, 2 ** (level - 2))
        if level == 2:
            return lane_pair(s, 32) * 0.125
        return s * 0.25

    def refine(values, first_row, count):
        n = values.shape[1]
        f_s[0:3, pl.ds(0, n, 2), :] = values
        f_s[0:3, pl.ds(1, n, 2), :] = values
        return f_s[0:3, first_row : first_row + count, :]

    both = w_s[3:5]
    roots, sols = {2: safe(both[0:1])}, {2: both[1:2]}
    for level in (2, 3, 4):
        both = coarsen(jnp.concatenate([roots[level], sols[level]], axis=0), level, coef_s)
        roots[level + 1], sols[level + 1] = safe(both[0:1]), both[1:2]
    sol5 = sols[5]
    sol5_safe = jnp.where(sol5 > 0.0, sol5, 1.0)
    inverse = {level: 1.0 / roots[level] for level in (2, 3, 4, 5)}
    powers = {level: (sols[level], sols[level]) for level in (2, 3, 4)}
    powers[5] = (sol5 * sol5, sol5 * sol5 * sol5)
    g5 = jnp.where(sol5 > 0.0, inverse[5] / sol5_safe, 0.0)
    scales = {level: powers[level][0] * inverse[level] * (1.0 / (0.25**level * center)) for level in (2, 3, 4, 5)}
    masks = {level: powers[level][1] * by26 for level in (2, 3, 4, 5)}
    windows = {4: (0, 40), 3: (24, 48), 2: (56, 80)}

    b = w_s[0:3]
    betas, vs = {}, {}
    for level in (2, 3, 4):
        beta = b * scales[level]
        v = first(beta, masks[level], level)
        r = b - (sols[level] * roots[level]) * (scale27 * (0.25**level / 27.0)) * stencil(v, level)
        betas[level], vs[level] = beta, v
        b = coarsen(r, level, f_s)
    e = first(b * scales[5], masks[5], 5) * g5
    first_row = 0
    for level in (4, 3, 2):
        lo, hi = windows[level]
        e = refine(e, lo - first_row, hi - lo)
        root, sol = roots[level][:, lo:hi], sols[level][:, lo:hi]
        v = vs[level][:, lo:hi] + (root * sol) * e
        v = again(v, betas[level][:, lo:hi], masks[level][:, lo:hi], level)
        e = jnp.where(sol > 0.0, v * inverse[level][:, lo:hi], e)
        first_row = 2 * lo
    e2_s[...] = e

    rows = {}
    for k, name in enumerate(("left", "own", "right")):
        rows[name] = sol_ref[k : k + 1, :]

    def layers(name, n):
        return jnp.broadcast_to(rows[name][None], (n, 8, 128))

    sol = jnp.concatenate([layers("left", 5), layers("own", 8), layers("right", 5)], axis=0)
    root1 = root1_ref[...]
    spread = (iota((8, 128), 0) >> 1) * 32 + (iota((8, 128), 1) >> 2)
    zero = jnp.zeros((1, 8, 128), F32)

    def stencil1(v):
        before = jnp.concatenate([zero, v[:-1]], axis=0)
        after = jnp.concatenate([v[1:], zero], axis=0)
        return 27.5 * v - lane_sum(row_sum(before + v + after), 2, 128)

    odd_lane = (iota((8, 128), 1) & 1) == 1
    across = jnp.where(is_odd, here == 7, here == 0)

    def edge_slabs(k, left):
        mine = msg_in_ref[24 + 8 * k : 32 + 8 * k, :]
        other = jnp.where(across, far_ref[272 + 8 * k : 280 + 8 * k, :], row_ref[272 + 8 * k : 280 + 8 * k, :])
        p = jnp.where(is_odd == left, mine, other)
        first = jnp.where(odd_lane, pltpu.roll(p, 1, 1), p)
        second = jnp.where(odd_lane, p, pltpu.roll(p, 127, 1))
        return [first[None], second[None]]

    edges = {}
    for left in (True, False):
        slabs = [edge_slabs(k, left) for k in range(8)]
        edges[left] = [slabs[2 * c] + slabs[2 * c + 1] for c in range(3)], [slabs[6][0], slabs[6][1], slabs[7][0]]

    for c in range(3):
        v = jnp.concatenate(
            edges[True][0][c] + [v1_ref[c][2:12]] + edges[False][0][c],
            axis=0,
        )
        beta = jnp.concatenate([zero, edges[True][1][c], beta1_ref[c], edges[False][1][c], zero], axis=0)
        slabs = []
        for j in range(10):
            row = e2_s[c, pl.ds(5 + 4 * odd + j, 1), :]
            slab = jnp.take_along_axis(jnp.broadcast_to(row, (8, 128)), spread, axis=1)[None]
            slabs += [slab, slab]
        e = jnp.concatenate(slabs[1:19], axis=0)
        m = sol * (kappa[c] / 26.5)
        v = v + (root1 * sol) * e
        d = INV_MID * (beta - m * stencil1(v))
        v = v + d
        d = A1 * d + C1 * (beta - m * stencil1(v))
        v = v + d
        d = A2 * d + C2 * (beta - m * stencil1(v))
        v = v + d
        e = jnp.where(sol > 0.0, v / root1, e)[3:15]
        pe_s[c, :, pl.ds(0, 8, 2), :] = e
        pe_s[c, :, pl.ds(1, 8, 2), :] = e

    shift = HALO - 4

    broad = {name: jnp.broadcast_to(row, (16, 128)) for name, row in rows.items()}

    def sol0(k):
        return broad["left"] if k < 4 else broad["own"] if k < 20 else broad["right"]

    for k in range(1, 23):
        g = root0_ref[k + shift] * sol0(k)
        for c in range(3):
            a_s[c, k] = v0_ref[c, k + shift] + g * pe_s[c, k >> 1]


    for k in range(2, 22):
        sol = sol0(k)
        for c in range(3):
            v, t = stencil0(a_s, c, k)
            d = INV_MID * (beta0_ref[c, k + shift] - (sol * (kappa[c] / 26.5)) * t)
            d_s[c, k] = d
            bb_s[c, k] = v + d


    for k in range(3, 21):
        sol = sol0(k)
        for c in range(3):
            v, t = stencil0(bb_s, c, k)
            pre = beta0_ref[c, k + shift] - (sol * (kappa[c] / 26.5)) * t
            d = A1 * d_s[c, k] + C1 * pre
            d_s[c, k] = d
            a_s[c, k] = v + d

    own_solid = jnp.broadcast_to(rows["own"], (16, 128))

    copies = []
    for k in range(4, 20):
        inverse = 1.0 / root0_ref[k + shift]
        x = []
        for c in range(3):
            v, t = stencil0(a_s, c, k)
            pre = beta0_ref[c, k + shift] - (own_solid * (kappa[c] / 26.5)) * t
            v = v + A2 * d_s[c, k] + C2 * pre
            x.append(jnp.where(own_solid > 0.0, v * inverse, pe_s[c, k >> 1]))
        third = x[2] * (1.0 / 3.0)
        out_ref[0, k - 4] = x[0] + third
        out_ref[1, k - 4] = x[1] + third
        out_ref[2, k - 4] = third - x[0] - x[1]
        if k % 4 == 3:
            part = pl.ds(k - 7, 4)
            copy = pltpu.make_async_copy(out_ref.at[:, part], out_hbm.at[:, part], sems.at[k // 4 - 1])
            copy.start()
            copies.append(copy)
    for copy in copies:
        copy.wait()


VMEM = pl.BlockSpec(memory_space=pltpu.VMEM)
HBM = pl.BlockSpec(memory_space=pltpu.HBM)
PARAMS = pltpu.CompilerParams(vmem_limit_bytes=40 * 2**20)


def shaped(*shape):
    return jax.ShapeDtypeStruct(shape, F32)


def swap_bits(values, bits):
    n = lax.axis_size("bricks")
    return lax.ppermute(values, "bricks", [(i, i ^ bits) for i in range(n)])


def swap_before(values):
    n = lax.axis_size("bricks")
    return lax.ppermute(values, "bricks", [(i, i + 1 if i % 2 else i - 1) for i in range(1, n - 1)])


def swap_ring(values):
    n = lax.axis_size("bricks")
    pairs = []
    for i in range(0, n, 2):
        j = i // 16 * 16 + (i - 1) % 16
        pairs += [(i, j), (j, i)]
    return lax.ppermute(values, "bricks", sorted(pairs))


def next_rows(values):
    n = lax.axis_size("bricks")
    pairs = [(i, i + 16 if i % 2 == 0 else i - 16) for i in range(n)]
    return lax.ppermute(values, "bricks", [(i, j) for i, j in pairs if 0 <= j < n])


def body(load_field, material_class, occupancy, moduli):
    x_msg, o_msg, root = pl.pallas_call(
        pack_kernel,
        out_shape=(shaped(38, 16, 128), shaped(38, 16, 128), shaped(17, 16, 128)),
        in_specs=[HBM, HBM, HBM, HBM],
        out_specs=(VMEM,) * 3,
        scratch_shapes=[
            pltpu.VMEM((16, 16, 128), jnp.int32),
            pltpu.SMEM((1, 1, 8), jnp.int32),
            pltpu.SMEM((8,), F32),
            pltpu.SemaphoreType.DMA((9,)),
        ],
        compiler_params=pltpu.CompilerParams(vmem_limit_bytes=56 * 2**20),
        name="pack",
    )(load_field, material_class, occupancy, moduli)
    x_in = swap_bits(x_msg, 1)
    o_in = swap_before(o_msg)
    ext = shaped(3, EXT, 16, 128)
    fine = (ext, ext, shaped(EXT, 16, 128), ext, ext, ext, ext, shaped(3, 14, 16, 128))
    inner = pl.pallas_call(
        inner_kernel,
        out_shape=fine,
        in_specs=[VMEM] * 3,
        out_specs=(VMEM,) * 8,
        compiler_params=PARAMS,
        cost_estimate=pl.CostEstimate(flops=10_000_000, bytes_accessed=4_000_000, transcendentals=0),
        name="inner",
    )(load_field, root, x_in)
    _, beta0, root0, _, _, _, v0, _, msg, edge, v1, beta1, root1, solid_rows = pl.pallas_call(
        down_kernel,
        out_shape=fine
        + (
            shaped(88, 128), shaped(64, 128),
            shaped(3, 14, 8, 128), shaped(3, 14, 8, 128), shaped(18, 8, 128), shaped(8, 128),
        ),
        in_specs=[VMEM] * 11,
        out_specs=(VMEM,) * 14,
        input_output_aliases={3 + k: k for k in range(8)},
        scratch_shapes=[
            pltpu.VMEM((18, 16, 128), F32),
        ],
        compiler_params=PARAMS,
        name="down",
    )(root, x_in, o_in, *inner)
    row_of = iota((8, 128), 0)

    def joined(a, b, bit):
        return jnp.where((row_of & bit) == 0, a, b)

    msg_in = swap_bits(msg, 1)
    blocks = jnp.concatenate([msg[:16], msg_in[:16]], axis=0)
    solids = joined(msg[16:24], msg_in[16:24], 1)
    got = swap_ring(jnp.concatenate([blocks, solids, edge], axis=0))
    blocks = jnp.concatenate([blocks, got[:32]], axis=0)
    solids = joined(solids, got[32:40], 2)
    edge_in = got[40:]
    got = swap_bits(jnp.concatenate([blocks, solids], axis=0), 4)
    blocks = jnp.concatenate([blocks, got[:64]], axis=0)
    solids = joined(solids, got[64:], 4)
    got = swap_bits(jnp.concatenate([blocks, solids], axis=0), 12)
    row = jnp.concatenate([blocks, got[:128], solids, got[128:], edge_in], axis=0)
    far = next_rows(row)
    far2 = swap_bits(far, 1)
    return pl.pallas_call(
        up_kernel,
        out_shape=shaped(3, 16, 16, 128),
        in_specs=[VMEM] * 11,
        out_specs=HBM,
        scratch_shapes=[
            pltpu.VMEM((48, 16, 128), F32),
            pltpu.VMEM((48, 128), F32),
            pltpu.VMEM((5, 136, 128), F32),
            pltpu.VMEM((2, 144, 128), F32),
            pltpu.VMEM((3, 144, 128), F32),
            pltpu.VMEM((3, 24, 128), F32),
            pltpu.VMEM((3, 12, 16, 128), F32),
            pltpu.VMEM((3, 24, 16, 128), F32),
            pltpu.VMEM((3, 24, 16, 128), F32),
            pltpu.VMEM((3, 24, 16, 128), F32),
            pltpu.VMEM((3, 16, 16, 128), F32),
            pltpu.SemaphoreType.DMA((4,)),
        ],
        compiler_params=PARAMS,
        name="up",
    )(row, far, far2, msg_in, v0, beta0, root0, v1, beta1, root1, solid_rows)


def solution(mesh):
    in_specs = (
        P(None, "bricks", None, None),
        P("bricks", None, None),
        P("bricks", None, None),
        P(),
    )
    out_specs = P(None, "bricks", None, None)
    return jax.shard_map(body, mesh=mesh, in_specs=in_specs, out_specs=out_specs, check_vma=False)
```

```python
import jax
import jax.numpy as jnp
from jax import lax
from jax.experimental import pallas as pl
from jax.experimental.pallas import tpu as pltpu
from jax.sharding import PartitionSpec as P

F32 = jnp.float32
center = 26.5 / 27.0
cheb_mid = 1.65
cheb_half = 1.35
sigma = cheb_mid / cheb_half
kappa = (0.75, 0.75, 1.5)
HALO = 10
EXT = 16 + 2 * HALO


def cheb_pairs():
    rho, out = 1.0 / sigma, []
    for _ in range(2):
        new = 1.0 / (2.0 * sigma - rho)
        out.append((new * rho, 2.0 * new / cheb_half))
        rho = new
    return out


(A1, C1), (A2, C2) = cheb_pairs()
INV_MID = 1.0 / cheb_mid


def iota(shape, axis):
    return lax.broadcasted_iota(jnp.int32, shape, axis)


def lane_sum(s, step, period):
    axis = s.ndim - 1
    lane = iota((1,) * axis + (128,), axis) & (period - 1)
    low = jnp.where(lane >= step, 1.0, 0.0).astype(F32)
    high = jnp.where(lane < period - step, 1.0, 0.0).astype(F32)
    return s + low * pltpu.roll(s, step, axis) + high * pltpu.roll(s, 128 - step, axis)


def row_sum(s):
    axis = s.ndim - 2
    n = s.shape[axis]
    row = iota(s.shape, axis)
    before = jnp.where(row >= 1, pltpu.roll(s, 1, axis), 0.0)
    after = jnp.where(row < n - 1, pltpu.roll(s, n - 1, axis), 0.0)
    return s + before + after


def lane_pair(s, step):
    axis = s.ndim - 1
    upper = (iota(s.shape, axis) & step) != 0
    return s + jnp.where(upper, pltpu.roll(s, step, axis), pltpu.roll(s, 128 - step, axis))


def safe(root):
    return jnp.where(root > 0.0, root, 1.0)


def pack_kernel(load_ref, class_ref, occ_ref, moduli_ref, x_ref, o_ref, root_ref, class_s, occ_s, moduli_s, sems):
    odd = lax.axis_index("bricks") & 1
    small = [
        pltpu.make_async_copy(class_ref, class_s, sems.at[0]),
        pltpu.make_async_copy(occ_ref, occ_s, sems.at[1]),
        pltpu.make_async_copy(moduli_ref, moduli_s, sems.at[2]),
    ]
    for copy in small:
        copy.start()
    large = []
    for k, (ref, first) in enumerate(((x_ref, 1 - odd), (o_ref, odd))):
        for c in range(3):
            copy = pltpu.make_async_copy(
                load_ref.at[c, pl.ds(first * 7, 9)], ref.at[pl.ds(9 * c, 9)], sems.at[3 + 3 * k + c]
            )
            copy.start()
            large.append(copy)
    for copy in small:
        copy.wait()

    def fill(z, _):
        cls = class_s[z]
        modulus = jnp.zeros(cls.shape, F32)
        for k in range(8):
            modulus = jnp.where(cls == k, moduli_s[k], modulus)
        root_ref[z] = jnp.sqrt(modulus)
        return 0

    lax.fori_loop(0, 16, fill, 0, unroll=8)
    lane = iota((16, 128), 1) >> 4
    solid = jnp.zeros((16, 128), F32)
    for k in range(8):
        solid = jnp.where(lane == k, occ_s[0, 0, k].astype(F32), solid)
    root_ref[16] = solid
    x_ref[37] = solid
    o_ref[37] = solid
    for ref, first in ((x_ref, 1 - odd), (o_ref, odd)):
        for j in range(10):
            ref[27 + j] = root_ref[first * 6 + j]
    for copy in large:
        copy.wait()


def start0(e, loads, scale, b_ref, beta_ref, va_ref):
    total = loads[0] + loads[1] + loads[2]
    third = total * (1.0 / 3.0)
    for c, p in enumerate((loads[0] - third, loads[1] - third, total)):
        b_ref[c, e] = p
        beta = p * scale
        beta_ref[c, e] = beta
        va_ref[c, e] = beta * INV_MID


def stencil0(ref, c, e):
    mid = ref[c, e]
    s = ref[c, e - 1] + mid + ref[c, e + 1]
    return mid, 27.5 * mid - lane_sum(row_sum(s), 1, 128)


def first0(e, sol, beta_ref, va_ref, d_ref, vb_ref):
    for c in range(3):
        v, t = stencil0(va_ref, c, e)
        d = A1 * v + C1 * (beta_ref[c, e] - (sol * (kappa[c] / 26.5)) * t)
        d_ref[c, e] = d
        vb_ref[c, e] = v + d


def second0(e, sol, beta_ref, vb_ref, d_ref, v0_ref):
    for c in range(3):
        v, t = stencil0(vb_ref, c, e)
        pre = beta_ref[c, e] - (sol * (kappa[c] / 26.5)) * t
        v0_ref[c, e] = v + A2 * d_ref[c, e] + C2 * pre


def residual0(k, sols, root_ref, b_ref, v0_ref, t_ref):
    for c in range(3):
        total = None
        for j in range(2):
            e = 4 + 2 * k + j
            _, t = stencil0(v0_ref, c, e)
            r = b_ref[c, e] - (sols[j] * root_ref[e]) * (kappa[c] / 27.0) * t
            total = r if total is None else total + r
        t_ref[c, k] = total


def side0(before, message, own_solid, b_ref, beta_ref, root0_ref, va_ref, d_ref, vb_ref, v0_ref, t_ref):
    side_solid = message[37]

    def at(after_e, before_e):
        return after_e + before * (before_e - after_e)

    first = at(26, 0)
    for j in range(HALO):
        root0_ref[first + j] = safe(message[27 + j])
    first = at(26, 1)
    for j in range(9):
        scale = side_solid / (center * root0_ref[first + j])
        start0(first + j, [message[9 * c + j] for c in range(3)], scale, b_ref, beta_ref, va_ref)
    sign = at(1, -1)
    for j in range(9):
        first0(at(25, 10) + sign * j, own_solid if j < 1 else side_solid, beta_ref, va_ref, d_ref, vb_ref)
    for j in range(9):
        second0(at(24, 11) + sign * j, own_solid if j < 2 else side_solid, beta_ref, vb_ref, d_ref, v0_ref)
    for j in range(5):
        sol = own_solid if j < 2 else side_solid
        residual0(at(9, 4) + sign * j, (sol, sol), root0_ref, b_ref, v0_ref, t_ref)


def inner_kernel(load_ref, own_ref, x_ref, b_ref, beta_ref, root0_ref, va_ref, d_ref, vb_ref, v0_ref, t_ref):
    odd = lax.axis_index("bricks") & 1
    solid = own_ref[16]

    def start(z, _):
        root = own_ref[z]
        root0_ref[z + HALO] = root
        scale = solid / (center * root)
        start0(z + HALO, [load_ref[c, z] for c in range(3)], scale, b_ref, beta_ref, va_ref)
        return 0

    lax.fori_loop(0, 16, start, 0, unroll=8)

    def app1(e, _):
        first0(e, solid, beta_ref, va_ref, d_ref, vb_ref)
        return 0

    lax.fori_loop(HALO + 1, HALO + 15, app1, 0, unroll=7)

    def app2(e, _):
        second0(e, solid, beta_ref, vb_ref, d_ref, v0_ref)
        return 0

    lax.fori_loop(HALO + 2, HALO + 14, app2, 0, unroll=6)

    def resid(k, _):
        residual0(k, (solid, solid), root0_ref, b_ref, v0_ref, t_ref)
        return 0

    lax.fori_loop(5, 9, resid, 0, unroll=4)
    side0(odd, x_ref, solid, b_ref, beta_ref, root0_ref, va_ref, d_ref, vb_ref, v0_ref, t_ref)


def down_kernel(
    own_ref, x_solid_ref, o_ref, b_in, beta_in, root_in, va_in, d_in, vb_in, v0_in, t_in,
    b_ref, beta0_ref, root0_ref, va_ref, d_ref, vb_ref, v0_ref, t_s,
    msg_ref, edge_ref, v1_ref, beta1_ref, root1_ref, sol_ref,
    tr_s,
):
    odd = lax.axis_index("bricks") & 1
    is_odd = odd == 1
    own_solid = own_ref[16]
    x_solid, o_solid = x_solid_ref[37], o_ref[37]
    left_solid = jnp.where(is_odd, x_solid, o_solid)
    right_solid = jnp.where(is_odd, o_solid, x_solid)
    sol_ref[...] = jnp.zeros((8, 128), F32)
    sol_ref[0:1, :] = left_solid[:1]
    sol_ref[1:2, :] = own_solid[:1]
    sol_ref[2:3, :] = right_solid[:1]
    side0(1 - odd, o_ref, own_solid, b_ref, beta0_ref, root0_ref, va_ref, d_ref, vb_ref, v0_ref, t_s)

    def root_pair(k, _):
        tr_s[k] = root0_ref[2 * k] + root0_ref[2 * k + 1]
        return 0

    lax.fori_loop(0, 18, root_pair, 0, unroll=18)

    root1 = lane_pair(tr_s[:, pl.ds(0, 8, 2), :] + tr_s[:, pl.ds(1, 8, 2), :], 1) * 0.125
    root1_ref[...] = root1
    rt = root1[2:16]
    sol = jnp.concatenate(
        [
            jnp.broadcast_to(left_solid[None, :8], (3, 8, 128)),
            jnp.broadcast_to(own_solid[None, :8], (8, 8, 128)),
            jnp.broadcast_to(right_solid[None, :8], (3, 8, 128)),
        ],
        axis=0,
    )
    scale1 = sol / (0.25 * center * rt)
    zero = jnp.zeros((1, 8, 128), F32)

    def stencil1(v):
        before = jnp.concatenate([zero, v[:-1]], axis=0)
        after = jnp.concatenate([v[1:], zero], axis=0)
        return 27.5 * v - lane_sum(row_sum(before + v + after), 2, 128)

    gather = 4 * (iota((8, 128), 1) & 31)
    group = (iota((8, 128), 1) >> 5) == (iota((8, 128), 0) >> 1)

    def compact(q):
        q = q + pltpu.roll(q, 126, 1)
        q = jnp.take_along_axis(q, gather, axis=1)
        return jnp.sum(jnp.where(group, q, 0.0), axis=0, keepdims=True) * 0.125

    odd_lane = (iota((8, 128), 1) & 1) == 1
    to_after, to_before = [], []

    def pair(a, b):
        return jnp.where(odd_lane, b, a)

    def send_edge(k, after, before):
        msg_ref[24 + 8 * k : 32 + 8 * k, :] = jnp.where(is_odd, before, after)
        edge_ref[8 * k : 8 * k + 8, :] = jnp.where(is_odd, after, before)

    b1 = [
        lane_pair(t_s[c, :, pl.ds(0, 8, 2), :] + t_s[c, :, pl.ds(1, 8, 2), :], 1) * 0.125 for c in range(3)
    ]
    m = [sol * (kappa[c] / 26.5) for c in (0, 2)]
    m = [m[0], m[0], m[1]]
    beta = [b1[c] * scale1 for c in range(3)]
    v = [beta[c] * INV_MID for c in range(3)]
    d = list(v)
    for a, b in ((A1, C1), (A2, C2)):
        t = [stencil1(v[c]) for c in range(3)]
        for c in range(3):
            d[c] = a * d[c] + b * (beta[c] - m[c] * t[c])
            v[c] = v[c] + d[c]
    t = [stencil1(v[c])[3:11] for c in range(3)]
    g = (sol * rt)[3:11]
    for c in range(3):
        v1_ref[c] = v[c]
        beta1_ref[c] = beta[c]
        r = b1[c][3:11] - g * (0.25 * kappa[c] / 27.0) * t[c]
        for z in range(4):
            msg_ref[4 * c + z : 4 * c + z + 1, :] = compact(r[2 * z] + r[2 * z + 1])
        for j in range(2):
            send_edge(2 * c + j, pair(v[c][6 + 2 * j], v[c][7 + 2 * j]), pair(v[c][4 + 2 * j], v[c][5 + 2 * j]))
        to_after.append(beta[c][7])
        to_before.append(beta[c][6])
    send_edge(6, pair(*to_after[:2]), pair(*to_before[:2]))
    send_edge(7, to_after[2], to_before[2])
    for z in range(4):
        msg_ref[12 + z : 13 + z, :] = compact(root1[5 + 2 * z] + root1[6 + 2 * z])
    msg_ref[16:24, :] = jnp.take_along_axis(own_solid[:8], gather, axis=1)


def up_kernel(
    row_ref, far_ref, far2_ref, msg_in_ref,
    v0_ref, beta0_ref, root0_ref, v1_ref, beta1_ref, root1_ref, sol_ref,
    out_hbm,
    all_s, solid_s, w_s, coef_s, f_s, e2_s, pe_s, a_s, bb_s, d_s, out_ref, sems,
):
    me = lax.axis_index("bricks")
    odd = me & 1
    is_odd = odd == 1

    for t in range(16):
        rows = slice(16 * t, 16 * t + 16)
        far, far2 = far_ref[rows, :], far2_ref[rows, :]
        all_s[t] = jnp.where(is_odd, far2, far)
        all_s[16 + t] = row_ref[rows, :]
        all_s[32 + t] = jnp.where(is_odd, far, far2)
    far, far2 = far_ref[256:272, :], far2_ref[256:272, :]
    solid_s[0:16, :] = jnp.where(is_odd, far2, far)
    solid_s[16:32, :] = row_ref[256:272, :]
    solid_s[32:48, :] = jnp.where(is_odd, far, far2)
    chip0 = (me >> 1) - 8
    here = (me >> 1) & 7
    low_rows = iota((8, 128), 0) < 4
    for w in range(17):
        chip = chip0 + w
        rel = (chip >> 3) - (me >> 4)
        holder = jnp.where(rel == 0, odd, jnp.where(rel < 0, 0, 1))
        beside = (chip ^ here) & 1
        x0, x1 = (((chip + sign * beside) ^ here) & 7 for sign in (1, -1))
        six0, six1 = x0 >> 2, x1 >> 2
        two0, two1 = ((x0 >> 1) & 1) ^ six0, ((x1 >> 1) & 1) ^ six1
        slot = (rel + 1) * 16 + beside
        block0 = slot + 2 * two0 + 4 * six0 + 8 * holder
        block1 = slot + 2 * six1 + 4 * two1 + 8 * (1 - holder)
        straight = beside == 0
        blocks = (jnp.where(straight, block0, block1), jnp.where(straight, block1, block0))
        for half in range(2):
            first, second = (all_s[block, 8 * half : 8 * half + 8, :] for block in blocks)
            w_s[2 * half, 8 * w : 8 * w + 8, :] = jnp.where(low_rows, first, pltpu.roll(second, 4, 0))
            w_s[2 * half + 1, 8 * w : 8 * w + 8, :] = jnp.where(low_rows, pltpu.roll(first, 4, 0), second)
        solid = (jnp.broadcast_to(solid_s[pl.ds(block, 1), :], (8, 128)) for block in blocks)
        w_s[4, 8 * w : 8 * w + 8, :] = jnp.where(low_rows, *solid)

    lane = iota((1, 1, 128), 2)

    def lane_mask(cond):
        return jnp.where(cond, 1.0, 0.0).astype(F32)

    masks_x = (lane_mask(lane >= 32), lane_mask(lane < 96))
    masks_y = {
        level: (lane_mask((lane & 31) >= step), lane_mask((lane & 31) < 32 - step))
        for level, step in ((2, 1), (3, 2), (4, 4), (5, 8))
    }
    scale27 = jnp.concatenate([jnp.full((1, 1, 128), k, F32) for k in kappa], axis=0)
    by26 = scale27 * (1.0 / 26.5)

    def stencil(v, level):
        n = v.shape[1]
        s = v + pltpu.roll(v, 1, 1) + pltpu.roll(v, n - 1, 1)
        step = 2 ** (level - 2)
        low, high = masks_y[level]
        if level > 2:
            beside = low * (pltpu.roll(s, step, 2) + pltpu.roll(s, 64 + step, 2))
            beside = beside + high * (pltpu.roll(s, 128 - step, 2) + pltpu.roll(s, 64 - step, 2))
            return (27.5 * v - (s + pltpu.roll(s, 64, 2))) - beside
        lower, upper = masks_x
        s = s + lower * pltpu.roll(s, 32, 2) + upper * pltpu.roll(s, 96, 2)
        return 27.5 * v - (s + low * pltpu.roll(s, 1, 2) + high * pltpu.roll(s, 127, 2))

    def first(beta, m, level):
        v = beta * INV_MID
        d = A1 * v + C1 * (beta - m * stencil(v, level))
        v = v + d
        d = A2 * d + C2 * (beta - m * stencil(v, level))
        return v + d

    def again(v, beta, m, level):
        d = INV_MID * (beta - m * stencil(v, level))
        v = v + d
        d = A1 * d + C1 * (beta - m * stencil(v, level))
        v = v + d
        d = A2 * d + C2 * (beta - m * stencil(v, level))
        return v + d

    def coarsen(values, level, room):
        k, n = values.shape[:2]
        half = (n // 2 + 7) // 8 * 8
        if 2 * half > n:
            room[0:k, n : 2 * half, :] = jnp.zeros((k, 2 * half - n, 128), F32)
        room[0:k, 0:n, :] = values
        s = room[0:k, pl.ds(0, half, 2), :] + room[0:k, pl.ds(1, half, 2), :]
        s = lane_pair(s, 2 ** (level - 2))
        if level == 2:
            return lane_pair(s, 32) * 0.125
        return s * 0.25

    def refine(values, first_row, count):
        n = values.shape[1]
        f_s[0:3, pl.ds(0, n, 2), :] = values
        f_s[0:3, pl.ds(1, n, 2), :] = values
        return f_s[0:3, first_row : first_row + count, :]

    both = w_s[3:5]
    roots, sols = {2: safe(both[0:1])}, {2: both[1:2]}
    for level in (2, 3, 4):
        both = coarsen(jnp.concatenate([roots[level], sols[level]], axis=0), level, coef_s)
        roots[level + 1], sols[level + 1] = safe(both[0:1]), both[1:2]
    sol5 = sols[5]
    sol5_safe = jnp.where(sol5 > 0.0, sol5, 1.0)
    inverse = {level: 1.0 / roots[level] for level in (2, 3, 4, 5)}
    powers = {level: (sols[level], sols[level]) for level in (2, 3, 4)}
    powers[5] = (sol5 * sol5, sol5 * sol5 * sol5)
    g5 = jnp.where(sol5 > 0.0, inverse[5] / sol5_safe, 0.0)
    scales = {level: powers[level][0] * inverse[level] * (1.0 / (0.25**level * center)) for level in (2, 3, 4, 5)}
    masks = {level: powers[level][1] * by26 for level in (2, 3, 4, 5)}
    windows = {4: (0, 40), 3: (24, 48), 2: (56, 80)}

    b = w_s[0:3]
    betas, vs = {}, {}
    for level in (2, 3, 4):
        beta = b * scales[level]
        v = first(beta, masks[level], level)
        r = b - (sols[level] * roots[level]) * (scale27 * (0.25**level / 27.0)) * stencil(v, level)
        betas[level], vs[level] = beta, v
        b = coarsen(r, level, f_s)
    e = first(b * scales[5], masks[5], 5) * g5
    first_row = 0
    for level in (4, 3, 2):
        lo, hi = windows[level]
        e = refine(e, lo - first_row, hi - lo)
        root, sol = roots[level][:, lo:hi], sols[level][:, lo:hi]
        v = vs[level][:, lo:hi] + (root * sol) * e
        v = again(v, betas[level][:, lo:hi], masks[level][:, lo:hi], level)
        e = jnp.where(sol > 0.0, v * inverse[level][:, lo:hi], e)
        first_row = 2 * lo
    e2_s[...] = e

    rows = {}
    for k, name in enumerate(("left", "own", "right")):
        rows[name] = sol_ref[k : k + 1, :]

    def layers(name, n):
        return jnp.broadcast_to(rows[name][None], (n, 8, 128))

    sol = jnp.concatenate([layers("left", 5), layers("own", 8), layers("right", 5)], axis=0)
    root1 = root1_ref[...]
    spread = (iota((8, 128), 0) >> 1) * 32 + (iota((8, 128), 1) >> 2)
    zero = jnp.zeros((1, 8, 128), F32)

    def stencil1(v):
        before = jnp.concatenate([zero, v[:-1]], axis=0)
        after = jnp.concatenate([v[1:], zero], axis=0)
        return 27.5 * v - lane_sum(row_sum(before + v + after), 2, 128)

    odd_lane = (iota((8, 128), 1) & 1) == 1
    across = jnp.where(is_odd, here == 7, here == 0)

    def edge_slabs(k, left):
        mine = msg_in_ref[136 + 8 * k : 144 + 8 * k, :]
        other = jnp.where(across, far_ref[272 + 8 * k : 280 + 8 * k, :], row_ref[272 + 8 * k : 280 + 8 * k, :])
        p = jnp.where(is_odd == left, mine, other)
        first = jnp.where(odd_lane, pltpu.roll(p, 1, 1), p)
        second = jnp.where(odd_lane, p, pltpu.roll(p, 127, 1))
        return [first[None], second[None]]

    edges = {}
    for left in (True, False):
        slabs = [edge_slabs(k, left) for k in range(8)]
        edges[left] = [slabs[2 * c] + slabs[2 * c + 1] for c in range(3)], [slabs[6][0], slabs[6][1], slabs[7][0]]

    layers_v, layers_b, layers_e = [], [], []
    for c in range(3):
        layers_v.append(jnp.concatenate(edges[True][0][c] + [v1_ref[c][2:12]] + edges[False][0][c], axis=0))
        layers_b.append(jnp.concatenate([zero, edges[True][1][c], beta1_ref[c], edges[False][1][c], zero], axis=0))
        slabs = []
        for j in range(10):
            row = e2_s[c, pl.ds(5 + 4 * odd + j, 1), :]
            slab = jnp.take_along_axis(jnp.broadcast_to(row, (8, 128)), spread, axis=1)[None]
            slabs += [slab, slab]
        layers_e.append(jnp.concatenate(slabs[1:19], axis=0))
    m = [sol * (kappa[c] / 26.5) for c in (0, 2)]
    m = [m[0], m[0], m[1]]
    g = root1 * sol
    v = [layers_v[c] + g * layers_e[c] for c in range(3)]
    d = [None] * 3
    for a, b in ((None, INV_MID), (A1, C1), (A2, C2)):
        t = [stencil1(v[c]) for c in range(3)]
        for c in range(3):
            pre = b * (layers_b[c] - m[c] * t[c])
            d[c] = pre if a is None else a * d[c] + pre
            v[c] = v[c] + d[c]
    inverse1 = 1.0 / root1
    for c in range(3):
        e = jnp.where(sol > 0.0, v[c] * inverse1, layers_e[c])[3:15]
        pe_s[c, :, pl.ds(0, 8, 2), :] = e
        pe_s[c, :, pl.ds(1, 8, 2), :] = e

    shift = HALO - 4

    broad = {name: jnp.broadcast_to(row, (16, 128)) for name, row in rows.items()}

    def sol0(k):
        return broad["left"] if k < 4 else broad["own"] if k < 20 else broad["right"]

    for k in range(1, 23):
        g = root0_ref[k + shift] * sol0(k)
        for c in range(3):
            a_s[c, k] = v0_ref[c, k + shift] + g * pe_s[c, k >> 1]


    for k in range(2, 22):
        sol = sol0(k)
        for c in range(3):
            v, t = stencil0(a_s, c, k)
            d = INV_MID * (beta0_ref[c, k + shift] - (sol * (kappa[c] / 26.5)) * t)
            d_s[c, k] = d
            bb_s[c, k] = v + d


    for k in range(3, 21):
        sol = sol0(k)
        for c in range(3):
            v, t = stencil0(bb_s, c, k)
            pre = beta0_ref[c, k + shift] - (sol * (kappa[c] / 26.5)) * t
            d = A1 * d_s[c, k] + C1 * pre
            d_s[c, k] = d
            a_s[c, k] = v + d

    own_solid = jnp.broadcast_to(rows["own"], (16, 128))

    copies = []
    for k in range(4, 20):
        inverse = 1.0 / root0_ref[k + shift]
        x = []
        for c in range(3):
            v, t = stencil0(a_s, c, k)
            pre = beta0_ref[c, k + shift] - (own_solid * (kappa[c] / 26.5)) * t
            v = v + A2 * d_s[c, k] + C2 * pre
            x.append(jnp.where(own_solid > 0.0, v * inverse, pe_s[c, k >> 1]))
        third = x[2] * (1.0 / 3.0)
        out_ref[0, k - 4] = x[0] + third
        out_ref[1, k - 4] = x[1] + third
        out_ref[2, k - 4] = third - x[0] - x[1]
        if k % 4 == 3:
            part = pl.ds(k - 7, 4)
            copy = pltpu.make_async_copy(out_ref.at[:, part], out_hbm.at[:, part], sems.at[k // 4 - 1])
            copy.start()
            copies.append(copy)
    for copy in copies:
        copy.wait()


VMEM = pl.BlockSpec(memory_space=pltpu.VMEM)
HBM = pl.BlockSpec(memory_space=pltpu.HBM)
PARAMS = pltpu.CompilerParams(vmem_limit_bytes=40 * 2**20)


def shaped(*shape):
    return jax.ShapeDtypeStruct(shape, F32)


def swap_bits(values, bits):
    n = lax.axis_size("bricks")
    return lax.ppermute(values, "bricks", [(i, i ^ bits) for i in range(n)])


def swap_chips(values, bits):
    n = lax.axis_size("bricks")
    return lax.ppermute(values, "bricks", [(i, i ^ bits[i % 2]) for i in range(n)])


def swap_before(values):
    n = lax.axis_size("bricks")
    return lax.ppermute(values, "bricks", [(i, i + 1 if i % 2 else i - 1) for i in range(1, n - 1)])


def swap_ring(values):
    n = lax.axis_size("bricks")
    pairs = []
    for i in range(0, n, 2):
        j = i // 16 * 16 + (i - 1) % 16
        pairs += [(i, j), (j, i)]
    return lax.ppermute(values, "bricks", sorted(pairs))


def next_rows(values):
    n = lax.axis_size("bricks")
    pairs = [(i, i + 16 if i % 2 == 0 else i - 16) for i in range(n)]
    return lax.ppermute(values, "bricks", [(i, j) for i, j in pairs if 0 <= j < n])


def body(load_field, material_class, occupancy, moduli):
    x_msg, o_msg, root = pl.pallas_call(
        pack_kernel,
        out_shape=(shaped(38, 16, 128), shaped(38, 16, 128), shaped(17, 16, 128)),
        in_specs=[HBM, HBM, HBM, HBM],
        out_specs=(VMEM,) * 3,
        scratch_shapes=[
            pltpu.VMEM((16, 16, 128), jnp.int32),
            pltpu.SMEM((1, 1, 8), jnp.int32),
            pltpu.SMEM((8,), F32),
            pltpu.SemaphoreType.DMA((9,)),
        ],
        compiler_params=pltpu.CompilerParams(vmem_limit_bytes=56 * 2**20),
        name="pack",
    )(load_field, material_class, occupancy, moduli)
    x_in = swap_bits(x_msg, 1)
    o_in = swap_before(o_msg)
    ext = shaped(3, EXT, 16, 128)
    fine = (ext, ext, shaped(EXT, 16, 128), ext, ext, ext, ext, shaped(3, 14, 16, 128))
    inner = pl.pallas_call(
        inner_kernel,
        out_shape=fine,
        in_specs=[VMEM] * 3,
        out_specs=(VMEM,) * 8,
        compiler_params=PARAMS,
        cost_estimate=pl.CostEstimate(flops=10_000_000, bytes_accessed=4_000_000, transcendentals=0),
        name="inner",
    )(load_field, root, x_in)
    _, beta0, root0, _, _, _, v0, _, msg, edge, v1, beta1, root1, solid_rows = pl.pallas_call(
        down_kernel,
        out_shape=fine
        + (
            shaped(88, 128), shaped(64, 128),
            shaped(3, 14, 8, 128), shaped(3, 14, 8, 128), shaped(18, 8, 128), shaped(8, 128),
        ),
        in_specs=[VMEM] * 11,
        out_specs=(VMEM,) * 14,
        input_output_aliases={3 + k: k for k in range(8)},
        scratch_shapes=[
            pltpu.VMEM((18, 16, 128), F32),
        ],
        compiler_params=PARAMS,
        name="down",
    )(root, x_in, o_in, *inner)
    row_of = iota((8, 128), 0)

    def joined(a, b, bit):
        return jnp.where((row_of & bit) == 0, a, b)

    blocks, solids = msg[:16], msg[16:24]
    got = swap_ring(jnp.concatenate([blocks, solids, edge], axis=0))
    blocks = jnp.concatenate([blocks, got[:16]], axis=0)
    solids = joined(solids, got[16:24], 1)
    edge_in = got[24:]
    got = swap_chips(jnp.concatenate([blocks, solids], axis=0), (4, 12))
    blocks = jnp.concatenate([blocks, got[:32]], axis=0)
    solids = joined(solids, got[32:], 2)
    got = swap_chips(jnp.concatenate([blocks, solids], axis=0), (12, 4))
    blocks = jnp.concatenate([blocks, got[:64]], axis=0)
    solids = joined(solids, got[64:], 4)
    msg_in = swap_bits(jnp.concatenate([blocks, solids, msg[24:]], axis=0), 1)
    row = jnp.concatenate([blocks, msg_in[:128], solids, msg_in[128:136], edge_in], axis=0)
    far = next_rows(row)
    far2 = swap_bits(far, 1)
    return pl.pallas_call(
        up_kernel,
        out_shape=shaped(3, 16, 16, 128),
        in_specs=[VMEM] * 11,
        out_specs=HBM,
        scratch_shapes=[
            pltpu.VMEM((48, 16, 128), F32),
            pltpu.VMEM((48, 128), F32),
            pltpu.VMEM((5, 136, 128), F32),
            pltpu.VMEM((2, 144, 128), F32),
            pltpu.VMEM((3, 144, 128), F32),
            pltpu.VMEM((3, 24, 128), F32),
            pltpu.VMEM((3, 12, 16, 128), F32),
            pltpu.VMEM((3, 24, 16, 128), F32),
            pltpu.VMEM((3, 24, 16, 128), F32),
            pltpu.VMEM((3, 24, 16, 128), F32),
            pltpu.VMEM((3, 16, 16, 128), F32),
            pltpu.SemaphoreType.DMA((4,)),
        ],
        compiler_params=PARAMS,
        name="up",
    )(row, far, far2, msg_in, v0, beta0, root0, v1, beta1, root1, solid_rows)


def solution(mesh):
    in_specs = (
        P(None, "bricks", None, None),
        P("bricks", None, None),
        P("bricks", None, None),
        P(),
    )
    out_specs = P(None, "bricks", None, None)
    return jax.shard_map(body, mesh=mesh, in_specs=in_specs, out_specs=out_specs, check_vma=False)
```

```python
import jax
import jax.numpy as jnp
from jax import lax
from jax.experimental import pallas as pl
from jax.experimental.pallas import tpu as pltpu
from jax.sharding import PartitionSpec as P

F32 = jnp.float32
center = 26.5 / 27.0
cheb_mid = 1.65
cheb_half = 1.35
sigma = cheb_mid / cheb_half
kappa = (0.75, 0.75, 1.5)
HALO = 10
EXT = 16 + 2 * HALO


def cheb_pairs():
    rho, out = 1.0 / sigma, []
    for _ in range(2):
        new = 1.0 / (2.0 * sigma - rho)
        out.append((new * rho, 2.0 * new / cheb_half))
        rho = new
    return out


(A1, C1), (A2, C2) = cheb_pairs()
INV_MID = 1.0 / cheb_mid


def iota(shape, axis):
    return lax.broadcasted_iota(jnp.int32, shape, axis)


def lane_sum(s, step, period):
    axis = s.ndim - 1
    lane = iota((1,) * axis + (128,), axis) & (period - 1)
    low = jnp.where(lane >= step, 1.0, 0.0).astype(F32)
    high = jnp.where(lane < period - step, 1.0, 0.0).astype(F32)
    return s + low * pltpu.roll(s, step, axis) + high * pltpu.roll(s, 128 - step, axis)


def row_sum(s):
    axis = s.ndim - 2
    n = s.shape[axis]
    row = iota(s.shape, axis)
    before = jnp.where(row >= 1, pltpu.roll(s, 1, axis), 0.0)
    after = jnp.where(row < n - 1, pltpu.roll(s, n - 1, axis), 0.0)
    return s + before + after


def lane_pair(s, step):
    axis = s.ndim - 1
    upper = (iota(s.shape, axis) & step) != 0
    return s + jnp.where(upper, pltpu.roll(s, step, axis), pltpu.roll(s, 128 - step, axis))


def safe(root):
    return jnp.where(root > 0.0, root, 1.0)


def pack_kernel(load_ref, class_ref, occ_ref, moduli_ref, x_ref, o_ref, root_ref, class_s, occ_s, moduli_s, sems):
    odd = lax.axis_index("bricks") & 1
    small = [
        pltpu.make_async_copy(class_ref, class_s, sems.at[0]),
        pltpu.make_async_copy(occ_ref, occ_s, sems.at[1]),
        pltpu.make_async_copy(moduli_ref, moduli_s, sems.at[2]),
    ]
    for copy in small:
        copy.start()
    large = []
    for k, (ref, first) in enumerate(((x_ref, 1 - odd), (o_ref, odd))):
        for c in range(3):
            copy = pltpu.make_async_copy(
                load_ref.at[c, pl.ds(first * 7, 9)], ref.at[pl.ds(9 * c, 9)], sems.at[3 + 3 * k + c]
            )
            copy.start()
            large.append(copy)
    for copy in small:
        copy.wait()

    def fill(z, _):
        cls = class_s[z]
        modulus = jnp.zeros(cls.shape, F32)
        for k in range(8):
            modulus = jnp.where(cls == k, moduli_s[k], modulus)
        root_ref[z] = jnp.sqrt(modulus)
        return 0

    lax.fori_loop(0, 16, fill, 0, unroll=8)
    lane = iota((16, 128), 1) >> 4
    solid = jnp.zeros((16, 128), F32)
    for k in range(8):
        solid = jnp.where(lane == k, occ_s[0, 0, k].astype(F32), solid)
    root_ref[16] = solid
    x_ref[37] = solid
    o_ref[37] = solid
    for ref, first in ((x_ref, 1 - odd), (o_ref, odd)):
        for j in range(10):
            ref[27 + j] = root_ref[first * 6 + j]
    for copy in large:
        copy.wait()


def start0(e, loads, scale, b_ref, beta_ref, va_ref):
    total = loads[0] + loads[1] + loads[2]
    third = total * (1.0 / 3.0)
    for c, p in enumerate((loads[0] - third, loads[1] - third, total)):
        b_ref[c, e] = p
        beta = p * scale
        beta_ref[c, e] = beta
        va_ref[c, e] = beta * INV_MID


def stencil0(ref, c, e):
    mid = ref[c, e]
    s = ref[c, e - 1] + mid + ref[c, e + 1]
    return mid, 27.5 * mid - lane_sum(row_sum(s), 1, 128)


def first0(e, sol, beta_ref, va_ref, d_ref, vb_ref):
    for c in range(3):
        v, t = stencil0(va_ref, c, e)
        d = A1 * v + C1 * (beta_ref[c, e] - (sol * (kappa[c] / 26.5)) * t)
        d_ref[c, e] = d
        vb_ref[c, e] = v + d


def second0(e, sol, beta_ref, vb_ref, d_ref, v0_ref):
    for c in range(3):
        v, t = stencil0(vb_ref, c, e)
        pre = beta_ref[c, e] - (sol * (kappa[c] / 26.5)) * t
        v0_ref[c, e] = v + A2 * d_ref[c, e] + C2 * pre


def residual0(k, sols, root_ref, b_ref, v0_ref, t_ref):
    for c in range(3):
        total = None
        for j in range(2):
            e = 4 + 2 * k + j
            _, t = stencil0(v0_ref, c, e)
            r = b_ref[c, e] - (sols[j] * root_ref[e]) * (kappa[c] / 27.0) * t
            total = r if total is None else total + r
        t_ref[c, k] = total


def side0(before, message, own_solid, b_ref, beta_ref, root0_ref, va_ref, d_ref, vb_ref, v0_ref, t_ref):
    side_solid = message[37]

    def at(after_e, before_e):
        return after_e + before * (before_e - after_e)

    first = at(26, 0)
    for j in range(HALO):
        root0_ref[first + j] = safe(message[27 + j])
    first = at(26, 1)
    for j in range(9):
        scale = side_solid / (center * root0_ref[first + j])
        start0(first + j, [message[9 * c + j] for c in range(3)], scale, b_ref, beta_ref, va_ref)
    sign = at(1, -1)
    for j in range(9):
        first0(at(25, 10) + sign * j, own_solid if j < 1 else side_solid, beta_ref, va_ref, d_ref, vb_ref)
    for j in range(9):
        second0(at(24, 11) + sign * j, own_solid if j < 2 else side_solid, beta_ref, vb_ref, d_ref, v0_ref)
    for j in range(5):
        sol = own_solid if j < 2 else side_solid
        residual0(at(9, 4) + sign * j, (sol, sol), root0_ref, b_ref, v0_ref, t_ref)


def inner_kernel(load_ref, own_ref, x_ref, b_ref, beta_ref, root0_ref, va_ref, d_ref, vb_ref, v0_ref, t_ref):
    odd = lax.axis_index("bricks") & 1
    solid = own_ref[16]

    def start(z, _):
        root = own_ref[z]
        root0_ref[z + HALO] = root
        scale = solid / (center * root)
        start0(z + HALO, [load_ref[c, z] for c in range(3)], scale, b_ref, beta_ref, va_ref)
        return 0

    lax.fori_loop(0, 16, start, 0, unroll=8)

    def app1(e, _):
        first0(e, solid, beta_ref, va_ref, d_ref, vb_ref)
        return 0

    lax.fori_loop(HALO + 1, HALO + 15, app1, 0, unroll=7)

    def app2(e, _):
        second0(e, solid, beta_ref, vb_ref, d_ref, v0_ref)
        return 0

    lax.fori_loop(HALO + 2, HALO + 14, app2, 0, unroll=6)

    def resid(k, _):
        residual0(k, (solid, solid), root0_ref, b_ref, v0_ref, t_ref)
        return 0

    lax.fori_loop(5, 9, resid, 0, unroll=4)
    side0(odd, x_ref, solid, b_ref, beta_ref, root0_ref, va_ref, d_ref, vb_ref, v0_ref, t_ref)


def down_kernel(
    own_ref, x_solid_ref, o_ref, b_in, beta_in, root_in, va_in, d_in, vb_in, v0_in, t_in,
    b_ref, beta0_ref, root0_ref, va_ref, d_ref, vb_ref, v0_ref, t_s,
    msg_ref, edge_ref, v1_ref, beta1_ref, root1_ref, sol_ref,
    tr_s,
):
    odd = lax.axis_index("bricks") & 1
    is_odd = odd == 1
    own_solid = own_ref[16]
    x_solid, o_solid = x_solid_ref[37], o_ref[37]
    left_solid = jnp.where(is_odd, x_solid, o_solid)
    right_solid = jnp.where(is_odd, o_solid, x_solid)
    sol_ref[...] = jnp.zeros((8, 128), F32)
    sol_ref[0:1, :] = left_solid[:1]
    sol_ref[1:2, :] = own_solid[:1]
    sol_ref[2:3, :] = right_solid[:1]
    side0(1 - odd, o_ref, own_solid, b_ref, beta0_ref, root0_ref, va_ref, d_ref, vb_ref, v0_ref, t_s)

    def root_pair(k, _):
        tr_s[k] = root0_ref[2 * k] + root0_ref[2 * k + 1]
        return 0

    lax.fori_loop(0, 18, root_pair, 0, unroll=18)

    root1 = lane_pair(tr_s[:, pl.ds(0, 8, 2), :] + tr_s[:, pl.ds(1, 8, 2), :], 1) * 0.125
    root1_ref[...] = root1
    rt = root1[2:16]
    sol = jnp.concatenate(
        [
            jnp.broadcast_to(left_solid[None, :8], (3, 8, 128)),
            jnp.broadcast_to(own_solid[None, :8], (8, 8, 128)),
            jnp.broadcast_to(right_solid[None, :8], (3, 8, 128)),
        ],
        axis=0,
    )
    scale1 = sol / (0.25 * center * rt)
    zero = jnp.zeros((1, 8, 128), F32)

    def stencil1(v):
        before = jnp.concatenate([zero, v[:-1]], axis=0)
        after = jnp.concatenate([v[1:], zero], axis=0)
        return 27.5 * v - lane_sum(row_sum(before + v + after), 2, 128)

    gather = 4 * (iota((8, 128), 1) & 31)
    group = (iota((8, 128), 1) >> 5) == (iota((8, 128), 0) >> 1)

    def compact(q):
        q = q + pltpu.roll(q, 126, 1)
        q = jnp.take_along_axis(q, gather, axis=1)
        return jnp.sum(jnp.where(group, q, 0.0), axis=0, keepdims=True) * 0.125

    odd_lane = (iota((8, 128), 1) & 1) == 1
    to_after, to_before = [], []

    def pair(a, b):
        return jnp.where(odd_lane, b, a)

    def send_edge(k, after, before):
        msg_ref[24 + 8 * k : 32 + 8 * k, :] = jnp.where(is_odd, before, after)
        edge_ref[8 * k : 8 * k + 8, :] = jnp.where(is_odd, after, before)

    b1 = [
        lane_pair(t_s[c, :, pl.ds(0, 8, 2), :] + t_s[c, :, pl.ds(1, 8, 2), :], 1) * 0.125 for c in range(3)
    ]
    m = [sol * (kappa[c] / 26.5) for c in (0, 2)]
    m = [m[0], m[0], m[1]]
    beta = [b1[c] * scale1 for c in range(3)]
    v = [beta[c] * INV_MID for c in range(3)]
    d = list(v)
    for a, b in ((A1, C1), (A2, C2)):
        t = [stencil1(v[c]) for c in range(3)]
        for c in range(3):
            d[c] = a * d[c] + b * (beta[c] - m[c] * t[c])
            v[c] = v[c] + d[c]
    t = [stencil1(v[c])[3:11] for c in range(3)]
    g = (sol * rt)[3:11]
    for c in range(3):
        v1_ref[c] = v[c]
        beta1_ref[c] = beta[c]
        r = b1[c][3:11] - g * (0.25 * kappa[c] / 27.0) * t[c]
        for z in range(4):
            msg_ref[4 * c + z : 4 * c + z + 1, :] = compact(r[2 * z] + r[2 * z + 1])
        for j in range(2):
            send_edge(2 * c + j, pair(v[c][6 + 2 * j], v[c][7 + 2 * j]), pair(v[c][4 + 2 * j], v[c][5 + 2 * j]))
        to_after.append(beta[c][7])
        to_before.append(beta[c][6])
    send_edge(6, pair(*to_after[:2]), pair(*to_before[:2]))
    send_edge(7, to_after[2], to_before[2])
    for z in range(4):
        msg_ref[12 + z : 13 + z, :] = compact(root1[5 + 2 * z] + root1[6 + 2 * z])
    msg_ref[16:24, :] = jnp.take_along_axis(own_solid[:8], gather, axis=1)


def up_kernel(
    row_ref, far_ref, far2_ref, msg_in_ref,
    v0_ref, beta0_ref, root0_ref, v1_ref, beta1_ref, root1_ref, sol_ref,
    out_hbm,
    all_s, solid_s, w_s, coef_s, f_s, e2_s, pe_s, a_s, bb_s, d_s, out_ref, sems,
):
    me = lax.axis_index("bricks")
    odd = me & 1
    is_odd = odd == 1

    for t in range(16):
        rows = slice(16 * t, 16 * t + 16)
        far, far2 = far_ref[rows, :], far2_ref[rows, :]
        all_s[t] = jnp.where(is_odd, far2, far)
        all_s[16 + t] = row_ref[rows, :]
        all_s[32 + t] = jnp.where(is_odd, far, far2)
    far, far2 = far_ref[256:272, :], far2_ref[256:272, :]
    solid_s[0:16, :] = jnp.where(is_odd, far2, far)
    solid_s[16:32, :] = row_ref[256:272, :]
    solid_s[32:48, :] = jnp.where(is_odd, far, far2)
    chip0 = (me >> 1) - 8
    here = (me >> 1) & 7
    low_rows = iota((8, 128), 0) < 4
    for w in range(17):
        chip = chip0 + w
        rel = (chip >> 3) - (me >> 4)
        holder = jnp.where(rel == 0, odd, jnp.where(rel < 0, 0, 1))
        beside = (chip ^ here) & 1
        x0, x1 = ((chip ^ (here - sign * beside)) & 7 for sign in (1, -1))
        six0, six1 = x0 >> 2, x1 >> 2
        two0, two1 = ((x0 >> 1) & 1) ^ six0, ((x1 >> 1) & 1) ^ six1
        slot = (rel + 1) * 16 + 4 * beside
        block0 = slot + two0 + 2 * six0 + 8 * holder
        block1 = slot + two1 + 2 * six1 + 8 * (1 - holder)
        straight = beside == 0
        blocks = (jnp.where(straight, block0, block1), jnp.where(straight, block1, block0))
        for half in range(2):
            first, second = (all_s[block, 8 * half : 8 * half + 8, :] for block in blocks)
            w_s[2 * half, 8 * w : 8 * w + 8, :] = jnp.where(low_rows, first, pltpu.roll(second, 4, 0))
            w_s[2 * half + 1, 8 * w : 8 * w + 8, :] = jnp.where(low_rows, pltpu.roll(first, 4, 0), second)
        solid = (jnp.broadcast_to(solid_s[pl.ds(block, 1), :], (8, 128)) for block in blocks)
        w_s[4, 8 * w : 8 * w + 8, :] = jnp.where(low_rows, *solid)

    lane = iota((1, 1, 128), 2)

    def lane_mask(cond):
        return jnp.where(cond, 1.0, 0.0).astype(F32)

    masks_x = (lane_mask(lane >= 32), lane_mask(lane < 96))
    masks_y = {
        level: (lane_mask((lane & 31) >= step), lane_mask((lane & 31) < 32 - step))
        for level, step in ((2, 1), (3, 2), (4, 4), (5, 8))
    }
    scale27 = jnp.concatenate([jnp.full((1, 1, 128), k, F32) for k in kappa], axis=0)
    by26 = scale27 * (1.0 / 26.5)

    def stencil(v, level):
        n = v.shape[1]
        s = v + pltpu.roll(v, 1, 1) + pltpu.roll(v, n - 1, 1)
        step = 2 ** (level - 2)
        low, high = masks_y[level]
        if level > 2:
            beside = low * (pltpu.roll(s, step, 2) + pltpu.roll(s, 64 + step, 2))
            beside = beside + high * (pltpu.roll(s, 128 - step, 2) + pltpu.roll(s, 64 - step, 2))
            return (27.5 * v - (s + pltpu.roll(s, 64, 2))) - beside
        lower, upper = masks_x
        s = s + lower * pltpu.roll(s, 32, 2) + upper * pltpu.roll(s, 96, 2)
        return 27.5 * v - (s + low * pltpu.roll(s, 1, 2) + high * pltpu.roll(s, 127, 2))

    def first(beta, m, level):
        v = beta * INV_MID
        d = A1 * v + C1 * (beta - m * stencil(v, level))
        v = v + d
        d = A2 * d + C2 * (beta - m * stencil(v, level))
        return v + d

    def again(v, beta, m, level):
        d = INV_MID * (beta - m * stencil(v, level))
        v = v + d
        d = A1 * d + C1 * (beta - m * stencil(v, level))
        v = v + d
        d = A2 * d + C2 * (beta - m * stencil(v, level))
        return v + d

    def coarsen(values, level, room):
        k, n = values.shape[:2]
        half = (n // 2 + 7) // 8 * 8
        if 2 * half > n:
            room[0:k, n : 2 * half, :] = jnp.zeros((k, 2 * half - n, 128), F32)
        room[0:k, 0:n, :] = values
        s = room[0:k, pl.ds(0, half, 2), :] + room[0:k, pl.ds(1, half, 2), :]
        s = lane_pair(s, 2 ** (level - 2))
        if level == 2:
            return lane_pair(s, 32) * 0.125
        return s * 0.25

    def refine(values, first_row, count):
        n = values.shape[1]
        f_s[0:3, pl.ds(0, n, 2), :] = values
        f_s[0:3, pl.ds(1, n, 2), :] = values
        return f_s[0:3, first_row : first_row + count, :]

    both = w_s[3:5]
    roots, sols = {2: safe(both[0:1])}, {2: both[1:2]}
    for level in (2, 3, 4):
        both = coarsen(jnp.concatenate([roots[level], sols[level]], axis=0), level, coef_s)
        roots[level + 1], sols[level + 1] = safe(both[0:1]), both[1:2]
    sol5 = sols[5]
    sol5_safe = jnp.where(sol5 > 0.0, sol5, 1.0)
    inverse = {level: 1.0 / roots[level] for level in (2, 3, 4, 5)}
    powers = {level: (sols[level], sols[level]) for level in (2, 3, 4)}
    powers[5] = (sol5 * sol5, sol5 * sol5 * sol5)
    g5 = jnp.where(sol5 > 0.0, inverse[5] / sol5_safe, 0.0)
    scales = {level: powers[level][0] * inverse[level] * (1.0 / (0.25**level * center)) for level in (2, 3, 4, 5)}
    masks = {level: powers[level][1] * by26 for level in (2, 3, 4, 5)}
    windows = {4: (0, 40), 3: (24, 48), 2: (56, 80)}

    b = w_s[0:3]
    betas, vs = {}, {}
    for level in (2, 3, 4):
        beta = b * scales[level]
        v = first(beta, masks[level], level)
        r = b - (sols[level] * roots[level]) * (scale27 * (0.25**level / 27.0)) * stencil(v, level)
        betas[level], vs[level] = beta, v
        b = coarsen(r, level, f_s)
    e = first(b * scales[5], masks[5], 5) * g5
    first_row = 0
    for level in (4, 3, 2):
        lo, hi = windows[level]
        e = refine(e, lo - first_row, hi - lo)
        root, sol = roots[level][:, lo:hi], sols[level][:, lo:hi]
        v = vs[level][:, lo:hi] + (root * sol) * e
        v = again(v, betas[level][:, lo:hi], masks[level][:, lo:hi], level)
        e = jnp.where(sol > 0.0, v * inverse[level][:, lo:hi], e)
        first_row = 2 * lo
    e2_s[...] = e

    rows = {}
    for k, name in enumerate(("left", "own", "right")):
        rows[name] = sol_ref[k : k + 1, :]

    def layers(name, n):
        return jnp.broadcast_to(rows[name][None], (n, 8, 128))

    sol = jnp.concatenate([layers("left", 5), layers("own", 8), layers("right", 5)], axis=0)
    root1 = root1_ref[...]
    spread = (iota((8, 128), 0) >> 1) * 32 + (iota((8, 128), 1) >> 2)
    zero = jnp.zeros((1, 8, 128), F32)

    def stencil1(v):
        before = jnp.concatenate([zero, v[:-1]], axis=0)
        after = jnp.concatenate([v[1:], zero], axis=0)
        return 27.5 * v - lane_sum(row_sum(before + v + after), 2, 128)

    odd_lane = (iota((8, 128), 1) & 1) == 1
    across = jnp.where(is_odd, here == 7, here == 0)

    def edge_slabs(k, left):
        mine = msg_in_ref[136 + 8 * k : 144 + 8 * k, :]
        other = jnp.where(across, far_ref[272 + 8 * k : 280 + 8 * k, :], row_ref[272 + 8 * k : 280 + 8 * k, :])
        p = jnp.where(is_odd == left, mine, other)
        first = jnp.where(odd_lane, pltpu.roll(p, 1, 1), p)
        second = jnp.where(odd_lane, p, pltpu.roll(p, 127, 1))
        return [first[None], second[None]]

    edges = {}
    for left in (True, False):
        slabs = [edge_slabs(k, left) for k in range(8)]
        edges[left] = [slabs[2 * c] + slabs[2 * c + 1] for c in range(3)], [slabs[6][0], slabs[6][1], slabs[7][0]]

    layers_v, layers_b, layers_e = [], [], []
    for c in range(3):
        layers_v.append(jnp.concatenate(edges[True][0][c] + [v1_ref[c][2:12]] + edges[False][0][c], axis=0))
        layers_b.append(jnp.concatenate([zero, edges[True][1][c], beta1_ref[c], edges[False][1][c], zero], axis=0))
        slabs = []
        for j in range(10):
            row = e2_s[c, pl.ds(5 + 4 * odd + j, 1), :]
            slab = jnp.take_along_axis(jnp.broadcast_to(row, (8, 128)), spread, axis=1)[None]
            slabs += [slab, slab]
        layers_e.append(jnp.concatenate(slabs[1:19], axis=0))
    m = [sol * (kappa[c] / 26.5) for c in (0, 2)]
    m = [m[0], m[0], m[1]]
    g = root1 * sol
    v = [layers_v[c] + g * layers_e[c] for c in range(3)]
    d = [None] * 3
    for a, b in ((None, INV_MID), (A1, C1), (A2, C2)):
        t = [stencil1(v[c]) for c in range(3)]
        for c in range(3):
            pre = b * (layers_b[c] - m[c] * t[c])
            d[c] = pre if a is None else a * d[c] + pre
            v[c] = v[c] + d[c]
    inverse1 = 1.0 / root1
    for c in range(3):
        e = jnp.where(sol > 0.0, v[c] * inverse1, layers_e[c])[3:15]
        pe_s[c, :, pl.ds(0, 8, 2), :] = e
        pe_s[c, :, pl.ds(1, 8, 2), :] = e

    shift = HALO - 4

    broad = {name: jnp.broadcast_to(row, (16, 128)) for name, row in rows.items()}

    def sol0(k):
        return broad["left"] if k < 4 else broad["own"] if k < 20 else broad["right"]

    for k in range(1, 23):
        g = root0_ref[k + shift] * sol0(k)
        for c in range(3):
            a_s[c, k] = v0_ref[c, k + shift] + g * pe_s[c, k >> 1]


    for k in range(2, 22):
        sol = sol0(k)
        for c in range(3):
            v, t = stencil0(a_s, c, k)
            d = INV_MID * (beta0_ref[c, k + shift] - (sol * (kappa[c] / 26.5)) * t)
            d_s[c, k] = d
            bb_s[c, k] = v + d


    for k in range(3, 21):
        sol = sol0(k)
        for c in range(3):
            v, t = stencil0(bb_s, c, k)
            pre = beta0_ref[c, k + shift] - (sol * (kappa[c] / 26.5)) * t
            d = A1 * d_s[c, k] + C1 * pre
            d_s[c, k] = d
            a_s[c, k] = v + d

    own_solid = jnp.broadcast_to(rows["own"], (16, 128))

    copies = []
    for k in range(4, 20):
        inverse = 1.0 / root0_ref[k + shift]
        x = []
        for c in range(3):
            v, t = stencil0(a_s, c, k)
            pre = beta0_ref[c, k + shift] - (own_solid * (kappa[c] / 26.5)) * t
            v = v + A2 * d_s[c, k] + C2 * pre
            x.append(jnp.where(own_solid > 0.0, v * inverse, pe_s[c, k >> 1]))
        third = x[2] * (1.0 / 3.0)
        out_ref[0, k - 4] = x[0] + third
        out_ref[1, k - 4] = x[1] + third
        out_ref[2, k - 4] = third - x[0] - x[1]
        if k % 4 == 3:
            part = pl.ds(k - 7, 4)
            copy = pltpu.make_async_copy(out_ref.at[:, part], out_hbm.at[:, part], sems.at[k // 4 - 1])
            copy.start()
            copies.append(copy)
    for copy in copies:
        copy.wait()


VMEM = pl.BlockSpec(memory_space=pltpu.VMEM)
HBM = pl.BlockSpec(memory_space=pltpu.HBM)
PARAMS = pltpu.CompilerParams(vmem_limit_bytes=40 * 2**20)


def shaped(*shape):
    return jax.ShapeDtypeStruct(shape, F32)


def swap_bits(values, bits):
    n = lax.axis_size("bricks")
    return lax.ppermute(values, "bricks", [(i, i ^ bits) for i in range(n)])


def swap_before(values):
    n = lax.axis_size("bricks")
    return lax.ppermute(values, "bricks", [(i, i + 1 if i % 2 else i - 1) for i in range(1, n - 1)])


def swap_ring(values):
    n = lax.axis_size("bricks")
    pairs = []
    for i in range(0, n, 2):
        j = i // 16 * 16 + (i - 1) % 16
        pairs += [(i, j), (j, i)]
    return lax.ppermute(values, "bricks", sorted(pairs))


def next_rows(values):
    n = lax.axis_size("bricks")
    pairs = [(i, i + 16 if i % 2 == 0 else i - 16) for i in range(n)]
    return lax.ppermute(values, "bricks", [(i, j) for i, j in pairs if 0 <= j < n])


def body(load_field, material_class, occupancy, moduli):
    x_msg, o_msg, root = pl.pallas_call(
        pack_kernel,
        out_shape=(shaped(38, 16, 128), shaped(38, 16, 128), shaped(17, 16, 128)),
        in_specs=[HBM, HBM, HBM, HBM],
        out_specs=(VMEM,) * 3,
        scratch_shapes=[
            pltpu.VMEM((16, 16, 128), jnp.int32),
            pltpu.SMEM((1, 1, 8), jnp.int32),
            pltpu.SMEM((8,), F32),
            pltpu.SemaphoreType.DMA((9,)),
        ],
        compiler_params=pltpu.CompilerParams(vmem_limit_bytes=56 * 2**20),
        name="pack",
    )(load_field, material_class, occupancy, moduli)
    x_in = swap_bits(x_msg, 1)
    o_in = swap_before(o_msg)
    ext = shaped(3, EXT, 16, 128)
    fine = (ext, ext, shaped(EXT, 16, 128), ext, ext, ext, ext, shaped(3, 14, 16, 128))
    inner = pl.pallas_call(
        inner_kernel,
        out_shape=fine,
        in_specs=[VMEM] * 3,
        out_specs=(VMEM,) * 8,
        compiler_params=PARAMS,
        cost_estimate=pl.CostEstimate(flops=10_000_000, bytes_accessed=4_000_000, transcendentals=0),
        name="inner",
    )(load_field, root, x_in)
    _, beta0, root0, _, _, _, v0, _, msg, edge, v1, beta1, root1, solid_rows = pl.pallas_call(
        down_kernel,
        out_shape=fine
        + (
            shaped(88, 128), shaped(64, 128),
            shaped(3, 14, 8, 128), shaped(3, 14, 8, 128), shaped(18, 8, 128), shaped(8, 128),
        ),
        in_specs=[VMEM] * 11,
        out_specs=(VMEM,) * 14,
        input_output_aliases={3 + k: k for k in range(8)},
        scratch_shapes=[
            pltpu.VMEM((18, 16, 128), F32),
        ],
        compiler_params=PARAMS,
        name="down",
    )(root, x_in, o_in, *inner)
    row_of = iota((8, 128), 0)

    def joined(a, b, bit):
        return jnp.where((row_of & bit) == 0, a, b)

    mine = msg[:24]
    parts = [mine] + [swap_bits(mine, bits) for bits in (4, 12, 8)]
    blocks = jnp.concatenate([part[:16] for part in parts], axis=0)
    solids = parts[0][16:]
    for k in (1, 2, 3):
        solids = jnp.where((row_of & 3) == k, parts[k][16:], solids)
    got = swap_ring(jnp.concatenate([blocks, solids, edge], axis=0))
    blocks = jnp.concatenate([blocks, got[:64]], axis=0)
    solids = joined(solids, got[64:72], 4)
    edge_in = got[72:]
    msg_in = swap_bits(jnp.concatenate([blocks, solids, msg[24:]], axis=0), 1)
    row = jnp.concatenate([blocks, msg_in[:128], solids, msg_in[128:136], edge_in], axis=0)
    far = next_rows(row)
    far2 = swap_bits(far, 1)
    return pl.pallas_call(
        up_kernel,
        out_shape=shaped(3, 16, 16, 128),
        in_specs=[VMEM] * 11,
        out_specs=HBM,
        scratch_shapes=[
            pltpu.VMEM((48, 16, 128), F32),
            pltpu.VMEM((48, 128), F32),
            pltpu.VMEM((5, 136, 128), F32),
            pltpu.VMEM((2, 144, 128), F32),
            pltpu.VMEM((3, 144, 128), F32),
            pltpu.VMEM((3, 24, 128), F32),
            pltpu.VMEM((3, 12, 16, 128), F32),
            pltpu.VMEM((3, 24, 16, 128), F32),
            pltpu.VMEM((3, 24, 16, 128), F32),
            pltpu.VMEM((3, 24, 16, 128), F32),
            pltpu.VMEM((3, 16, 16, 128), F32),
            pltpu.SemaphoreType.DMA((4,)),
        ],
        compiler_params=PARAMS,
        name="up",
    )(row, far, far2, msg_in, v0, beta0, root0, v1, beta1, root1, solid_rows)


def solution(mesh):
    in_specs = (
        P(None, "bricks", None, None),
        P("bricks", None, None),
        P("bricks", None, None),
        P(),
    )
    out_specs = P(None, "bricks", None, None)
    return jax.shard_map(body, mesh=mesh, in_specs=in_specs, out_specs=out_specs, check_vma=False)
```

```python
import jax
import jax.numpy as jnp
from jax import lax
from jax.experimental import pallas as pl
from jax.experimental.pallas import tpu as pltpu
from jax.sharding import PartitionSpec as P

F32 = jnp.float32
center = 26.5 / 27.0
cheb_mid = 1.65
cheb_half = 1.35
sigma = cheb_mid / cheb_half
kappa = (0.75, 0.75, 1.5)
HALO = 10
RING_ORDER = (12, 8, 4)
FIRST_TWO, FIRST_SIX = 1 + RING_ORDER.index(4), 1 + RING_ORDER.index(12)
EXT = 16 + 2 * HALO


def cheb_pairs():
    rho, out = 1.0 / sigma, []
    for _ in range(2):
        new = 1.0 / (2.0 * sigma - rho)
        out.append((new * rho, 2.0 * new / cheb_half))
        rho = new
    return out


(A1, C1), (A2, C2) = cheb_pairs()
INV_MID = 1.0 / cheb_mid


def iota(shape, axis):
    return lax.broadcasted_iota(jnp.int32, shape, axis)


def lane_sum(s, step, period):
    axis = s.ndim - 1
    lane = iota((1,) * axis + (128,), axis) & (period - 1)
    low = jnp.where(lane >= step, 1.0, 0.0).astype(F32)
    high = jnp.where(lane < period - step, 1.0, 0.0).astype(F32)
    return s + low * pltpu.roll(s, step, axis) + high * pltpu.roll(s, 128 - step, axis)


def row_sum(s):
    axis = s.ndim - 2
    n = s.shape[axis]
    row = iota(s.shape, axis)
    before = jnp.where(row >= 1, pltpu.roll(s, 1, axis), 0.0)
    after = jnp.where(row < n - 1, pltpu.roll(s, n - 1, axis), 0.0)
    return s + before + after


def lane_pair(s, step):
    axis = s.ndim - 1
    upper = (iota(s.shape, axis) & step) != 0
    return s + jnp.where(upper, pltpu.roll(s, step, axis), pltpu.roll(s, 128 - step, axis))


def safe(root):
    return jnp.where(root > 0.0, root, 1.0)


def pack_kernel(load_ref, class_ref, occ_ref, moduli_ref, x_ref, o_ref, root_ref, class_s, occ_s, moduli_s, sems):
    odd = lax.axis_index("bricks") & 1
    small = [
        pltpu.make_async_copy(class_ref, class_s, sems.at[0]),
        pltpu.make_async_copy(occ_ref, occ_s, sems.at[1]),
        pltpu.make_async_copy(moduli_ref, moduli_s, sems.at[2]),
    ]
    for copy in small:
        copy.start()
    large = []
    for k, (ref, first) in enumerate(((x_ref, 1 - odd), (o_ref, odd))):
        for c in range(3):
            copy = pltpu.make_async_copy(
                load_ref.at[c, pl.ds(first * 7, 9)], ref.at[pl.ds(9 * c, 9)], sems.at[3 + 3 * k + c]
            )
            copy.start()
            large.append(copy)
    for copy in small:
        copy.wait()

    def fill(z, _):
        cls = class_s[z]
        modulus = jnp.zeros(cls.shape, F32)
        for k in range(8):
            modulus = jnp.where(cls == k, moduli_s[k], modulus)
        root_ref[z] = jnp.sqrt(modulus)
        return 0

    lax.fori_loop(0, 16, fill, 0, unroll=8)
    lane = iota((16, 128), 1) >> 4
    solid = jnp.zeros((16, 128), F32)
    for k in range(8):
        solid = jnp.where(lane == k, occ_s[0, 0, k].astype(F32), solid)
    root_ref[16] = solid
    x_ref[37] = solid
    o_ref[37] = solid
    for ref, first in ((x_ref, 1 - odd), (o_ref, odd)):
        for j in range(10):
            ref[27 + j] = root_ref[first * 6 + j]
    for copy in large:
        copy.wait()


def start0(e, loads, scale, b_ref, beta_ref, va_ref):
    total = loads[0] + loads[1] + loads[2]
    third = total * (1.0 / 3.0)
    for c, p in enumerate((loads[0] - third, loads[1] - third, total)):
        b_ref[c, e] = p
        beta = p * scale
        beta_ref[c, e] = beta
        va_ref[c, e] = beta * INV_MID


def stencil0(ref, c, e):
    mid = ref[c, e]
    s = ref[c, e - 1] + mid + ref[c, e + 1]
    return mid, 27.5 * mid - lane_sum(row_sum(s), 1, 128)


def first0(e, sol, beta_ref, va_ref, d_ref, vb_ref):
    for c in range(3):
        v, t = stencil0(va_ref, c, e)
        d = A1 * v + C1 * (beta_ref[c, e] - (sol * (kappa[c] / 26.5)) * t)
        d_ref[c, e] = d
        vb_ref[c, e] = v + d


def second0(e, sol, beta_ref, vb_ref, d_ref, v0_ref):
    for c in range(3):
        v, t = stencil0(vb_ref, c, e)
        pre = beta_ref[c, e] - (sol * (kappa[c] / 26.5)) * t
        v0_ref[c, e] = v + A2 * d_ref[c, e] + C2 * pre


def residual0(k, sols, root_ref, b_ref, v0_ref, t_ref):
    for c in range(3):
        total = None
        for j in range(2):
            e = 4 + 2 * k + j
            _, t = stencil0(v0_ref, c, e)
            r = b_ref[c, e] - (sols[j] * root_ref[e]) * (kappa[c] / 27.0) * t
            total = r if total is None else total + r
        t_ref[c, k] = total


def side0(before, message, own_solid, b_ref, beta_ref, root0_ref, va_ref, d_ref, vb_ref, v0_ref, t_ref):
    side_solid = message[37]

    def at(after_e, before_e):
        return after_e + before * (before_e - after_e)

    first = at(26, 0)
    for j in range(HALO):
        root0_ref[first + j] = safe(message[27 + j])
    first = at(26, 1)
    for j in range(9):
        scale = side_solid / (center * root0_ref[first + j])
        start0(first + j, [message[9 * c + j] for c in range(3)], scale, b_ref, beta_ref, va_ref)
    sign = at(1, -1)
    for j in range(9):
        first0(at(25, 10) + sign * j, own_solid if j < 1 else side_solid, beta_ref, va_ref, d_ref, vb_ref)
    for j in range(9):
        second0(at(24, 11) + sign * j, own_solid if j < 2 else side_solid, beta_ref, vb_ref, d_ref, v0_ref)
    for j in range(5):
        sol = own_solid if j < 2 else side_solid
        residual0(at(9, 4) + sign * j, (sol, sol), root0_ref, b_ref, v0_ref, t_ref)


def inner_kernel(load_ref, own_ref, x_ref, b_ref, beta_ref, root0_ref, va_ref, d_ref, vb_ref, v0_ref, t_ref):
    odd = lax.axis_index("bricks") & 1
    solid = own_ref[16]

    def start(z, _):
        root = own_ref[z]
        root0_ref[z + HALO] = root
        scale = solid / (center * root)
        start0(z + HALO, [load_ref[c, z] for c in range(3)], scale, b_ref, beta_ref, va_ref)
        return 0

    lax.fori_loop(0, 16, start, 0, unroll=8)

    def app1(e, _):
        first0(e, solid, beta_ref, va_ref, d_ref, vb_ref)
        return 0

    lax.fori_loop(HALO + 1, HALO + 15, app1, 0, unroll=7)

    def app2(e, _):
        second0(e, solid, beta_ref, vb_ref, d_ref, v0_ref)
        return 0

    lax.fori_loop(HALO + 2, HALO + 14, app2, 0, unroll=6)

    def resid(k, _):
        residual0(k, (solid, solid), root0_ref, b_ref, v0_ref, t_ref)
        return 0

    lax.fori_loop(5, 9, resid, 0, unroll=4)
    side0(odd, x_ref, solid, b_ref, beta_ref, root0_ref, va_ref, d_ref, vb_ref, v0_ref, t_ref)


def down_kernel(
    own_ref, x_solid_ref, o_ref, b_in, beta_in, root_in, va_in, d_in, vb_in, v0_in, t_in,
    b_ref, beta0_ref, root0_ref, va_ref, d_ref, vb_ref, v0_ref, t_s,
    msg_ref, edge_ref, v1_ref, beta1_ref, root1_ref, sol_ref,
    tr_s,
):
    odd = lax.axis_index("bricks") & 1
    is_odd = odd == 1
    own_solid = own_ref[16]
    x_solid, o_solid = x_solid_ref[37], o_ref[37]
    left_solid = jnp.where(is_odd, x_solid, o_solid)
    right_solid = jnp.where(is_odd, o_solid, x_solid)
    sol_ref[...] = jnp.zeros((8, 128), F32)
    sol_ref[0:1, :] = left_solid[:1]
    sol_ref[1:2, :] = own_solid[:1]
    sol_ref[2:3, :] = right_solid[:1]
    side0(1 - odd, o_ref, own_solid, b_ref, beta0_ref, root0_ref, va_ref, d_ref, vb_ref, v0_ref, t_s)

    def root_pair(k, _):
        tr_s[k] = root0_ref[2 * k] + root0_ref[2 * k + 1]
        return 0

    lax.fori_loop(0, 18, root_pair, 0, unroll=18)

    root1 = lane_pair(tr_s[:, pl.ds(0, 8, 2), :] + tr_s[:, pl.ds(1, 8, 2), :], 1) * 0.125
    root1_ref[...] = root1
    rt = root1[2:16]
    sol = jnp.concatenate(
        [
            jnp.broadcast_to(left_solid[None, :8], (3, 8, 128)),
            jnp.broadcast_to(own_solid[None, :8], (8, 8, 128)),
            jnp.broadcast_to(right_solid[None, :8], (3, 8, 128)),
        ],
        axis=0,
    )
    scale1 = sol / (0.25 * center * rt)
    zero = jnp.zeros((1, 8, 128), F32)

    def stencil1(v):
        before = jnp.concatenate([zero, v[:-1]], axis=0)
        after = jnp.concatenate([v[1:], zero], axis=0)
        return 27.5 * v - lane_sum(row_sum(before + v + after), 2, 128)

    gather = 4 * (iota((8, 128), 1) & 31)
    group = (iota((8, 128), 1) >> 5) == (iota((8, 128), 0) >> 1)

    def compact(q):
        q = q + pltpu.roll(q, 126, 1)
        q = jnp.take_along_axis(q, gather, axis=1)
        return jnp.sum(jnp.where(group, q, 0.0), axis=0, keepdims=True) * 0.125

    odd_lane = (iota((8, 128), 1) & 1) == 1
    to_after, to_before = [], []

    def pair(a, b):
        return jnp.where(odd_lane, b, a)

    def send_edge(k, after, before):
        msg_ref[24 + 8 * k : 32 + 8 * k, :] = jnp.where(is_odd, before, after)
        edge_ref[8 * k : 8 * k + 8, :] = jnp.where(is_odd, after, before)

    b1 = [
        lane_pair(t_s[c, :, pl.ds(0, 8, 2), :] + t_s[c, :, pl.ds(1, 8, 2), :], 1) * 0.125 for c in range(3)
    ]
    m = [sol * (kappa[c] / 26.5) for c in (0, 2)]
    m = [m[0], m[0], m[1]]
    beta = [b1[c] * scale1 for c in range(3)]
    v = [beta[c] * INV_MID for c in range(3)]
    d = list(v)
    for a, b in ((A1, C1), (A2, C2)):
        t = [stencil1(v[c]) for c in range(3)]
        for c in range(3):
            d[c] = a * d[c] + b * (beta[c] - m[c] * t[c])
            v[c] = v[c] + d[c]
    t = [stencil1(v[c])[3:11] for c in range(3)]
    g = (sol * rt)[3:11]
    for c in range(3):
        v1_ref[c] = v[c]
        beta1_ref[c] = beta[c]
        r = b1[c][3:11] - g * (0.25 * kappa[c] / 27.0) * t[c]
        for z in range(4):
            msg_ref[4 * c + z : 4 * c + z + 1, :] = compact(r[2 * z] + r[2 * z + 1])
        for j in range(2):
            send_edge(2 * c + j, pair(v[c][6 + 2 * j], v[c][7 + 2 * j]), pair(v[c][4 + 2 * j], v[c][5 + 2 * j]))
        to_after.append(beta[c][7])
        to_before.append(beta[c][6])
    send_edge(6, pair(*to_after[:2]), pair(*to_before[:2]))
    send_edge(7, to_after[2], to_before[2])
    for z in range(4):
        msg_ref[12 + z : 13 + z, :] = compact(root1[5 + 2 * z] + root1[6 + 2 * z])
    msg_ref[16:24, :] = jnp.take_along_axis(own_solid[:8], gather, axis=1)


def up_kernel(
    mine_ref, far_ref, near_ref, other_ref,
    v0_ref, beta0_ref, root0_ref, v1_ref, beta1_ref, root1_ref, sol_ref,
    out_hbm,
    all_s, solid_s, w_s, coef_s, f_s, e2_s, pe_s, a_s, bb_s, d_s, out_ref, sems,
):
    me = lax.axis_index("bricks")
    odd = me & 1
    is_odd = odd == 1

    for k, ref in enumerate((far_ref, mine_ref, near_ref)):
        start = (136, 0, 272)[k]
        for t in range(8):
            all_s[16 * k + t] = ref[16 * t : 16 * t + 16, :]
            all_s[16 * k + 8 + t] = other_ref[start + 16 * t : start + 16 * t + 16, :]
        solid_s[16 * k : 16 * k + 8, :] = ref[128:136, :]
        solid_s[16 * k + 8 : 16 * k + 16, :] = other_ref[start + 128 : start + 136, :]
    even_row = ((me >> 4) & 1) == 0
    chip0 = (me >> 1) - 8
    here = (me >> 1) & 7
    low_rows = iota((8, 128), 0) < 4
    for w in range(17):
        chip = chip0 + w
        rel = (chip >> 3) - (me >> 4)
        beside = (chip ^ here) & 1
        x0, x1 = ((chip ^ (here - sign * beside)) & 7 for sign in (1, -1))
        six0, six1 = x0 >> 2, x1 >> 2
        two0, two1 = ((x0 >> 1) & 1) ^ six0, ((x1 >> 1) & 1) ^ six1
        place = jnp.where(rel == 0, 1, jnp.where((rel < 0) == even_row, 0, 2))
        slot = 16 * place + 4 * beside
        block0 = slot + (FIRST_TWO * two0 ^ FIRST_SIX * six0) + 8 * odd
        block1 = slot + (FIRST_TWO * two1 ^ FIRST_SIX * six1) + 8 * (1 - odd)
        straight = beside == 0
        blocks = (jnp.where(straight, block0, block1), jnp.where(straight, block1, block0))
        for half in range(2):
            first, second = (all_s[block, 8 * half : 8 * half + 8, :] for block in blocks)
            w_s[2 * half, 8 * w : 8 * w + 8, :] = jnp.where(low_rows, first, pltpu.roll(second, 4, 0))
            w_s[2 * half + 1, 8 * w : 8 * w + 8, :] = jnp.where(low_rows, pltpu.roll(first, 4, 0), second)
        solid = (jnp.broadcast_to(solid_s[pl.ds(block, 1), :], (8, 128)) for block in blocks)
        w_s[4, 8 * w : 8 * w + 8, :] = jnp.where(low_rows, *solid)

    lane = iota((1, 1, 128), 2)

    def lane_mask(cond):
        return jnp.where(cond, 1.0, 0.0).astype(F32)

    masks_x = (lane_mask(lane >= 32), lane_mask(lane < 96))
    masks_y = {
        level: (lane_mask((lane & 31) >= step), lane_mask((lane & 31) < 32 - step))
        for level, step in ((2, 1), (3, 2), (4, 4), (5, 8))
    }
    scale27 = jnp.concatenate([jnp.full((1, 1, 128), k, F32) for k in kappa], axis=0)
    by26 = scale27 * (1.0 / 26.5)

    def stencil(v, level):
        n = v.shape[1]
        s = v + pltpu.roll(v, 1, 1) + pltpu.roll(v, n - 1, 1)
        step = 2 ** (level - 2)
        low, high = masks_y[level]
        if level > 2:
            beside = low * (pltpu.roll(s, step, 2) + pltpu.roll(s, 64 + step, 2))
            beside = beside + high * (pltpu.roll(s, 128 - step, 2) + pltpu.roll(s, 64 - step, 2))
            return (27.5 * v - (s + pltpu.roll(s, 64, 2))) - beside
        lower, upper = masks_x
        s = s + lower * pltpu.roll(s, 32, 2) + upper * pltpu.roll(s, 96, 2)
        return 27.5 * v - (s + low * pltpu.roll(s, 1, 2) + high * pltpu.roll(s, 127, 2))

    def first(beta, m, level):
        v = beta * INV_MID
        d = A1 * v + C1 * (beta - m * stencil(v, level))
        v = v + d
        d = A2 * d + C2 * (beta - m * stencil(v, level))
        return v + d

    def again(v, beta, m, level):
        d = INV_MID * (beta - m * stencil(v, level))
        v = v + d
        d = A1 * d + C1 * (beta - m * stencil(v, level))
        v = v + d
        d = A2 * d + C2 * (beta - m * stencil(v, level))
        return v + d

    def coarsen(values, level, room):
        k, n = values.shape[:2]
        half = (n // 2 + 7) // 8 * 8
        if 2 * half > n:
            room[0:k, n : 2 * half, :] = jnp.zeros((k, 2 * half - n, 128), F32)
        room[0:k, 0:n, :] = values
        s = room[0:k, pl.ds(0, half, 2), :] + room[0:k, pl.ds(1, half, 2), :]
        s = lane_pair(s, 2 ** (level - 2))
        if level == 2:
            return lane_pair(s, 32) * 0.125
        return s * 0.25

    def refine(values, first_row, count):
        n = values.shape[1]
        f_s[0:3, pl.ds(0, n, 2), :] = values
        f_s[0:3, pl.ds(1, n, 2), :] = values
        return f_s[0:3, first_row : first_row + count, :]

    both = w_s[3:5]
    roots, sols = {2: safe(both[0:1])}, {2: both[1:2]}
    for level in (2, 3, 4):
        both = coarsen(jnp.concatenate([roots[level], sols[level]], axis=0), level, coef_s)
        roots[level + 1], sols[level + 1] = safe(both[0:1]), both[1:2]
    sol5 = sols[5]
    sol5_safe = jnp.where(sol5 > 0.0, sol5, 1.0)
    inverse = {level: 1.0 / roots[level] for level in (2, 3, 4, 5)}
    powers = {level: (sols[level], sols[level]) for level in (2, 3, 4)}
    powers[5] = (sol5 * sol5, sol5 * sol5 * sol5)
    g5 = jnp.where(sol5 > 0.0, inverse[5] / sol5_safe, 0.0)
    scales = {level: powers[level][0] * inverse[level] * (1.0 / (0.25**level * center)) for level in (2, 3, 4, 5)}
    masks = {level: powers[level][1] * by26 for level in (2, 3, 4, 5)}
    windows = {4: (0, 40), 3: (24, 48), 2: (56, 80)}

    b = w_s[0:3]
    betas, vs = {}, {}
    for level in (2, 3, 4):
        beta = b * scales[level]
        v = first(beta, masks[level], level)
        r = b - (sols[level] * roots[level]) * (scale27 * (0.25**level / 27.0)) * stencil(v, level)
        betas[level], vs[level] = beta, v
        b = coarsen(r, level, f_s)
    e = first(b * scales[5], masks[5], 5) * g5
    first_row = 0
    for level in (4, 3, 2):
        lo, hi = windows[level]
        e = refine(e, lo - first_row, hi - lo)
        root, sol = roots[level][:, lo:hi], sols[level][:, lo:hi]
        v = vs[level][:, lo:hi] + (root * sol) * e
        v = again(v, betas[level][:, lo:hi], masks[level][:, lo:hi], level)
        e = jnp.where(sol > 0.0, v * inverse[level][:, lo:hi], e)
        first_row = 2 * lo
    e2_s[...] = e

    rows = {}
    for k, name in enumerate(("left", "own", "right")):
        rows[name] = sol_ref[k : k + 1, :]

    def layers(name, n):
        return jnp.broadcast_to(rows[name][None], (n, 8, 128))

    sol = jnp.concatenate([layers("left", 5), layers("own", 8), layers("right", 5)], axis=0)
    root1 = root1_ref[...]
    spread = (iota((8, 128), 0) >> 1) * 32 + (iota((8, 128), 1) >> 2)
    zero = jnp.zeros((1, 8, 128), F32)

    def stencil1(v):
        before = jnp.concatenate([zero, v[:-1]], axis=0)
        after = jnp.concatenate([v[1:], zero], axis=0)
        return 27.5 * v - lane_sum(row_sum(before + v + after), 2, 128)

    odd_lane = (iota((8, 128), 1) & 1) == 1
    across = jnp.where(is_odd, here == 7, here == 0)

    def edge_slabs(k, left):
        mine = other_ref[408 + 8 * k : 416 + 8 * k, :]
        rows = slice(136 + 8 * k, 144 + 8 * k)
        beyond = jnp.where(is_odd == even_row, near_ref[rows, :], far_ref[rows, :])
        other = jnp.where(across, beyond, mine_ref[rows, :])
        p = jnp.where(is_odd == left, mine, other)
        first = jnp.where(odd_lane, pltpu.roll(p, 1, 1), p)
        second = jnp.where(odd_lane, p, pltpu.roll(p, 127, 1))
        return [first[None], second[None]]

    edges = {}
    for left in (True, False):
        slabs = [edge_slabs(k, left) for k in range(8)]
        edges[left] = [slabs[2 * c] + slabs[2 * c + 1] for c in range(3)], [slabs[6][0], slabs[6][1], slabs[7][0]]

    layers_v, layers_b, layers_e = [], [], []
    for c in range(3):
        layers_v.append(jnp.concatenate(edges[True][0][c] + [v1_ref[c][2:12]] + edges[False][0][c], axis=0))
        layers_b.append(jnp.concatenate([zero, edges[True][1][c], beta1_ref[c], edges[False][1][c], zero], axis=0))
        slabs = []
        for j in range(10):
            row = e2_s[c, pl.ds(5 + 4 * odd + j, 1), :]
            slab = jnp.take_along_axis(jnp.broadcast_to(row, (8, 128)), spread, axis=1)[None]
            slabs += [slab, slab]
        layers_e.append(jnp.concatenate(slabs[1:19], axis=0))
    m = [sol * (kappa[c] / 26.5) for c in (0, 2)]
    m = [m[0], m[0], m[1]]
    g = root1 * sol
    v = [layers_v[c] + g * layers_e[c] for c in range(3)]
    d = [None] * 3
    for a, b in ((None, INV_MID), (A1, C1), (A2, C2)):
        t = [stencil1(v[c]) for c in range(3)]
        for c in range(3):
            pre = b * (layers_b[c] - m[c] * t[c])
            d[c] = pre if a is None else a * d[c] + pre
            v[c] = v[c] + d[c]
    inverse1 = 1.0 / root1
    for c in range(3):
        e = jnp.where(sol > 0.0, v[c] * inverse1, layers_e[c])[3:15]
        pe_s[c, :, pl.ds(0, 8, 2), :] = e
        pe_s[c, :, pl.ds(1, 8, 2), :] = e

    shift = HALO - 4

    broad = {name: jnp.broadcast_to(row, (16, 128)) for name, row in rows.items()}

    def sol0(k):
        return broad["left"] if k < 4 else broad["own"] if k < 20 else broad["right"]

    for k in range(1, 23):
        g = root0_ref[k + shift] * sol0(k)
        for c in range(3):
            a_s[c, k] = v0_ref[c, k + shift] + g * pe_s[c, k >> 1]


    for k in range(2, 22):
        sol = sol0(k)
        for c in range(3):
            v, t = stencil0(a_s, c, k)
            d = INV_MID * (beta0_ref[c, k + shift] - (sol * (kappa[c] / 26.5)) * t)
            d_s[c, k] = d
            bb_s[c, k] = v + d


    for k in range(3, 21):
        sol = sol0(k)
        for c in range(3):
            v, t = stencil0(bb_s, c, k)
            pre = beta0_ref[c, k + shift] - (sol * (kappa[c] / 26.5)) * t
            d = A1 * d_s[c, k] + C1 * pre
            d_s[c, k] = d
            a_s[c, k] = v + d

    own_solid = jnp.broadcast_to(rows["own"], (16, 128))

    copies = []
    for k in range(4, 20):
        inverse = 1.0 / root0_ref[k + shift]
        x = []
        for c in range(3):
            v, t = stencil0(a_s, c, k)
            pre = beta0_ref[c, k + shift] - (own_solid * (kappa[c] / 26.5)) * t
            v = v + A2 * d_s[c, k] + C2 * pre
            x.append(jnp.where(own_solid > 0.0, v * inverse, pe_s[c, k >> 1]))
        third = x[2] * (1.0 / 3.0)
        out_ref[0, k - 4] = x[0] + third
        out_ref[1, k - 4] = x[1] + third
        out_ref[2, k - 4] = third - x[0] - x[1]
        if k % 4 == 3:
            part = pl.ds(k - 7, 4)
            copy = pltpu.make_async_copy(out_ref.at[:, part], out_hbm.at[:, part], sems.at[k // 4 - 1])
            copy.start()
            copies.append(copy)
    for copy in copies:
        copy.wait()


VMEM = pl.BlockSpec(memory_space=pltpu.VMEM)
HBM = pl.BlockSpec(memory_space=pltpu.HBM)
PARAMS = pltpu.CompilerParams(vmem_limit_bytes=40 * 2**20)


def shaped(*shape):
    return jax.ShapeDtypeStruct(shape, F32)


def swap_bits(values, bits):
    n = lax.axis_size("bricks")
    return lax.ppermute(values, "bricks", [(i, i ^ bits) for i in range(n)])


def swap_before(values):
    n = lax.axis_size("bricks")
    return lax.ppermute(values, "bricks", [(i, i + 1 if i % 2 else i - 1) for i in range(1, n - 1)])


def swap_ring(values):
    n = lax.axis_size("bricks")
    pairs = []
    for i in range(0, n, 2):
        j = i // 16 * 16 + (i - 1) % 16
        pairs += [(i, j), (j, i)]
    return lax.ppermute(values, "bricks", sorted(pairs))


def swap_far_rows(values):
    n = lax.axis_size("bricks")
    return lax.ppermute(values, "bricks", [(i, i + 16 if i >> 4 & 1 else i - 16) for i in range(16, n - 16)])


def body(load_field, material_class, occupancy, moduli):
    x_msg, o_msg, root = pl.pallas_call(
        pack_kernel,
        out_shape=(shaped(38, 16, 128), shaped(38, 16, 128), shaped(17, 16, 128)),
        in_specs=[HBM, HBM, HBM, HBM],
        out_specs=(VMEM,) * 3,
        scratch_shapes=[
            pltpu.VMEM((16, 16, 128), jnp.int32),
            pltpu.SMEM((1, 1, 8), jnp.int32),
            pltpu.SMEM((8,), F32),
            pltpu.SemaphoreType.DMA((9,)),
        ],
        compiler_params=pltpu.CompilerParams(vmem_limit_bytes=56 * 2**20),
        name="pack",
    )(load_field, material_class, occupancy, moduli)
    x_in = swap_bits(x_msg, 1)
    o_in = swap_before(o_msg)
    ext = shaped(3, EXT, 16, 128)
    fine = (ext, ext, shaped(EXT, 16, 128), ext, ext, ext, ext, shaped(3, 14, 16, 128))
    inner = pl.pallas_call(
        inner_kernel,
        out_shape=fine,
        in_specs=[VMEM] * 3,
        out_specs=(VMEM,) * 8,
        compiler_params=PARAMS,
        cost_estimate=pl.CostEstimate(flops=10_000_000, bytes_accessed=4_000_000, transcendentals=0),
        name="inner",
    )(load_field, root, x_in)
    _, beta0, root0, _, _, _, v0, _, msg, edge, v1, beta1, root1, solid_rows = pl.pallas_call(
        down_kernel,
        out_shape=fine
        + (
            shaped(88, 128), shaped(64, 128),
            shaped(3, 14, 8, 128), shaped(3, 14, 8, 128), shaped(18, 8, 128), shaped(8, 128),
        ),
        in_specs=[VMEM] * 11,
        out_specs=(VMEM,) * 14,
        input_output_aliases={3 + k: k for k in range(8)},
        scratch_shapes=[
            pltpu.VMEM((18, 16, 128), F32),
        ],
        compiler_params=PARAMS,
        name="down",
    )(root, x_in, o_in, *inner)
    row_of = iota((8, 128), 0)

    def joined(a, b, bit):
        return jnp.where((row_of & bit) == 0, a, b)

    mine = msg[:24]
    parts = [mine] + [swap_bits(mine, bits) for bits in RING_ORDER]
    blocks = jnp.concatenate([part[:16] for part in parts], axis=0)
    solids = parts[0][16:]
    for k in (1, 2, 3):
        solids = jnp.where((row_of & 3) == k, parts[k][16:], solids)
    got = swap_ring(jnp.concatenate([blocks, solids, edge], axis=0))
    blocks = jnp.concatenate([blocks, got[:64]], axis=0)
    solids = joined(solids, got[64:72], 4)
    edge_in = got[72:]
    mine = jnp.concatenate([blocks, solids, edge_in], axis=0)
    far, near = swap_far_rows(mine), swap_bits(mine, 16)
    other = swap_bits(jnp.concatenate([mine[:136], far[:136], near[:136], msg[24:]], axis=0), 1)
    return pl.pallas_call(
        up_kernel,
        out_shape=shaped(3, 16, 16, 128),
        in_specs=[VMEM] * 11,
        out_specs=HBM,
        scratch_shapes=[
            pltpu.VMEM((48, 16, 128), F32),
            pltpu.VMEM((48, 128), F32),
            pltpu.VMEM((5, 136, 128), F32),
            pltpu.VMEM((2, 144, 128), F32),
            pltpu.VMEM((3, 144, 128), F32),
            pltpu.VMEM((3, 24, 128), F32),
            pltpu.VMEM((3, 12, 16, 128), F32),
            pltpu.VMEM((3, 24, 16, 128), F32),
            pltpu.VMEM((3, 24, 16, 128), F32),
            pltpu.VMEM((3, 24, 16, 128), F32),
            pltpu.VMEM((3, 16, 16, 128), F32),
            pltpu.SemaphoreType.DMA((4,)),
        ],
        compiler_params=PARAMS,
        name="up",
    )(mine, far, near, other, v0, beta0, root0, v1, beta1, root1, solid_rows)


def solution(mesh):
    in_specs = (
        P(None, "bricks", None, None),
        P("bricks", None, None),
        P("bricks", None, None),
        P(),
    )
    out_specs = P(None, "bricks", None, None)
    return jax.shard_map(body, mesh=mesh, in_specs=in_specs, out_specs=out_specs, check_vma=False)
```

```python
import jax
import jax.numpy as jnp
from jax import lax
from jax.experimental import pallas as pl
from jax.experimental.pallas import tpu as pltpu
from jax.sharding import PartitionSpec as P

F32 = jnp.float32
center = 26.5 / 27.0
cheb_mid = 1.65
cheb_half = 1.35
sigma = cheb_mid / cheb_half
kappa = (0.75, 0.75, 1.5)
HALO = 10
RING_ORDER = (12, 8, 4)
FIRST_TWO, FIRST_SIX = 1 + RING_ORDER.index(4), 1 + RING_ORDER.index(12)
EXT = 16 + 2 * HALO


def cheb_pairs():
    rho, out = 1.0 / sigma, []
    for _ in range(2):
        new = 1.0 / (2.0 * sigma - rho)
        out.append((new * rho, 2.0 * new / cheb_half))
        rho = new
    return out


(A1, C1), (A2, C2) = cheb_pairs()
INV_MID = 1.0 / cheb_mid


def iota(shape, axis):
    return lax.broadcasted_iota(jnp.int32, shape, axis)


def lane_sum(s, step, period):
    axis = s.ndim - 1
    lane = iota((1,) * axis + (128,), axis) & (period - 1)
    low = jnp.where(lane >= step, 1.0, 0.0).astype(F32)
    high = jnp.where(lane < period - step, 1.0, 0.0).astype(F32)
    return s + low * pltpu.roll(s, step, axis) + high * pltpu.roll(s, 128 - step, axis)


def row_sum(s):
    axis = s.ndim - 2
    n = s.shape[axis]
    row = iota(s.shape, axis)
    before = jnp.where(row >= 1, pltpu.roll(s, 1, axis), 0.0)
    after = jnp.where(row < n - 1, pltpu.roll(s, n - 1, axis), 0.0)
    return s + before + after


def lane_pair(s, step):
    axis = s.ndim - 1
    upper = (iota(s.shape, axis) & step) != 0
    return s + jnp.where(upper, pltpu.roll(s, step, axis), pltpu.roll(s, 128 - step, axis))


def safe(root):
    return jnp.where(root > 0.0, root, 1.0)


def pack_kernel(load_ref, class_ref, occ_ref, moduli_ref, x_ref, o_ref, root_ref, class_s, occ_s, moduli_s, sems):
    odd = lax.axis_index("bricks") & 1
    small = [
        pltpu.make_async_copy(class_ref, class_s, sems.at[0]),
        pltpu.make_async_copy(occ_ref, occ_s, sems.at[1]),
        pltpu.make_async_copy(moduli_ref, moduli_s, sems.at[2]),
    ]
    for copy in small:
        copy.start()
    large = []
    for k, (ref, first) in enumerate(((x_ref, 1 - odd), (o_ref, odd))):
        for c in range(3):
            copy = pltpu.make_async_copy(
                load_ref.at[c, pl.ds(first * 7, 9)], ref.at[pl.ds(9 * c, 9)], sems.at[3 + 3 * k + c]
            )
            copy.start()
            large.append(copy)
    for copy in small:
        copy.wait()

    def fill(z, _):
        cls = class_s[z]
        modulus = jnp.zeros(cls.shape, F32)
        for k in range(8):
            modulus = jnp.where(cls == k, moduli_s[k], modulus)
        root_ref[z] = jnp.sqrt(modulus)
        return 0

    lax.fori_loop(0, 16, fill, 0, unroll=8)
    lane = iota((16, 128), 1) >> 4
    solid = jnp.zeros((16, 128), F32)
    for k in range(8):
        solid = jnp.where(lane == k, occ_s[0, 0, k].astype(F32), solid)
    root_ref[16] = solid
    x_ref[37] = solid
    o_ref[37] = solid
    for ref, first in ((x_ref, 1 - odd), (o_ref, odd)):
        for j in range(10):
            ref[27 + j] = root_ref[first * 6 + j]
    for copy in large:
        copy.wait()


def start0(e, loads, scale, b_ref, beta_ref, va_ref):
    total = loads[0] + loads[1] + loads[2]
    third = total * (1.0 / 3.0)
    for c, p in enumerate((loads[0] - third, loads[1] - third, total)):
        b_ref[c, e] = p
        beta = p * scale
        beta_ref[c, e] = beta
        va_ref[c, e] = beta * INV_MID


def stencil0(ref, c, e):
    mid = ref[c, e]
    s = ref[c, e - 1] + mid + ref[c, e + 1]
    return mid, 27.5 * mid - lane_sum(row_sum(s), 1, 128)


def first0(e, sol, beta_ref, va_ref, d_ref, vb_ref):
    for c in range(3):
        v, t = stencil0(va_ref, c, e)
        d = A1 * v + C1 * (beta_ref[c, e] - (sol * (kappa[c] / 26.5)) * t)
        d_ref[c, e] = d
        vb_ref[c, e] = v + d


def second0(e, sol, beta_ref, vb_ref, d_ref, v0_ref):
    for c in range(3):
        v, t = stencil0(vb_ref, c, e)
        pre = beta_ref[c, e] - (sol * (kappa[c] / 26.5)) * t
        v0_ref[c, e] = v + A2 * d_ref[c, e] + C2 * pre


def residual0(k, sols, root_ref, b_ref, v0_ref, t_ref):
    for c in range(3):
        total = None
        for j in range(2):
            e = 4 + 2 * k + j
            _, t = stencil0(v0_ref, c, e)
            r = b_ref[c, e] - (sols[j] * root_ref[e]) * (kappa[c] / 27.0) * t
            total = r if total is None else total + r
        t_ref[c, k] = total


def side0(before, message, own_solid, b_ref, beta_ref, root0_ref, va_ref, d_ref, vb_ref, v0_ref, t_ref):
    side_solid = message[37]

    def at(after_e, before_e):
        return after_e + before * (before_e - after_e)

    first = at(26, 0)
    for j in range(HALO):
        root0_ref[first + j] = safe(message[27 + j])
    first = at(26, 1)
    for j in range(9):
        scale = side_solid / (center * root0_ref[first + j])
        start0(first + j, [message[9 * c + j] for c in range(3)], scale, b_ref, beta_ref, va_ref)
    sign = at(1, -1)
    for j in range(9):
        first0(at(25, 10) + sign * j, own_solid if j < 1 else side_solid, beta_ref, va_ref, d_ref, vb_ref)
    for j in range(9):
        second0(at(24, 11) + sign * j, own_solid if j < 2 else side_solid, beta_ref, vb_ref, d_ref, v0_ref)
    for j in range(5):
        sol = own_solid if j < 2 else side_solid
        residual0(at(9, 4) + sign * j, (sol, sol), root0_ref, b_ref, v0_ref, t_ref)


def inner_kernel(load_ref, own_ref, x_ref, b_ref, beta_ref, root0_ref, va_ref, d_ref, vb_ref, v0_ref, t_ref):
    odd = lax.axis_index("bricks") & 1
    solid = own_ref[16]

    def start(z, _):
        root = own_ref[z]
        root0_ref[z + HALO] = root
        scale = solid / (center * root)
        start0(z + HALO, [load_ref[c, z] for c in range(3)], scale, b_ref, beta_ref, va_ref)
        return 0

    lax.fori_loop(0, 16, start, 0, unroll=8)

    def app1(e, _):
        first0(e, solid, beta_ref, va_ref, d_ref, vb_ref)
        return 0

    lax.fori_loop(HALO + 1, HALO + 15, app1, 0, unroll=7)

    def app2(e, _):
        second0(e, solid, beta_ref, vb_ref, d_ref, v0_ref)
        return 0

    lax.fori_loop(HALO + 2, HALO + 14, app2, 0, unroll=6)

    def resid(k, _):
        residual0(k, (solid, solid), root0_ref, b_ref, v0_ref, t_ref)
        return 0

    lax.fori_loop(5, 9, resid, 0, unroll=4)
    side0(odd, x_ref, solid, b_ref, beta_ref, root0_ref, va_ref, d_ref, vb_ref, v0_ref, t_ref)


def down_kernel(
    own_ref, x_solid_ref, o_ref, b_in, beta_in, root_in, va_in, d_in, vb_in, v0_in, t_in,
    b_ref, beta0_ref, root0_ref, va_ref, d_ref, vb_ref, v0_ref, t_s,
    msg_ref, edge_ref, v1_ref, beta1_ref, root1_ref, sol_ref,
    tr_s,
):
    odd = lax.axis_index("bricks") & 1
    is_odd = odd == 1
    own_solid = own_ref[16]
    x_solid, o_solid = x_solid_ref[37], o_ref[37]
    left_solid = jnp.where(is_odd, x_solid, o_solid)
    right_solid = jnp.where(is_odd, o_solid, x_solid)
    sol_ref[...] = jnp.zeros((8, 128), F32)
    sol_ref[0:1, :] = left_solid[:1]
    sol_ref[1:2, :] = own_solid[:1]
    sol_ref[2:3, :] = right_solid[:1]
    side0(1 - odd, o_ref, own_solid, b_ref, beta0_ref, root0_ref, va_ref, d_ref, vb_ref, v0_ref, t_s)

    def root_pair(k, _):
        tr_s[k] = root0_ref[2 * k] + root0_ref[2 * k + 1]
        return 0

    lax.fori_loop(0, 18, root_pair, 0, unroll=18)

    root1 = lane_pair(tr_s[:, pl.ds(0, 8, 2), :] + tr_s[:, pl.ds(1, 8, 2), :], 1) * 0.125
    root1_ref[...] = root1
    rt = root1[2:16]
    sol = jnp.concatenate(
        [
            jnp.broadcast_to(left_solid[None, :8], (3, 8, 128)),
            jnp.broadcast_to(own_solid[None, :8], (8, 8, 128)),
            jnp.broadcast_to(right_solid[None, :8], (3, 8, 128)),
        ],
        axis=0,
    )
    scale1 = sol / (0.25 * center * rt)
    zero = jnp.zeros((1, 8, 128), F32)

    def stencil1(v):
        before = jnp.concatenate([zero, v[:-1]], axis=0)
        after = jnp.concatenate([v[1:], zero], axis=0)
        return 27.5 * v - lane_sum(row_sum(before + v + after), 2, 128)

    gather = 4 * (iota((8, 128), 1) & 31)
    group = (iota((8, 128), 1) >> 5) == (iota((8, 128), 0) >> 1)

    def compact(q):
        q = q + pltpu.roll(q, 126, 1)
        q = jnp.take_along_axis(q, gather, axis=1)
        return jnp.sum(jnp.where(group, q, 0.0), axis=0, keepdims=True) * 0.125

    odd_lane = (iota((8, 128), 1) & 1) == 1
    to_after, to_before = [], []

    def pair(a, b):
        return jnp.where(odd_lane, b, a)

    def send_edge(k, after, before):
        msg_ref[24 + 8 * k : 32 + 8 * k, :] = jnp.where(is_odd, before, after)
        edge_ref[8 * k : 8 * k + 8, :] = jnp.where(is_odd, after, before)

    b1 = [
        lane_pair(t_s[c, :, pl.ds(0, 8, 2), :] + t_s[c, :, pl.ds(1, 8, 2), :], 1) * 0.125 for c in range(3)
    ]
    m = [sol * (kappa[c] / 26.5) for c in (0, 2)]
    m = [m[0], m[0], m[1]]
    beta = [b1[c] * scale1 for c in range(3)]
    v = [beta[c] * INV_MID for c in range(3)]
    d = list(v)
    for a, b in ((A1, C1), (A2, C2)):
        t = [stencil1(v[c]) for c in range(3)]
        for c in range(3):
            d[c] = a * d[c] + b * (beta[c] - m[c] * t[c])
            v[c] = v[c] + d[c]
    t = [stencil1(v[c])[3:11] for c in range(3)]
    g = (sol * rt)[3:11]
    for c in range(3):
        v1_ref[c] = v[c]
        beta1_ref[c] = beta[c]
        r = b1[c][3:11] - g * (0.25 * kappa[c] / 27.0) * t[c]
        for z in range(4):
            msg_ref[4 * c + z : 4 * c + z + 1, :] = compact(r[2 * z] + r[2 * z + 1])
        for j in range(2):
            send_edge(2 * c + j, pair(v[c][6 + 2 * j], v[c][7 + 2 * j]), pair(v[c][4 + 2 * j], v[c][5 + 2 * j]))
        to_after.append(beta[c][7])
        to_before.append(beta[c][6])
    send_edge(6, pair(*to_after[:2]), pair(*to_before[:2]))
    send_edge(7, to_after[2], to_before[2])
    for z in range(4):
        msg_ref[12 + z : 13 + z, :] = compact(root1[5 + 2 * z] + root1[6 + 2 * z])
    msg_ref[16:24, :] = jnp.take_along_axis(own_solid[:8], gather, axis=1)


def up_kernel(
    mine_ref, far_ref, near_ref, other_ref,
    v0_ref, beta0_ref, root0_ref, v1_ref, beta1_ref, root1_ref, sol_ref,
    out_hbm,
    all_s, solid_s, w_s, coef_s, f_s, e2_s, pe_s, a_s, bb_s, d_s, out_ref, sems,
):
    me = lax.axis_index("bricks")
    odd = me & 1
    is_odd = odd == 1

    for k, ref in enumerate((far_ref, mine_ref, near_ref)):
        start = (136, 0, 272)[k]
        for t in range(8):
            all_s[16 * k + t] = ref[16 * t : 16 * t + 16, :]
            all_s[16 * k + 8 + t] = other_ref[start + 16 * t : start + 16 * t + 16, :]
        solid_s[16 * k : 16 * k + 8, :] = ref[128:136, :]
        solid_s[16 * k + 8 : 16 * k + 16, :] = other_ref[start + 128 : start + 136, :]
    even_row = ((me >> 4) & 1) == 0
    chip0 = (me >> 1) - 8
    here = (me >> 1) & 7
    low_rows = iota((8, 128), 0) < 4
    for w in range(17):
        chip = chip0 + w
        rel = (chip >> 3) - (me >> 4)
        beside = (chip ^ here) & 1
        x0, x1 = ((chip ^ (here - sign * beside)) & 7 for sign in (1, -1))
        six0, six1 = x0 >> 2, x1 >> 2
        two0, two1 = ((x0 >> 1) & 1) ^ six0, ((x1 >> 1) & 1) ^ six1
        place = jnp.where(rel == 0, 1, jnp.where((rel < 0) == even_row, 0, 2))
        slot = 16 * place + 4 * beside
        block0 = slot + (FIRST_TWO * two0 ^ FIRST_SIX * six0) + 8 * odd
        block1 = slot + (FIRST_TWO * two1 ^ FIRST_SIX * six1) + 8 * (1 - odd)
        straight = beside == 0
        blocks = (jnp.where(straight, block0, block1), jnp.where(straight, block1, block0))
        for half in range(2):
            first, second = (all_s[block, 8 * half : 8 * half + 8, :] for block in blocks)
            w_s[2 * half, 8 * w : 8 * w + 8, :] = jnp.where(low_rows, first, pltpu.roll(second, 4, 0))
            w_s[2 * half + 1, 8 * w : 8 * w + 8, :] = jnp.where(low_rows, pltpu.roll(first, 4, 0), second)
        solid = (jnp.broadcast_to(solid_s[pl.ds(block, 1), :], (8, 128)) for block in blocks)
        w_s[4, 8 * w : 8 * w + 8, :] = jnp.where(low_rows, *solid)

    lane = iota((1, 1, 128), 2)

    def lane_mask(cond):
        return jnp.where(cond, 1.0, 0.0).astype(F32)

    masks_x = (lane_mask(lane >= 32), lane_mask(lane < 96))
    masks_y = {
        level: (lane_mask((lane & 31) >= step), lane_mask((lane & 31) < 32 - step))
        for level, step in ((2, 1), (3, 2), (4, 4), (5, 8))
    }
    scale27 = jnp.concatenate([jnp.full((1, 1, 128), k, F32) for k in kappa], axis=0)
    by26 = scale27 * (1.0 / 26.5)

    def stencil(v, level):
        n = v.shape[1]
        s = v + pltpu.roll(v, 1, 1) + pltpu.roll(v, n - 1, 1)
        step = 2 ** (level - 2)
        low, high = masks_y[level]
        if level > 2:
            beside = low * (pltpu.roll(s, step, 2) + pltpu.roll(s, 64 + step, 2))
            beside = beside + high * (pltpu.roll(s, 128 - step, 2) + pltpu.roll(s, 64 - step, 2))
            return (27.5 * v - (s + pltpu.roll(s, 64, 2))) - beside
        lower, upper = masks_x
        s = s + lower * pltpu.roll(s, 32, 2) + upper * pltpu.roll(s, 96, 2)
        return 27.5 * v - (s + low * pltpu.roll(s, 1, 2) + high * pltpu.roll(s, 127, 2))

    def first(beta, m, level):
        v = beta * INV_MID
        d = A1 * v + C1 * (beta - m * stencil(v, level))
        v = v + d
        d = A2 * d + C2 * (beta - m * stencil(v, level))
        return v + d

    def again(v, beta, m, level):
        d = INV_MID * (beta - m * stencil(v, level))
        v = v + d
        d = A1 * d + C1 * (beta - m * stencil(v, level))
        v = v + d
        d = A2 * d + C2 * (beta - m * stencil(v, level))
        return v + d

    def coarsen(values, level, room):
        k, n = values.shape[:2]
        half = (n // 2 + 7) // 8 * 8
        if 2 * half > n:
            room[0:k, n : 2 * half, :] = jnp.zeros((k, 2 * half - n, 128), F32)
        room[0:k, 0:n, :] = values
        s = room[0:k, pl.ds(0, half, 2), :] + room[0:k, pl.ds(1, half, 2), :]
        s = lane_pair(s, 2 ** (level - 2))
        if level == 2:
            return lane_pair(s, 32) * 0.125
        return s * 0.25

    def refine(values, first_row, count):
        n = values.shape[1]
        f_s[0:3, pl.ds(0, n, 2), :] = values
        f_s[0:3, pl.ds(1, n, 2), :] = values
        return f_s[0:3, first_row : first_row + count, :]

    both = w_s[3:5]
    roots, sols = {2: safe(both[0:1])}, {2: both[1:2]}
    for level in (2, 3, 4):
        both = coarsen(jnp.concatenate([roots[level], sols[level]], axis=0), level, coef_s)
        roots[level + 1], sols[level + 1] = safe(both[0:1]), both[1:2]
    sol5 = sols[5]
    sol5_safe = jnp.where(sol5 > 0.0, sol5, 1.0)
    inverse = {level: 1.0 / roots[level] for level in (2, 3, 4, 5)}
    powers = {level: (sols[level], sols[level]) for level in (2, 3, 4)}
    powers[5] = (sol5 * sol5, sol5 * sol5 * sol5)
    g5 = jnp.where(sol5 > 0.0, inverse[5] / sol5_safe, 0.0)
    scales = {level: powers[level][0] * inverse[level] * (1.0 / (0.25**level * center)) for level in (2, 3, 4, 5)}
    masks = {level: powers[level][1] * by26 for level in (2, 3, 4, 5)}
    windows = {4: (0, 40), 3: (24, 48), 2: (56, 80)}

    b = w_s[0:3]
    betas, vs = {}, {}
    for level in (2, 3, 4):
        beta = b * scales[level]
        v = first(beta, masks[level], level)
        r = b - (sols[level] * roots[level]) * (scale27 * (0.25**level / 27.0)) * stencil(v, level)
        betas[level], vs[level] = beta, v
        b = coarsen(r, level, f_s)
    e = first(b * scales[5], masks[5], 5) * g5
    first_row = 0
    for level in (4, 3, 2):
        lo, hi = windows[level]
        e = refine(e, lo - first_row, hi - lo)
        root, sol = roots[level][:, lo:hi], sols[level][:, lo:hi]
        v = vs[level][:, lo:hi] + (root * sol) * e
        v = again(v, betas[level][:, lo:hi], masks[level][:, lo:hi], level)
        e = jnp.where(sol > 0.0, v * inverse[level][:, lo:hi], e)
        first_row = 2 * lo
    e2_s[...] = e

    rows = {}
    for k, name in enumerate(("left", "own", "right")):
        rows[name] = sol_ref[k : k + 1, :]

    def layers(name, n):
        return jnp.broadcast_to(rows[name][None], (n, 8, 128))

    sol = jnp.concatenate([layers("left", 5), layers("own", 8), layers("right", 5)], axis=0)
    root1 = root1_ref[...]
    spread = (iota((8, 128), 0) >> 1) * 32 + (iota((8, 128), 1) >> 2)
    zero = jnp.zeros((1, 8, 128), F32)

    def stencil1(v):
        before = jnp.concatenate([zero, v[:-1]], axis=0)
        after = jnp.concatenate([v[1:], zero], axis=0)
        return 27.5 * v - lane_sum(row_sum(before + v + after), 2, 128)

    odd_lane = (iota((8, 128), 1) & 1) == 1
    across = jnp.where(is_odd, here == 7, here == 0)

    def edge_slabs(k, left):
        mine = other_ref[408 + 8 * k : 416 + 8 * k, :]
        rows = slice(136 + 8 * k, 144 + 8 * k)
        beyond = jnp.where(is_odd == even_row, near_ref[rows, :], far_ref[rows, :])
        other = jnp.where(across, beyond, mine_ref[rows, :])
        p = jnp.where(is_odd == left, mine, other)
        first = jnp.where(odd_lane, pltpu.roll(p, 1, 1), p)
        second = jnp.where(odd_lane, p, pltpu.roll(p, 127, 1))
        return [first[None], second[None]]

    edges = {}
    for left in (True, False):
        slabs = [edge_slabs(k, left) for k in range(8)]
        edges[left] = [slabs[2 * c] + slabs[2 * c + 1] for c in range(3)], [slabs[6][0], slabs[6][1], slabs[7][0]]

    layers_v, layers_b, layers_e = [], [], []
    for c in range(3):
        layers_v.append(jnp.concatenate(edges[True][0][c] + [v1_ref[c][2:12]] + edges[False][0][c], axis=0))
        layers_b.append(jnp.concatenate([zero, edges[True][1][c], beta1_ref[c], edges[False][1][c], zero], axis=0))
        slabs = []
        for j in range(10):
            row = e2_s[c, pl.ds(5 + 4 * odd + j, 1), :]
            slab = jnp.take_along_axis(jnp.broadcast_to(row, (8, 128)), spread, axis=1)[None]
            slabs += [slab, slab]
        layers_e.append(jnp.concatenate(slabs[1:19], axis=0))
    m = [sol * (kappa[c] / 26.5) for c in (0, 2)]
    m = [m[0], m[0], m[1]]
    g = root1 * sol
    v = [layers_v[c] + g * layers_e[c] for c in range(3)]
    d = [None] * 3
    for a, b in ((None, INV_MID), (A1, C1), (A2, C2)):
        t = [stencil1(v[c]) for c in range(3)]
        for c in range(3):
            pre = b * (layers_b[c] - m[c] * t[c])
            d[c] = pre if a is None else a * d[c] + pre
            v[c] = v[c] + d[c]
    inverse1 = 1.0 / root1
    for c in range(3):
        e = jnp.where(sol > 0.0, v[c] * inverse1, layers_e[c])[3:15]
        pe_s[c, :, pl.ds(0, 8, 2), :] = e
        pe_s[c, :, pl.ds(1, 8, 2), :] = e

    shift = HALO - 4

    broad = {name: jnp.broadcast_to(row, (16, 128)) for name, row in rows.items()}

    def sol0(k):
        return broad["left"] if k < 4 else broad["own"] if k < 20 else broad["right"]

    for k in range(1, 23):
        g = root0_ref[k + shift] * sol0(k)
        for c in range(3):
            a_s[c, k] = v0_ref[c, k + shift] + g * pe_s[c, k >> 1]


    for k in range(2, 22):
        sol = sol0(k)
        for c in range(3):
            v, t = stencil0(a_s, c, k)
            d = INV_MID * (beta0_ref[c, k + shift] - (sol * (kappa[c] / 26.5)) * t)
            d_s[c, k] = d
            bb_s[c, k] = v + d


    for k in range(3, 21):
        sol = sol0(k)
        for c in range(3):
            v, t = stencil0(bb_s, c, k)
            pre = beta0_ref[c, k + shift] - (sol * (kappa[c] / 26.5)) * t
            d = A1 * d_s[c, k] + C1 * pre
            d_s[c, k] = d
            a_s[c, k] = v + d

    own_solid = jnp.broadcast_to(rows["own"], (16, 128))

    copies = []
    for k in range(4, 20):
        inverse = 1.0 / root0_ref[k + shift]
        x = []
        for c in range(3):
            v, t = stencil0(a_s, c, k)
            pre = beta0_ref[c, k + shift] - (own_solid * (kappa[c] / 26.5)) * t
            v = v + A2 * d_s[c, k] + C2 * pre
            x.append(jnp.where(own_solid > 0.0, v * inverse, pe_s[c, k >> 1]))
        third = x[2] * (1.0 / 3.0)
        out_ref[0, k - 4] = x[0] + third
        out_ref[1, k - 4] = x[1] + third
        out_ref[2, k - 4] = third - x[0] - x[1]
        if k % 2 == 1:
            part = pl.ds(k - 5, 2)
            copy = pltpu.make_async_copy(out_ref.at[:, part], out_hbm.at[:, part], sems.at[k // 2 - 2])
            copy.start()
            copies.append(copy)
    for copy in copies:
        copy.wait()


VMEM = pl.BlockSpec(memory_space=pltpu.VMEM)
HBM = pl.BlockSpec(memory_space=pltpu.HBM)
PARAMS = pltpu.CompilerParams(vmem_limit_bytes=40 * 2**20)


def shaped(*shape):
    return jax.ShapeDtypeStruct(shape, F32)


def swap_bits(values, bits):
    n = lax.axis_size("bricks")
    return lax.ppermute(values, "bricks", [(i, i ^ bits) for i in range(n)])


def swap_before(values):
    n = lax.axis_size("bricks")
    return lax.ppermute(values, "bricks", [(i, i + 1 if i % 2 else i - 1) for i in range(1, n - 1)])


def swap_ring(values):
    n = lax.axis_size("bricks")
    pairs = []
    for i in range(0, n, 2):
        j = i // 16 * 16 + (i - 1) % 16
        pairs += [(i, j), (j, i)]
    return lax.ppermute(values, "bricks", sorted(pairs))


def swap_far_rows(values):
    n = lax.axis_size("bricks")
    return lax.ppermute(values, "bricks", [(i, i + 16 if i >> 4 & 1 else i - 16) for i in range(16, n - 16)])


def body(load_field, material_class, occupancy, moduli):
    x_msg, o_msg, root = pl.pallas_call(
        pack_kernel,
        out_shape=(shaped(38, 16, 128), shaped(38, 16, 128), shaped(17, 16, 128)),
        in_specs=[HBM, HBM, HBM, HBM],
        out_specs=(VMEM,) * 3,
        scratch_shapes=[
            pltpu.VMEM((16, 16, 128), jnp.int32),
            pltpu.SMEM((1, 1, 8), jnp.int32),
            pltpu.SMEM((8,), F32),
            pltpu.SemaphoreType.DMA((9,)),
        ],
        compiler_params=pltpu.CompilerParams(vmem_limit_bytes=56 * 2**20),
        name="pack",
    )(load_field, material_class, occupancy, moduli)
    x_in = swap_bits(x_msg, 1)
    o_in = swap_before(o_msg)
    ext = shaped(3, EXT, 16, 128)
    fine = (ext, ext, shaped(EXT, 16, 128), ext, ext, ext, ext, shaped(3, 14, 16, 128))
    inner = pl.pallas_call(
        inner_kernel,
        out_shape=fine,
        in_specs=[VMEM] * 3,
        out_specs=(VMEM,) * 8,
        compiler_params=PARAMS,
        cost_estimate=pl.CostEstimate(flops=10_000_000, bytes_accessed=4_000_000, transcendentals=0),
        name="inner",
    )(load_field, root, x_in)
    _, beta0, root0, _, _, _, v0, _, msg, edge, v1, beta1, root1, solid_rows = pl.pallas_call(
        down_kernel,
        out_shape=fine
        + (
            shaped(88, 128), shaped(64, 128),
            shaped(3, 14, 8, 128), shaped(3, 14, 8, 128), shaped(18, 8, 128), shaped(8, 128),
        ),
        in_specs=[VMEM] * 11,
        out_specs=(VMEM,) * 14,
        input_output_aliases={3 + k: k for k in range(8)},
        scratch_shapes=[
            pltpu.VMEM((18, 16, 128), F32),
        ],
        compiler_params=PARAMS,
        name="down",
    )(root, x_in, o_in, *inner)
    row_of = iota((8, 128), 0)

    def joined(a, b, bit):
        return jnp.where((row_of & bit) == 0, a, b)

    mine = msg[:24]
    parts = [mine] + [swap_bits(mine, bits) for bits in RING_ORDER]
    blocks = jnp.concatenate([part[:16] for part in parts], axis=0)
    solids = parts[0][16:]
    for k in (1, 2, 3):
        solids = jnp.where((row_of & 3) == k, parts[k][16:], solids)
    got = swap_ring(jnp.concatenate([blocks, solids, edge], axis=0))
    blocks = jnp.concatenate([blocks, got[:64]], axis=0)
    solids = joined(solids, got[64:72], 4)
    edge_in = got[72:]
    mine = jnp.concatenate([blocks, solids, edge_in], axis=0)
    far, near = swap_far_rows(mine), swap_bits(mine, 16)
    other = swap_bits(jnp.concatenate([mine[:136], far[:136], near[:136], msg[24:]], axis=0), 1)
    return pl.pallas_call(
        up_kernel,
        out_shape=shaped(3, 16, 16, 128),
        in_specs=[VMEM] * 11,
        out_specs=HBM,
        scratch_shapes=[
            pltpu.VMEM((48, 16, 128), F32),
            pltpu.VMEM((48, 128), F32),
            pltpu.VMEM((5, 136, 128), F32),
            pltpu.VMEM((2, 144, 128), F32),
            pltpu.VMEM((3, 144, 128), F32),
            pltpu.VMEM((3, 24, 128), F32),
            pltpu.VMEM((3, 12, 16, 128), F32),
            pltpu.VMEM((3, 24, 16, 128), F32),
            pltpu.VMEM((3, 24, 16, 128), F32),
            pltpu.VMEM((3, 24, 16, 128), F32),
            pltpu.VMEM((3, 16, 16, 128), F32),
            pltpu.SemaphoreType.DMA((8,)),
        ],
        compiler_params=PARAMS,
        name="up",
    )(mine, far, near, other, v0, beta0, root0, v1, beta1, root1, solid_rows)


def solution(mesh):
    in_specs = (
        P(None, "bricks", None, None),
        P("bricks", None, None),
        P("bricks", None, None),
        P(),
    )
    out_specs = P(None, "bricks", None, None)
    return jax.shard_map(body, mesh=mesh, in_specs=in_specs, out_specs=out_specs, check_vma=False)
```
